256 devices in a mesh: grp: 4 (over x_hi, core), blk: 64 (over y, x_lo, z).
Axes of the slice: x: 4 (x_hi: 2, x_lo: 2; x = x_hi * 2 + x_lo), y: 4, z: 8, core: 2. Of those that a mesh axis runs over, the one named last changes fastest.
Arguments:
- picture_tower_mean: bfloat16 [8192, 6144], P('blk', 'grp'), may hold values from -6 to 6
- caption_tower_mean: bfloat16 [8192, 4096], P('blk', 'grp'), may hold values from -6 to 6
- picture_projector: bfloat16 [6144, 1024], P('grp'), may hold values from -0.3046875 to 0.3046875
- caption_projector: bfloat16 [4096, 1024], P('grp'), may hold values from -0.375 to 0.375
- score_heat_param: float32 [1], replicated, may hold values from 5 to 15
- score_shift_param: float32 [1], replicated, may hold values from -5 to -2
- objective_cotangent: float32 [1], replicated, may hold values from 16384 to 65536
Outputs:
- image_grad: bfloat16 [8192, 6144], P('blk', 'grp')
- text_grad: bfloat16 [8192, 4096], P('blk', 'grp')
- image_proj_grad: float32 [6144, 1024], P(('grp', 'blk'))
- text_proj_grad: float32 [4096, 1024], P(('grp', 'blk'))
The draws below stay inside these ranges and needn't reach their ends.
All inputs are finite; a program needn't handle non-finite values.
Results may differ from the reference program's by a relative error of at most 0.02.
Values may be sent and summed in bfloat16 or wider, within the bound.
A program may use at most 128 MiB of HBM per device.

```python
import jax
import jax.numpy as jnp
from jax import lax

D_IMG = 6144
D_TXT = 4096
EMB = 1024
SAMPLE_TOTAL = 8192


def shard_levels(key, dims, pieces, least, high):
    def one(dim, shards_of):
        steps = jax.random.uniform(jax.random.fold_in(jax.random.fold_in(key, 6), dim), (shards_of,), jnp.float32, least / len(pieces), high / len(pieces))
        return jnp.repeat(jnp.exp(steps), dims[dim] // shards_of).reshape((-1,) + (1,) * (len(dims) - dim - 1))

    gain = one(*pieces[0])
    for cut in pieces[1:]:
        gain = gain * one(*cut)
    return gain


def centred(stream_key, shape, scale, limit, pieces=(), held_as=jnp.bfloat16):
    result = jax.random.normal(stream_key, shape, jnp.float32) * scale
    if len(pieces) > 0:
        result = shard_levels(stream_key, shape, pieces, -0.22, 0.18) * result
    return jnp.clip(result, min=-limit, max=limit).astype(held_as)


def setup_inputs(seed: int = 0) -> dict:
    keys = jax.random.split(jax.random.key(seed), 8)
    picture_tower_mean = centred(keys[0], (SAMPLE_TOTAL, D_IMG), 1.0, 6.0, ((0, 64), (1, 4)))
    caption_tower_mean = centred(keys[1], (SAMPLE_TOTAL, D_TXT), 1.0, 6.0, ((0, 64), (1, 4)))
    picture_projector = centred(keys[2], (D_IMG, EMB), (4.0 / D_IMG ** 0.5), 0.3046875, ((0, 4),))
    caption_projector = centred(keys[3], (D_TXT, EMB), (4.0 / D_TXT ** 0.5), 0.375, ((0, 4),))
    score_heat_param = jnp.clip(jax.random.uniform(keys[4], (1,), jnp.float32, 5.0, 15.0), 5.0, 15.0)
    score_shift_param = jnp.clip(jax.random.uniform(keys[5], (1,), jnp.float32, -5.0, -2.0), -5.0, -2.0)
    objective_cotangent = jnp.clip(jax.random.uniform(keys[6], (1,), jnp.float32, 16384.0, 65536.0), 16384.0, 65536.0)
    return {"picture_tower_mean": picture_tower_mean, "caption_tower_mean": caption_tower_mean, "picture_projector": picture_projector, "caption_projector": caption_projector, "score_heat_param": score_heat_param, "score_shift_param": score_shift_param, "objective_cotangent": objective_cotangent}


def unit(emb):
    return emb * jax.lax.rsqrt(lax.optimization_barrier(jnp.sum(emb * emb, axis=-1, keepdims=True)) + 1e-06)

def reference(picture_tower_mean, caption_tower_mean, picture_projector, caption_projector, score_heat_param, score_shift_param, objective_cotangent):
    img_emb = jnp.dot(picture_tower_mean, picture_projector, preferred_element_type=jnp.float32)
    txt_emb = jnp.dot(caption_tower_mean, caption_projector, preferred_element_type=jnp.float32)
    picture_normed = unit(img_emb).astype(jnp.bfloat16)
    caption_normed = unit(txt_emb).astype(jnp.bfloat16)
    similarity_scores = score_heat_param[0] * jnp.dot(picture_normed, caption_normed.T, preferred_element_type=jnp.float32) + score_shift_param[0]
    multiplier_amount = objective_cotangent[0] * score_heat_param[0] / SAMPLE_TOTAL
    pair_coefficient = (multiplier_amount * (jax.nn.sigmoid(similarity_scores) - jnp.eye(SAMPLE_TOTAL, dtype=jnp.float32))).astype(jnp.bfloat16)
    img_unit_grad = jnp.dot(pair_coefficient, caption_normed, preferred_element_type=jnp.float32)
    txt_unit_grad = jnp.dot(pair_coefficient.T, picture_normed, preferred_element_type=jnp.float32)
    _, img_back = jax.vjp(unit, img_emb)
    _, txt_back = jax.vjp(unit, txt_emb)
    img_emb_grad = img_back(img_unit_grad)[0].astype(jnp.bfloat16)
    txt_emb_grad = txt_back(txt_unit_grad)[0].astype(jnp.bfloat16)
    image_grad = jnp.dot(img_emb_grad, picture_projector.T, preferred_element_type=jnp.float32).astype(jnp.bfloat16)
    text_grad = jnp.dot(txt_emb_grad, caption_projector.T, preferred_element_type=jnp.float32).astype(jnp.bfloat16)
    image_proj_grad = jnp.dot(picture_tower_mean.T, img_emb_grad, preferred_element_type=jnp.float32)
    text_proj_grad = jnp.dot(caption_tower_mean.T, txt_emb_grad, preferred_element_type=jnp.float32)
    return (image_grad, text_grad, image_proj_grad, text_proj_grad)
```

```python
import functools

import jax
import jax.numpy as jnp
from jax import lax
from jax.experimental import pallas as pl
from jax.experimental.pallas import tpu as pltpu
from jax.sharding import PartitionSpec as P

MESH = pl.DeviceIdType.MESH
F32 = jnp.float32
BF16 = jnp.bfloat16
EPS = 1e-06

ROWS = 128
SHARE = 32
HALF = 16
EMB = 1024
WIDE = 512
FI, FT = 1536, 1024
FIY, FTY = FI // 4, FT // 4
OI, OT = FIY // 16, FTY // 16
CHUNK = 512
SENDS = 112


def dot_nn(a, b):
    return lax.dot_general(a, b, (((1,), (0,)), ((), ())), preferred_element_type=F32)


def dot_nt(a, b):
    return lax.dot_general(a, b, (((1,), (1,)), ((), ())), preferred_element_type=F32)


def dot_tn(a, b):
    return lax.dot_general(a, b, (((0,), (0,)), ((), ())), preferred_element_type=F32)


def scratch():
    v = pltpu.VMEM
    dma = pltpu.SemaphoreType.DMA
    return dict(
        xi=v((ROWS, FI), BF16),
        xt=v((ROWS, FT), BF16),
        wi=v((FI, EMB), BF16),
        wt=v((FT, EMB), BF16),
        part=v((2, ROWS, EMB), F32),
        a_out=v((2, 2, SHARE, EMB), BF16),
        a_in=v((2, 2, SHARE, EMB), BF16),
        half=v((2, SHARE, EMB), F32),
        b_out=v((2, SHARE, EMB), BF16),
        b_in=v((2, SHARE, EMB), BF16),
        emb=v((2, SHARE, EMB), F32),
        rst=v((2, SHARE, 128), F32),
        iu=v((2, 4, 4, SHARE, WIDE), BF16),
        tu=v((2, 8, SHARE, EMB), BF16),
        coef=v((2, 512, 256), BF16),
        c_out=v((8, SHARE, EMB), BF16),
        c_in=v((8, SHARE, EMB), BF16),
        own_t=v((8, SHARE, EMB), F32),
        d_out=v((4, 2, SHARE, EMB), BF16),
        d_in=v((4, 2, SHARE, EMB), BF16),
        own_i=v((2, 4, 4, SHARE, WIDE), F32),
        e1_out=v((2, 4, 4, SHARE, WIDE), BF16),
        e1_in=v((2, 4, 4, SHARE, WIDE), BF16),
        mid_i=v((2, 4, SHARE, WIDE), F32),
        e2_out=v((2, 4, SHARE, WIDE), BF16),
        e2_in=v((2, 4, SHARE, WIDE), BF16),
        sum_i=v((SHARE, EMB), F32),
        gi=v((2, 4, 2, SHARE, EMB), BF16),
        gt=v((2, 4, 2, SHARE, EMB), BF16),
        ti=v((4, ROWS, FIY), BF16),
        tt=v((4, ROWS, FTY), BF16),
        mi=v((512, FIY), BF16),
        mt=v((512, FTY), BF16),
        ni=v((2, FIY, 256), BF16),
        nt=v((2, FTY, 256), BF16),
        pi=v((FIY, EMB), F32),
        pt=v((FTY, EMB), F32),
        fi_out=v((2, 4, 2, 2 * OI, WIDE), BF16),
        fi_in=v((2, 3, 2, 2 * OI, WIDE), BF16),
        fi_end=v((2, 2, 2 * OI, WIDE), BF16),
        fi_side=v((2, 2 * OI, WIDE), BF16),
        ft_out=v((2, 4, 2, OT, EMB), BF16),
        ft_in=v((2, 3, 2, OT, EMB), BF16),
        ft_end=v((2, 2, OT, EMB), BF16),
        ft_side=v((2, OT, EMB), BF16),
        in_sem=dma((7,)),
        x_sem=dma((2, 4)),
        a_sem=dma((2,)),
        b_sem=dma((2,)),
        iu_sem=dma((2, 2, 4)),
        tu_sem=dma((9,)),
        tc_sem=dma((2,)),
        c_sem=dma((2,)),
        d_sem=dma((4, 2)),
        e1_sem=dma((2, 4)),
        e2_sem=dma((2, 4)),
        far_sem=dma((2,)),
        g_sem=dma((2, 2, 4)),
        gc_sem=dma((2, 3)),
        f_sem=dma((2, 2, 3)),
        end_sem=dma((2, 2, 2)),
        h_sem=dma((2,)),
        send_sem=dma((SENDS,)),
    )


NAMES = tuple(scratch())
AROUND = (0, 1, -1, 2, -2, 3, -3, 4)
ABOUT = (0, 1, -1, 2)


def rows_half(h):
    return pl.ds(h * HALF, HALF)


def interleave(order, **tasks):
    for name in order:
        next(tasks[name], None)
    left = list(tasks.values())
    while left:
        left = [task for task in left if next(task, True) is not True]


def together(*tasks):
    left = list(tasks)
    while left:
        left = [task for task in left if next(task, True) is not True]
        if left:
            yield


def kernel(xi_h, xt_h, wi_h, wt_h, heat_ref, shift_ref, cot_ref, og_i, og_t, op_i, op_t, *refs):
    s = dict(zip(NAMES, refs))
    g = lax.axis_index("grp")
    b = lax.axis_index("blk")
    xh, co = lax.div(g, 2), lax.rem(g, 2)
    y, xl, z = lax.div(b, 16), lax.rem(lax.div(b, 8), 2), lax.rem(b, 8)
    x = xh * 2 + xl
    oc, ox = 1 - co, 1 - xh

    def dev(x_, y_, z_, co_):
        return (lax.div(x_, 2) * 2 + co_, (y_ * 2 + lax.rem(x_, 2)) * 8 + z_)

    other_core = dev(x, y, z, oc)
    near = dev(xh * 2 + (1 - xl), y, z, co)
    along_x = {k: dev(lax.rem(x + 4 + k, 4), y, z, co) for k in (1, -1, 2)}
    far = along_x[2]
    along_y = {k: dev(x, lax.rem(y + 4 + k, 4), z, co) for k in (1, -1, 2)}
    along_z = {k: dev(x, y, lax.rem(z + 8 + k, 8), co) for k in (1, -1, 2, -2)}
    corner = {
        (h, k): dev(xh * 2 + h, y, lax.rem(z + 8 + k, 8), co) for h in range(2) for k in (1, -1)
    }
    corners = [dev(xh * 2 + (1 - xl), y, lax.rem(z + 8 + k, 8), co) for k in (1, -1)]

    sends = []

    def send(src, dst, sem, to):
        copy = pltpu.make_async_remote_copy(
            src_ref=src,
            dst_ref=dst,
            send_sem=s["send_sem"].at[len(sends)],
            recv_sem=sem,
            device_id=to,
            device_id_type=MESH,
        )
        copy.start()
        sends.append(copy)

    def arrived(dst, sem):
        pltpu.make_async_copy(dst, dst, sem).wait()

    def gather_eight(to, ref, sem, then):
        for way in (2, -2, 1, -1):
            send(ref(0, None), ref(-way, None), sem(-way), to[way])
        yield
        for half, way in enumerate((1, -1)):
            far_ = -2 * way
            arrived(ref(far_, None), sem(far_))
            send(ref(far_, half), ref(4, half), s["tu_sem"].at[7 + half], to[2 * way])
            send(ref(far_, None), ref(-3 * way, None), sem(-3 * way), to[way])
        for k in (1, -1):
            arrived(ref(k, None), sem(k))
        then(0)
        yield
        for k in (3, -3):
            arrived(ref(k, None), sem(k))
        for half in range(2):
            arrived(ref(4, half), s["tu_sem"].at[7 + half])
        then(1)

    def scatter_eight(to, own, out, inn, sem, totals):
        for n, way in enumerate((1, -1)):
            rows = rows_half(n)
            out[3, n, rows] = own(4)[n * HALF : (n + 1) * HALF].astype(BF16)
            send(out.at[3, n, rows], inn.at[3, n, rows], sem.at[3, n], to[2 * way])
        for n, way in enumerate((1, -1)):
            out[2, n] = own(3 * way).astype(BF16)
            send(out.at[2, n], inn.at[2, n], sem.at[2, n], to[way])
        for n, way in enumerate((1, -1)):
            out[0, n] = own(way).astype(BF16)
            send(out.at[0, n], inn.at[0, n], sem.at[0, n], to[way])
        yield
        for n, way in enumerate((1, -1)):
            rows = slice(n * HALF, (n + 1) * HALF)
            rest = slice((1 - n) * HALF, (2 - n) * HALF)
            value = own(2 * way)
            arrived(inn.at[2, n], sem.at[2, n])
            arrived(inn.at[3, n, rows_half(n)], sem.at[3, n])
            more = inn[2, n, rows].astype(F32) + inn[3, n, rows].astype(F32)
            out[1, n, rows] = (value[rows] + more).astype(BF16)
            out[1, n, rest] = (value[rest] + inn[2, n, rest].astype(F32)).astype(BF16)
            send(out.at[1, n], inn.at[1, n], sem.at[1, n], to[2 * way])
        value = own(0)
        yield
        for m in range(2):
            for n in range(2):
                arrived(inn.at[m, n], sem.at[m, n])
                value = value + inn[m, n].astype(F32)
        totals.append(value)

    def gather_four(to, ref, sem):
        for way in (1, -1):
            send(ref(0, None), ref(-way, None), sem.at[0 if way > 0 else 1], to[way])
        yield
        for way in (1, -1):
            n = 0 if way > 0 else 1
            arrived(ref(-way, None), sem.at[n])
            send(ref(-way, n), ref(2, n), sem.at[2 + n], to[way])
        yield
        for n in range(2):
            arrived(ref(2, n), sem.at[2 + n])

    def gather_direct(to, ref, sem):
        for way in (2, 1, -1):
            send(ref(0, None), ref(-way, None), sem.at[-way % 4], to[way])
        yield
        for k in (1, -1, 2):
            arrived(ref(k, None), sem.at[k % 4])

    def scatter_direct(to, own, out, inn, sem, totals):
        for way in (2, 1, -1):
            k = -way % 4
            out[k] = own(way).astype(BF16)
            send(out.at[k], inn.at[k], sem.at[k], to[way])
        value = own(0)
        yield
        for k in (1, -1, 2):
            arrived(inn.at[k % 4], sem.at[k % 4])
            value = value + inn[k % 4].astype(F32)
        totals.append(value)

    def scatter_corner(t, own, name, totals):
        out, inn, end, side = (s[name + part] for part in ("_out", "_in", "_end", "_side"))
        sem, end_sem = s["f_sem"].at[t], s["end_sem"].at[t]
        for step in range(1, 5):
            if step > 1:
                yield
            for d, way in enumerate((1, -1)):
                if step == 1:
                    out[d, 0, d] = own(4 * way, d).astype(BF16)
                    send(out.at[d, 0, d], inn.at[d, 0, d], sem.at[d, 0], along_z[way])
                    continue
                before = inn.at[d, step - 2]
                arrived(before.at[d] if step == 2 else before, sem.at[d, step - 2])
                for half in range(2):
                    value = own(way * (5 - step), half)
                    if step > 2 or half == d:
                        value = value + inn[d, step - 2, half].astype(F32)
                    out[d, step - 1, half] = value.astype(BF16)
                    if step == 4:
                        origin = lax.rem(xl + half, 2)
                        send(out.at[d, 3, half], end.at[origin, d], end_sem.at[origin, d], corner[half, way])
                if step < 4:
                    send(out.at[d, step - 1], inn.at[d, step - 1], sem.at[d, step - 1], along_z[way])
            if step == 1:
                side[0] = own(0, 1 - xl).astype(BF16)
                send(side.at[0], side.at[1], s["h_sem"].at[t], near)
        value = own(0, xl)
        yield
        arrived(side.at[1], s["h_sem"].at[t])
        value = value + side[1].astype(F32)
        for origin in range(2):
            for d in range(2):
                arrived(end.at[origin, d], end_sem.at[origin, d])
                value = value + end[origin, d].astype(F32)
        totals.append(value)

    def load(src, dst, n):
        copy = pltpu.make_async_copy(src, dst, s["in_sem"].at[n])
        copy.start()
        return copy

    def load_rows(src, dst, k, n):
        rows = pl.ds(k * CHUNK, CHUNK)
        return load(src.at[rows], dst.at[rows], n)

    xi_load = load(xi_h, s["xi"], 0)
    wi_loads = [load_rows(wi_h, s["wi"], k, 1 + k) for k in range(FI // CHUNK)]
    xt_load = load(xt_h, s["xt"], 4)
    wt_loads = [load_rows(wt_h, s["wt"], k, 5 + k) for k in range(FT // CHUNK)]

    barrier = pltpu.get_barrier_semaphore()
    peers = [other_core, *along_x.values(), *along_y.values(), *along_z.values(), *corners]
    for to in peers:
        pl.semaphore_signal(barrier, inc=1, device_id=to, device_id_type=MESH)

    def partial(t, x_ref, w_ref, x_load, w_loads):
        x_load.wait()
        for k, w_load in enumerate(w_loads):
            w_load.wait()
            rows = slice(k * CHUNK, (k + 1) * CHUNK)
            part = dot_nn(x_ref[:, rows], w_ref[rows, :])
            s["part"][t] = part if k == 0 else s["part"][t] + part
            yield
        for h in range(2):
            rows = pl.ds(pl.multiple_of((h * 2 + oc) * SHARE, SHARE), SHARE)
            s["a_out"][t, h] = s["part"][t, rows, :].astype(BF16)
        send(s["a_out"].at[t], s["a_in"].at[t], s["a_sem"].at[t], other_core)

    def mine(t, h):
        rows = pl.ds(pl.multiple_of((h * 2 + co) * SHARE, SHARE), SHARE)
        got = s["a_in"][t, pl.ds(h, 1)].reshape(SHARE, EMB)
        return s["part"][t, rows, :] + got.astype(F32)

    def to_far(t):
        arrived(s["a_in"].at[t], s["a_sem"].at[t])
        s["b_out"][t] = mine(t, ox).astype(BF16)
        send(s["b_out"].at[t], s["b_in"].at[t], s["b_sem"].at[t], far)
        s["half"][t] = mine(t, xh)

    def exchange(t, x_ref, t_ref, width):
        for k, to in along_y.items():
            cols = pl.ds(pl.multiple_of(lax.rem(y + 4 + k, 4) * width, 128), width)
            send(x_ref.at[:, cols], t_ref.at[-k % 4], s["x_sem"].at[t, -k % 4], to)
        cols = pl.ds(pl.multiple_of(y * width, 128), width)
        t_ref[0] = x_ref[:, cols]

    image_part = partial(0, s["xi"], s["wi"], xi_load, wi_loads)
    text_part = partial(1, s["xt"], s["wt"], xt_load, wt_loads)
    for _ in wi_loads:
        next(image_part)
    pl.semaphore_wait(barrier, len(peers))
    next(image_part, None)
    for _ in text_part:
        pass
    to_far(0)
    exchange(0, s["xi"], s["ti"], FIY)
    to_far(1)
    exchange(1, s["xt"], s["tt"], FTY)

    def units(t):
        arrived(s["b_in"].at[t], s["b_sem"].at[t])
        e = s["half"][t] + s["b_in"][t].astype(F32)
        rs = lax.rsqrt(jnp.sum(e * e, axis=-1, keepdims=True) + EPS)
        s["emb"][t] = e
        s["rst"][t] = jnp.broadcast_to(rs, (SHARE, 128))
        return (e * rs).astype(BF16)

    def images_ring(w):
        def one(k, half):
            at = (k % 4, 0) if w == 0 else (0, k % 4)
            rows = pl.ds(0, SHARE) if half is None else rows_half(half)
            return s["iu"].at[(w,) + at + (rows,)]

        def four(k, half):
            rows = pl.ds(0, SHARE) if half is None else rows_half(half)
            at = (pl.ds(0, 4), k % 4) if w == 0 else (k % 4, pl.ds(0, 4))
            return s["iu"].at[(w,) + at + (rows,)]

        first, second = (along_x, along_y) if w == 0 else (along_y, along_x)
        yield from gather_direct(first, one, s["iu_sem"].at[w, 0])
        yield from gather_direct(second, four, s["iu_sem"].at[w, 1])

    def texts_ring():
        s["tu"][0, 0] = units(1)

        def ref(k, half):
            rows = pl.ds(0, SHARE) if half is None else rows_half(half)
            return s["tu"].at[0, AROUND.index(k), rows]

        def sem(k):
            return s["tu_sem"].at[AROUND.index(k)]

        def across(part):
            slots = (pl.ds(0, 5), pl.ds(5, 3))[part]
            send(s["tu"].at[0, slots], s["tu"].at[1, slots], s["tc_sem"].at[part], other_core)

        yield from gather_eight(along_z, ref, sem, across)

    def images_rings():
        u = units(0)
        for w in range(2):
            s["iu"][w, 0, 0] = u[:, w * WIDE : (w + 1) * WIDE]
        yield from together(images_ring(0), images_ring(1))

    def turned(t, t_ref, m_ref, n_ref):
        for k in range(1, 4):
            arrived(t_ref.at[k], s["x_sem"].at[t, k])
        for n, core in enumerate((co, oc)):
            for k, dy in enumerate(ABOUT):
                for h in range(2):
                    at = (n * 8 + k * 2 + h) * SHARE
                    rows = pl.ds(pl.multiple_of((h * 2 + core) * SHARE, SHARE), SHARE)
                    m_ref[at : at + SHARE, :] = t_ref[dy % 4, rows, :]
            n_ref[n] = m_ref[n * 256 : (n + 1) * 256, :].T
            yield

    def towers():
        yield from turned(0, s["ti"], s["mi"], s["ni"])
        yield from turned(1, s["tt"], s["mt"], s["nt"])

    interleave("ititti", t=texts_ring(), i=images_rings())

    heat, shift = heat_ref[0], shift_ref[0]
    mult = cot_ref[0] * heat / 8192.0

    def texts(n, w):
        return s["tu"][n].reshape(256, EMB)[:, w * WIDE : (w + 1) * WIDE]

    def images(w):
        return s["iu"][w].reshape(512, WIDE)

    def coefficients(n):
        score = dot_nt(images(0), texts(n, 0)) + dot_nt(images(1), texts(n, 1))
        value = jax.nn.sigmoid(heat * score + shift)
        if n == 0:
            row = lax.broadcasted_iota(jnp.int32, (512, 256), 0)
            col = lax.broadcasted_iota(jnp.int32, (512, 256), 1)
            value = value - ((row == col) & (row < SHARE)).astype(F32)
        s["coef"][n] = (mult * value).astype(BF16)

    def text_half(n, w, out):
        grad = dot_tn(s["coef"][n], images(w)).reshape(8, SHARE, WIDE)
        out[:, :, w * WIDE : (w + 1) * WIDE] = grad.astype(out.dtype)

    coefficients(0)
    arrived(s["tu"].at[1, pl.ds(0, 5)], s["tc_sem"].at[0])
    arrived(s["tu"].at[1, pl.ds(5, 3)], s["tc_sem"].at[1])
    coefficients(1)
    for w in range(2):
        text_half(1, w, s["c_out"])
        cols = pl.ds(w * WIDE, WIDE)
        send(s["c_out"].at[:, :, cols], s["c_in"].at[:, :, cols], s["c_sem"].at[w], other_core)

    def back(t, grads, grad):
        rs = s["rst"][t][:, :1]
        u = s["emb"][t] * rs
        value = (grad - u * jnp.sum(u * grad, axis=-1, keepdims=True)) * rs
        grads[0, 0, pl.ds(xh, 1)] = value.astype(BF16).reshape(1, SHARE, EMB)

    def text_grad():
        for w in range(2):
            text_half(0, w, s["own_t"])
        for w in range(2):
            cols = pl.ds(w * WIDE, WIDE)
            arrived(s["c_in"].at[:, :, cols], s["c_sem"].at[w])

        def own(k):
            at = AROUND.index(k)
            return s["own_t"][at] + s["c_in"][at].astype(F32)

        totals = []
        yield from scatter_eight(along_z, own, s["d_out"], s["d_in"], s["d_sem"], totals)
        back(1, s["gt"], totals[0])

    def image_half(w):
        grad = dot_nn(s["coef"][0], texts(0, w)) + dot_nn(s["coef"][1], texts(1, w))
        s["own_i"][w] = grad.reshape(4, 4, SHARE, WIDE)

        def four(k):
            return s["own_i"][0, :, k % 4] if w == 0 else s["own_i"][1, k % 4]

        def one(k):
            return s["mid_i"][w, k % 4]

        first, second = (along_y, along_x) if w == 0 else (along_x, along_y)
        totals = []
        yield from scatter_direct(
            first, four, s["e1_out"].at[w], s["e1_in"].at[w], s["e1_sem"].at[w], totals
        )
        s["mid_i"][w] = totals[0]
        totals = []
        yield from scatter_direct(
            second, one, s["e2_out"].at[w], s["e2_in"].at[w], s["e2_sem"].at[w], totals
        )
        s["sum_i"][:, w * WIDE : (w + 1) * WIDE] = totals[0]

    def image_grad():
        yield from together(image_half(0), image_half(1))
        back(0, s["gi"], s["sum_i"][...])

    def spread(t, grads, first_dot):
        def across(slots, h, n):
            send(grads.at[0, slots, h], grads.at[1, slots, h], s["gc_sem"].at[t, n], other_core)

        def ring(h, n):
            def ref(k, half):
                rows = pl.ds(0, SHARE) if half is None else rows_half(half)
                return grads.at[0, ABOUT.index(k if k != -2 else 2), h, rows]

            if n == 0:
                send(ref(0, None), ref(0, None), s["far_sem"].at[t], far)
            else:
                arrived(ref(0, None), s["far_sem"].at[t])
            task = gather_four(along_y, ref, s["g_sem"].at[t, n])
            next(task)
            yield
            next(task)
            if n == 1:
                across(pl.ds(0, 3), h, 1)
            yield
            yield from task
            across(pl.ds(0, 4) if n == 0 else pl.ds(3, 1), h, 2 * n)

        first, second = ring(xh, 0), ring(ox, 1)
        next(first)
        yield
        next(first)
        next(second)
        yield
        next(first, None)
        next(second)
        yield
        next(second, None)
        first_dot()
        yield
        for n, (h, slots) in enumerate(((xh, pl.ds(0, 4)), (ox, pl.ds(0, 3)), (ox, pl.ds(3, 1)))):
            arrived(grads.at[1, slots, h], s["gc_sem"].at[t, n])

    def weights(t, grads, n_ref, p_ref, own, names, w_ref, out):
        def term(n):
            return dot_nn(n_ref[n], grads[n].reshape(256, EMB))

        def first_dot():
            p_ref[...] = term(0)

        yield from spread(t, grads, first_dot)
        p_ref[...] = p_ref[...] + term(1)
        totals = []
        ring = scatter_corner(t, own, names, totals)
        chunks = [slice(k, k + CHUNK) for k in range(0, w_ref.shape[0], CHUNK)]
        for _ in ring:
            for cols in (chunks.pop(0),) if chunks else ():
                value = dot_nt(grads[:, 0].reshape(ROWS, EMB), w_ref[cols, :]).astype(BF16)
                for n, core in enumerate((co, oc)):
                    for h in range(2):
                        rows = pl.ds(pl.multiple_of((h * 2 + core) * SHARE, SHARE), SHARE)
                        at = (n * 2 + h) * SHARE
                        out[rows, cols] = value[at : at + SHARE]
            yield
        return totals[0]

    def own_i(k, half):
        n = half * 8 + lax.rem(z + 8 + k, 8)
        rows = s["pi"][pl.ds(pl.multiple_of(n * OI, 8), OI), :]
        return jnp.concatenate([rows[:, :WIDE], rows[:, WIDE:]], axis=0)

    def own_t(k, half):
        n = half * 8 + lax.rem(z + 8 + k, 8)
        return s["pt"][pl.ds(pl.multiple_of(n * OT, 8), OT), :]

    def texts_back():
        yield from text_grad()
        op_t[...] = yield from weights(1, s["gt"], s["nt"], s["pt"], own_t, "ft", s["wt"], og_t)

    def images_back():
        yield from image_grad()
        total = yield from weights(0, s["gi"], s["ni"], s["pi"], own_i, "fi", s["wi"], og_i)
        op_i[:, :WIDE] = total[:OI]
        op_i[:, WIDE:] = total[OI:]

    interleave("itwwtwititwitiititwitititit", i=images_back(), t=texts_back(), w=towers())
    for copy in sends:
        copy.wait_send()


def per_device(xi, xt, wi, wt, heat, shift, cot):
    vmem = pl.BlockSpec(memory_space=pltpu.VMEM)
    smem = pl.BlockSpec(memory_space=pltpu.SMEM)
    hbm = pl.BlockSpec(memory_space=pl.ANY)
    shapes = (
        jax.ShapeDtypeStruct((ROWS, FI), BF16),
        jax.ShapeDtypeStruct((ROWS, FT), BF16),
        jax.ShapeDtypeStruct((OI, EMB), F32),
        jax.ShapeDtypeStruct((OT, EMB), F32),
    )
    return pl.pallas_call(
        kernel,
        out_shape=shapes,
        in_specs=[hbm] * 4 + [smem] * 3,
        out_specs=[vmem] * 4,
        scratch_shapes=list(scratch().values()),
        compiler_params=pltpu.CompilerParams(
            collective_id=0, has_side_effects=True, vmem_limit_bytes=52 * 1024 * 1024
        ),
    )(xi, xt, wi, wt, heat, shift, cot)


def solution(mesh):
    placed = (P("blk", "grp"), P("blk", "grp"), P("grp", None), P("grp", None), P(), P(), P())
    return jax.shard_map(
        per_device,
        mesh=mesh,
        in_specs=placed,
        out_specs=(
            P("blk", "grp"),
            P("blk", "grp"),
            P(("grp", "blk"), None),
            P(("grp", "blk"), None),
        ),
        check_vma=False,
    )
```

```python
import functools

import jax
import jax.numpy as jnp
from jax import lax
from jax.experimental import pallas as pl
from jax.experimental.pallas import tpu as pltpu
from jax.sharding import PartitionSpec as P

MESH = pl.DeviceIdType.MESH
F32 = jnp.float32
BF16 = jnp.bfloat16
EPS = 1e-06

ROWS = 128
SHARE = 32
HALF = 16
EMB = 1024
WIDE = 512
FI, FT = 1536, 1024
FIY, FTY = FI // 4, FT // 4
OI, OT = FIY // 16, FTY // 16
CHUNK = 512
SENDS = 112


def dot_nn(a, b):
    return lax.dot_general(a, b, (((1,), (0,)), ((), ())), preferred_element_type=F32)


def dot_nt(a, b):
    return lax.dot_general(a, b, (((1,), (1,)), ((), ())), preferred_element_type=F32)


def dot_tn(a, b):
    return lax.dot_general(a, b, (((0,), (0,)), ((), ())), preferred_element_type=F32)


def scratch():
    v = pltpu.VMEM
    dma = pltpu.SemaphoreType.DMA
    return dict(
        xi=v((ROWS, FI), BF16),
        xt=v((ROWS, FT), BF16),
        wi=v((FI, EMB), BF16),
        wt=v((FT, EMB), BF16),
        part=v((2, ROWS, EMB), F32),
        a_out=v((2, 2, SHARE, EMB), BF16),
        a_in=v((2, 2, SHARE, EMB), BF16),
        half=v((2, SHARE, EMB), F32),
        b_out=v((2, SHARE, EMB), BF16),
        b_in=v((2, SHARE, EMB), BF16),
        emb=v((2, SHARE, EMB), F32),
        rst=v((2, SHARE, 128), F32),
        iu=v((4, 4, SHARE, EMB), BF16),
        tu=v((2, 8, SHARE, EMB), BF16),
        coef=v((512, 512), BF16),
        c_out=v((8, SHARE, EMB), BF16),
        c_in=v((8, SHARE, EMB), BF16),
        own_t=v((8, SHARE, EMB), F32),
        d_out=v((4, 2, SHARE, EMB), BF16),
        d_in=v((4, 2, SHARE, EMB), BF16),
        own_i=v((2, 4, 4, SHARE, WIDE), F32),
        e1_out=v((2, 4, 4, SHARE, WIDE), BF16),
        e1_in=v((2, 4, 4, SHARE, WIDE), BF16),
        mid_i=v((2, 4, SHARE, WIDE), F32),
        e2_out=v((2, 4, SHARE, WIDE), BF16),
        e2_in=v((2, 4, SHARE, WIDE), BF16),
        sum_i=v((SHARE, EMB), F32),
        gi=v((2, 4, 2, SHARE, EMB), BF16),
        gt=v((2, 4, 2, SHARE, EMB), BF16),
        ti=v((4, ROWS, FIY), BF16),
        tt=v((4, ROWS, FTY), BF16),
        mi=v((512, FIY), BF16),
        mt=v((512, FTY), BF16),
        ni=v((2, FIY, 256), BF16),
        nt=v((2, FTY, 256), BF16),
        pi=v((FIY, EMB), F32),
        pt=v((FTY, EMB), F32),
        fi_out=v((2, 4, 2, 2 * OI, WIDE), BF16),
        fi_in=v((2, 3, 2, 2 * OI, WIDE), BF16),
        fi_end=v((2, 2, 2 * OI, WIDE), BF16),
        fi_side=v((2, 2 * OI, WIDE), BF16),
        ft_out=v((2, 4, 2, OT, EMB), BF16),
        ft_in=v((2, 3, 2, OT, EMB), BF16),
        ft_end=v((2, 2, OT, EMB), BF16),
        ft_side=v((2, OT, EMB), BF16),
        in_sem=dma((7,)),
        x_sem=dma((2, 4)),
        a_sem=dma((2,)),
        b_sem=dma((2,)),
        iu_sem=dma((2, 2, 4)),
        tu_sem=dma((9,)),
        tc_sem=dma((2,)),
        c_sem=dma,
        d_sem=dma((4, 2)),
        e1_sem=dma((2, 4)),
        e2_sem=dma((2, 4)),
        far_sem=dma((2,)),
        g_sem=dma((2, 2, 4)),
        gc_sem=dma((2, 3)),
        f_sem=dma((2, 2, 3)),
        end_sem=dma((2, 2, 2)),
        h_sem=dma((2,)),
        send_sem=dma((SENDS,)),
    )


NAMES = tuple(scratch())
AROUND = (0, 1, -1, 2, -2, 3, -3, 4)
ABOUT = (0, 1, -1, 2)


def rows_half(h):
    return pl.ds(h * HALF, HALF)


def interleave(order, **tasks):
    for name in order:
        next(tasks[name], None)
    left = list(tasks.values())
    while left:
        left = [task for task in left if next(task, True) is not True]


def kernel(xi_h, xt_h, wi_h, wt_h, heat_ref, shift_ref, cot_ref, og_i, og_t, op_i, op_t, *refs):
    s = dict(zip(NAMES, refs))
    g = lax.axis_index("grp")
    b = lax.axis_index("blk")
    xh, co = lax.div(g, 2), lax.rem(g, 2)
    y, xl, z = lax.div(b, 16), lax.rem(lax.div(b, 8), 2), lax.rem(b, 8)
    x = xh * 2 + xl
    oc, ox = 1 - co, 1 - xh

    def dev(x_, y_, z_, co_):
        return (lax.div(x_, 2) * 2 + co_, (y_ * 2 + lax.rem(x_, 2)) * 8 + z_)

    other_core = dev(x, y, z, oc)
    near = dev(xh * 2 + (1 - xl), y, z, co)
    along_x = {k: dev(lax.rem(x + 4 + k, 4), y, z, co) for k in (1, -1, 2)}
    far = along_x[2]
    along_y = {k: dev(x, lax.rem(y + 4 + k, 4), z, co) for k in (1, -1, 2)}
    along_z = {k: dev(x, y, lax.rem(z + 8 + k, 8), co) for k in (1, -1, 2, -2)}
    corner = {
        (h, k): dev(xh * 2 + h, y, lax.rem(z + 8 + k, 8), co) for h in range(2) for k in (1, -1)
    }
    corners = [dev(xh * 2 + (1 - xl), y, lax.rem(z + 8 + k, 8), co) for k in (1, -1)]

    sends, drained = [], []

    def send(src, dst, sem, to):
        copy = pltpu.make_async_remote_copy(
            src_ref=src,
            dst_ref=dst,
            send_sem=s["send_sem"].at[len(sends)],
            recv_sem=sem,
            device_id=to,
            device_id_type=MESH,
        )
        copy.start()
        sends.append(copy)

    def arrived(dst, sem):
        pltpu.make_async_copy(dst, dst, sem).wait()

    def gather_eight(to, ref, sem, then):
        for way in (2, -2, 1, -1):
            send(ref(0, None), ref(-way, None), sem(-way), to[way])
        yield
        for half, way in enumerate((1, -1)):
            far_ = -2 * way
            arrived(ref(far_, None), sem(far_))
            send(ref(far_, half), ref(4, half), s["tu_sem"].at[7 + half], to[2 * way])
            send(ref(far_, None), ref(-3 * way, None), sem(-3 * way), to[way])
        for k in (1, -1):
            arrived(ref(k, None), sem(k))
        then(0)
        yield
        for k in (3, -3):
            arrived(ref(k, None), sem(k))
        for half in range(2):
            arrived(ref(4, half), s["tu_sem"].at[7 + half])
        then(1)

    def scatter_eight(to, own, out, inn, sem, totals):
        for n, way in enumerate((1, -1)):
            rows = rows_half(n)
            out[3, n, rows] = own(4)[n * HALF : (n + 1) * HALF].astype(BF16)
            send(out.at[3, n, rows], inn.at[3, n, rows], sem.at[3, n], to[2 * way])
        for n, way in enumerate((1, -1)):
            out[2, n] = own(3 * way).astype(BF16)
            send(out.at[2, n], inn.at[2, n], sem.at[2, n], to[way])
        for n, way in enumerate((1, -1)):
            out[0, n] = own(way).astype(BF16)
            send(out.at[0, n], inn.at[0, n], sem.at[0, n], to[way])
        yield
        for n, way in enumerate((1, -1)):
            rows = slice(n * HALF, (n + 1) * HALF)
            rest = slice((1 - n) * HALF, (2 - n) * HALF)
            value = own(2 * way)
            arrived(inn.at[2, n], sem.at[2, n])
            arrived(inn.at[3, n, rows_half(n)], sem.at[3, n])
            more = inn[2, n, rows].astype(F32) + inn[3, n, rows].astype(F32)
            out[1, n, rows] = (value[rows] + more).astype(BF16)
            out[1, n, rest] = (value[rest] + inn[2, n, rest].astype(F32)).astype(BF16)
            send(out.at[1, n], inn.at[1, n], sem.at[1, n], to[2 * way])
        value = own(0)
        yield
        for m in range(2):
            for n in range(2):
                arrived(inn.at[m, n], sem.at[m, n])
                value = value + inn[m, n].astype(F32)
        totals.append(value)

    def gather_four(to, ref, sem):
        for way in (1, -1):
            send(ref(0, None), ref(-way, None), sem.at[0 if way > 0 else 1], to[way])
        yield
        for way in (1, -1):
            n = 0 if way > 0 else 1
            arrived(ref(-way, None), sem.at[n])
            send(ref(-way, n), ref(2, n), sem.at[2 + n], to[way])
        yield
        for n in range(2):
            arrived(ref(2, n), sem.at[2 + n])

    def gather_direct(to, ref, sem):
        for way in (2, 1, -1):
            send(ref(0, None), ref(-way, None), sem.at[-way % 4], to[way])
        yield
        for k in (1, -1, 2):
            arrived(ref(k, None), sem.at[k % 4])

    def scatter_direct(to, own, out, inn, sem, totals):
        for way in (2, 1, -1):
            k = -way % 4
            out[k] = own(way).astype(BF16)
            send(out.at[k], inn.at[k], sem.at[k], to[way])
        value = own(0)
        yield
        for k in (1, -1, 2):
            arrived(inn.at[k % 4], sem.at[k % 4])
            value = value + inn[k % 4].astype(F32)
        totals.append(value)

    def scatter_corner(t, own, name, totals):
        out, inn, end, side = (s[name + part] for part in ("_out", "_in", "_end", "_side"))
        sem, end_sem = s["f_sem"].at[t], s["end_sem"].at[t]
        for step in range(1, 5):
            if step > 1:
                yield
            for d, way in enumerate((1, -1)):
                if step == 1:
                    out[d, 0, d] = own(4 * way, d).astype(BF16)
                    send(out.at[d, 0, d], inn.at[d, 0, d], sem.at[d, 0], along_z[way])
                    continue
                before = inn.at[d, step - 2]
                arrived(before.at[d] if step == 2 else before, sem.at[d, step - 2])
                for half in range(2):
                    value = own(way * (5 - step), half)
                    if step > 2 or half == d:
                        value = value + inn[d, step - 2, half].astype(F32)
                    out[d, step - 1, half] = value.astype(BF16)
                    if step == 4:
                        origin = lax.rem(xl + half, 2)
                        send(out.at[d, 3, half], end.at[origin, d], end_sem.at[origin, d], corner[half, way])
                if step < 4:
                    send(out.at[d, step - 1], inn.at[d, step - 1], sem.at[d, step - 1], along_z[way])
            if step == 1:
                side[0] = own(0, 1 - xl).astype(BF16)
                send(side.at[0], side.at[1], s["h_sem"].at[t], near)
        value = own(0, xl)
        yield
        arrived(side.at[1], s["h_sem"].at[t])
        value = value + side[1].astype(F32)
        for origin in range(2):
            for d in range(2):
                arrived(end.at[origin, d], end_sem.at[origin, d])
                value = value + end[origin, d].astype(F32)
        totals.append(value)

    def load(src, dst, n):
        copy = pltpu.make_async_copy(src, dst, s["in_sem"].at[n])
        copy.start()
        return copy

    def load_rows(src, dst, k, n):
        rows = pl.ds(k * CHUNK, CHUNK)
        return load(src.at[rows], dst.at[rows], n)

    xi_load = load(xi_h, s["xi"], 0)
    wi_loads = [load_rows(wi_h, s["wi"], k, 1 + k) for k in range(FI // CHUNK)]
    xt_load = load(xt_h, s["xt"], 4)
    wt_loads = [load_rows(wt_h, s["wt"], k, 5 + k) for k in range(FT // CHUNK)]

    barrier = pltpu.get_barrier_semaphore()
    peers = [other_core, *along_x.values(), *along_y.values(), *along_z.values(), *corners]
    for to in peers:
        pl.semaphore_signal(barrier, inc=1, device_id=to, device_id_type=MESH)

    def partial(t, x_ref, w_ref, x_load, w_loads):
        x_load.wait()
        for k, w_load in enumerate(w_loads):
            w_load.wait()
            rows = slice(k * CHUNK, (k + 1) * CHUNK)
            part = dot_nn(x_ref[:, rows], w_ref[rows, :])
            s["part"][t] = part if k == 0 else s["part"][t] + part
            yield
        for h in range(2):
            rows = pl.ds(pl.multiple_of((h * 2 + oc) * SHARE, SHARE), SHARE)
            s["a_out"][t, h] = s["part"][t, rows, :].astype(BF16)
        send(s["a_out"].at[t], s["a_in"].at[t], s["a_sem"].at[t], other_core)

    def mine(t, h):
        rows = pl.ds(pl.multiple_of((h * 2 + co) * SHARE, SHARE), SHARE)
        got = s["a_in"][t, pl.ds(h, 1)].reshape(SHARE, EMB)
        return s["part"][t, rows, :] + got.astype(F32)

    def to_far(t):
        arrived(s["a_in"].at[t], s["a_sem"].at[t])
        s["b_out"][t] = mine(t, ox).astype(BF16)
        send(s["b_out"].at[t], s["b_in"].at[t], s["b_sem"].at[t], far)
        s["half"][t] = mine(t, xh)

    def exchange(t, x_ref, t_ref, width):
        for k, to in along_y.items():
            cols = pl.ds(pl.multiple_of(lax.rem(y + 4 + k, 4) * width, 128), width)
            send(x_ref.at[:, cols], t_ref.at[-k % 4], s["x_sem"].at[t, -k % 4], to)
        cols = pl.ds(pl.multiple_of(y * width, 128), width)
        t_ref[0] = x_ref[:, cols]

    image_part = partial(0, s["xi"], s["wi"], xi_load, wi_loads)
    text_part = partial(1, s["xt"], s["wt"], xt_load, wt_loads)
    for _ in wi_loads:
        next(image_part)
    pl.semaphore_wait(barrier, len(peers))
    next(image_part, None)
    for _ in text_part:
        pass
    to_far(0)
    exchange(0, s["xi"], s["ti"], FIY)
    to_far(1)
    exchange(1, s["xt"], s["tt"], FTY)

    def units(t):
        arrived(s["b_in"].at[t], s["b_sem"].at[t])
        e = s["half"][t] + s["b_in"][t].astype(F32)
        rs = lax.rsqrt(jnp.sum(e * e, axis=-1, keepdims=True) + EPS)
        s["emb"][t] = e
        s["rst"][t] = jnp.broadcast_to(rs, (SHARE, 128))
        return (e * rs).astype(BF16)

    def images_ring(w):
        if w == 0:
            s["iu"][0, 0] = units(0)
        cols = pl.ds(w * WIDE, WIDE)

        def one(k, half):
            at = (k % 4, 0) if w == 0 else (0, k % 4)
            return s["iu"].at[at + (pl.ds(0, SHARE), cols)]

        def four(k, half):
            at = (pl.ds(0, 4), k % 4) if w == 0 else (k % 4, pl.ds(0, 4))
            return s["iu"].at[at + (pl.ds(0, SHARE), cols)]

        first, second = (along_x, along_y) if w == 0 else (along_y, along_x)
        yield from gather_direct(first, one, s["iu_sem"].at[w, 0])
        yield from gather_direct(second, four, s["iu_sem"].at[w, 1])

    def texts_ring():
        s["tu"][0, 0] = units(1)

        def ref(k, half):
            rows = pl.ds(0, SHARE) if half is None else rows_half(half)
            return s["tu"].at[0, AROUND.index(k), rows]

        def sem(k):
            return s["tu_sem"].at[AROUND.index(k)]

        def across(part):
            slots = (pl.ds(0, 5), pl.ds(5, 3))[part]
            send(s["tu"].at[0, slots], s["tu"].at[1, slots], s["tc_sem"].at[part], other_core)

        yield from gather_eight(along_z, ref, sem, across)

    def turned(t, t_ref, m_ref, n_ref):
        for k in range(1, 4):
            arrived(t_ref.at[k], s["x_sem"].at[t, k])
        for n, core in enumerate((co, oc)):
            for k, dy in enumerate(ABOUT):
                for h in range(2):
                    at = (n * 8 + k * 2 + h) * SHARE
                    rows = pl.ds(pl.multiple_of((h * 2 + core) * SHARE, SHARE), SHARE)
                    m_ref[at : at + SHARE, :] = t_ref[dy % 4, rows, :]
            n_ref[n] = m_ref[n * 256 : (n + 1) * 256, :].T
            yield

    def towers():
        yield from turned(0, s["ti"], s["mi"], s["ni"])
        yield from turned(1, s["tt"], s["mt"], s["nt"])

    towers_task = towers()
    interleave(
        "tabwabtwatb",
        t=texts_ring(),
        a=images_ring(0),
        b=images_ring(1),
        w=(next(towers_task, None) for _ in range(2)),
    )

    heat, shift = heat_ref[0], shift_ref[0]
    mult = cot_ref[0] * heat / 8192.0

    def texts():
        return s["tu"][...].reshape(512, EMB)

    def images():
        return s["iu"][...].reshape(512, EMB)

    def coefficients(n):
        score = dot_nt(images(), s["tu"][n].reshape(256, EMB))
        value = jax.nn.sigmoid(heat * score + shift)
        if n == 0:
            row = lax.broadcasted_iota(jnp.int32, (512, 256), 0)
            col = lax.broadcasted_iota(jnp.int32, (512, 256), 1)
            value = value - ((row == col) & (row < SHARE)).astype(F32)
        s["coef"][:, n * 256 : (n + 1) * 256] = (mult * value).astype(BF16)

    def text_half(n, out):
        grad = dot_tn(s["coef"][:, n * 256 : (n + 1) * 256], images())
        out[...] = grad.reshape(8, SHARE, EMB).astype(out.dtype)

    coefficients(0)
    arrived(s["tu"].at[1, pl.ds(0, 5)], s["tc_sem"].at[0])
    arrived(s["tu"].at[1, pl.ds(5, 3)], s["tc_sem"].at[1])
    coefficients(1)
    text_half(1, s["c_out"])
    send(s["c_out"], s["c_in"], s["c_sem"], other_core)

    def back(t, grads, grad):
        rs = s["rst"][t][:, :1]
        u = s["emb"][t] * rs
        value = (grad - u * jnp.sum(u * grad, axis=-1, keepdims=True)) * rs
        grads[0, 0, pl.ds(xh, 1)] = value.astype(BF16).reshape(1, SHARE, EMB)

    def text_grad():
        text_half(0, s["own_t"])
        yield
        arrived(s["c_in"], s["c_sem"])

        def own(k):
            at = AROUND.index(k)
            return s["own_t"][at] + s["c_in"][at].astype(F32)

        totals = []
        yield from scatter_eight(along_z, own, s["d_out"], s["d_in"], s["d_sem"], totals)
        back(1, s["gt"], totals[0])

    def image_half(w):
        grad = dot_nn(s["coef"][...], texts()[:, w * WIDE : (w + 1) * WIDE])
        s["own_i"][w] = grad.reshape(4, 4, SHARE, WIDE)

        def four(k):
            return s["own_i"][0, :, k % 4] if w == 0 else s["own_i"][1, k % 4]

        def one(k):
            return s["mid_i"][w, k % 4]

        first, second = (along_y, along_x) if w == 0 else (along_x, along_y)
        totals = []
        yield from scatter_direct(
            first, four, s["e1_out"].at[w], s["e1_in"].at[w], s["e1_sem"].at[w], totals
        )
        s["mid_i"][w] = totals[0]
        totals = []
        yield from scatter_direct(
            second, one, s["e2_out"].at[w], s["e2_in"].at[w], s["e2_sem"].at[w], totals
        )
        s["sum_i"][:, w * WIDE : (w + 1) * WIDE] = totals[0]

    def spread(t, grads, first_dot):
        def across(slots, h, n):
            send(grads.at[0, slots, h], grads.at[1, slots, h], s["gc_sem"].at[t, n], other_core)

        def ring(h, n):
            def ref(k, half):
                rows = pl.ds(0, SHARE) if half is None else rows_half(half)
                return grads.at[0, ABOUT.index(k if k != -2 else 2), h, rows]

            if n == 0:
                send(ref(0, None), ref(0, None), s["far_sem"].at[t], far)
            else:
                arrived(ref(0, None), s["far_sem"].at[t])
            task = gather_four(along_y, ref, s["g_sem"].at[t, n])
            next(task)
            yield
            next(task)
            if n == 1:
                across(pl.ds(0, 3), h, 1)
            yield
            yield from task
            across(pl.ds(0, 4) if n == 0 else pl.ds(3, 1), h, 2 * n)

        first, second = ring(xh, 0), ring(ox, 1)
        next(first)
        yield
        next(first)
        next(second)
        yield
        next(first, None)
        next(second)
        yield
        next(second, None)
        first_dot()
        yield
        for n, (h, slots) in enumerate(((xh, pl.ds(0, 4)), (ox, pl.ds(0, 3)), (ox, pl.ds(3, 1)))):
            arrived(grads.at[1, slots, h], s["gc_sem"].at[t, n])

    def weights(t, grads, n_ref, p_ref, own, names):
        def term(n):
            return dot_nn(n_ref[n], grads[n].reshape(256, EMB))

        def first_dot():
            p_ref[...] = term(0)

        yield from spread(t, grads, first_dot)
        p_ref[...] = p_ref[...] + term(1)
        totals = []
        ring = scatter_corner(t, own, names, totals)
        yield from ring
        return totals[0]

    def inputs(grads, w_ref, out):
        for k in range(0, w_ref.shape[0], CHUNK):
            cols = slice(k, k + CHUNK)
            value = dot_nt(grads[:, 0].reshape(ROWS, EMB), w_ref[cols, :]).astype(BF16)
            for n, core in enumerate((co, oc)):
                for h in range(2):
                    rows = pl.ds(pl.multiple_of((h * 2 + core) * SHARE, SHARE), SHARE)
                    at = (n * 2 + h) * SHARE
                    out[rows, cols] = value[at : at + SHARE]
            yield

    def drain():
        while True:
            for _ in range(len(sends) - len(drained)):
                drained.append(sends[len(drained)])
                drained[-1].wait_send()
            yield

    def own_i(k, half):
        n = half * 8 + lax.rem(z + 8 + k, 8)
        rows = s["pi"][pl.ds(pl.multiple_of(n * OI, 8), OI), :]
        return jnp.concatenate([rows[:, :WIDE], rows[:, WIDE:]], axis=0)

    def own_t(k, half):
        n = half * 8 + lax.rem(z + 8 + k, 8)
        return s["pt"][pl.ds(pl.multiple_of(n * OT, 8), OT), :]

    def texts_back():
        yield from text_grad()
        op_t[...] = yield from weights(1, s["gt"], s["nt"], s["pt"], own_t, "ft")

    def images_back():
        back(0, s["gi"], s["sum_i"][...])
        total = yield from weights(0, s["gi"], s["ni"], s["pi"], own_i, "fi")
        op_i[:, :WIDE] = total[:OI]
        op_i[:, WIDE:] = total[OI:]

    drains = drain()
    interleave(
        "abttwatbabitwititiittiptiotoiptowxiopxt",
        t=texts_back(),
        a=image_half(0),
        b=image_half(1),
        i=images_back(),
        w=towers_task,
        o=inputs(s["gi"], s["wi"], og_i),
        p=inputs(s["gt"], s["wt"], og_t),
        x=(next(drains) for _ in range(2)),
    )
    next(drains)


def per_device(xi, xt, wi, wt, heat, shift, cot):
    vmem = pl.BlockSpec(memory_space=pltpu.VMEM)
    smem = pl.BlockSpec(memory_space=pltpu.SMEM)
    hbm = pl.BlockSpec(memory_space=pl.ANY)
    shapes = (
        jax.ShapeDtypeStruct((ROWS, FI), BF16),
        jax.ShapeDtypeStruct((ROWS, FT), BF16),
        jax.ShapeDtypeStruct((OI, EMB), F32),
        jax.ShapeDtypeStruct((OT, EMB), F32),
    )
    return pl.pallas_call(
        kernel,
        out_shape=shapes,
        in_specs=[hbm] * 4 + [smem] * 3,
        out_specs=[vmem] * 4,
        scratch_shapes=list(scratch().values()),
        compiler_params=pltpu.CompilerParams(
            collective_id=0, has_side_effects=True, vmem_limit_bytes=52 * 1024 * 1024
        ),
    )(xi, xt, wi, wt, heat, shift, cot)


def solution(mesh):
    placed = (P("blk", "grp"), P("blk", "grp"), P("grp", None), P("grp", None), P(), P(), P())
    return jax.shard_map(
        per_device,
        mesh=mesh,
        in_specs=placed,
        out_specs=(
            P("blk", "grp"),
            P("blk", "grp"),
            P(("grp", "blk"), None),
            P(("grp", "blk"), None),
        ),
        check_vma=False,
    )
```

```python
import functools

import jax
import jax.numpy as jnp
from jax import lax
from jax.experimental import pallas as pl
from jax.experimental.pallas import tpu as pltpu
from jax.sharding import PartitionSpec as P

MESH = pl.DeviceIdType.MESH
F32 = jnp.float32
BF16 = jnp.bfloat16
EPS = 1e-06

ROWS = 128
SHARE = 32
HALF = 16
EMB = 1024
WIDE = 512
FI, FT = 1536, 1024
FIY, FTY = FI // 4, FT // 4
OI, OT = FIY // 16, FTY // 16
CHUNK = 512
SENDS = 112


def dot_nn(a, b):
    return lax.dot_general(a, b, (((1,), (0,)), ((), ())), preferred_element_type=F32)


def dot_nt(a, b):
    return lax.dot_general(a, b, (((1,), (1,)), ((), ())), preferred_element_type=F32)


def dot_tn(a, b):
    return lax.dot_general(a, b, (((0,), (0,)), ((), ())), preferred_element_type=F32)


def scratch():
    v = pltpu.VMEM
    dma = pltpu.SemaphoreType.DMA
    return dict(
        xi=v((ROWS, FI), BF16),
        xt=v((ROWS, FT), BF16),
        wi=v((FI, EMB), BF16),
        wt=v((FT, EMB), BF16),
        part=v((2, ROWS, EMB), F32),
        a_out=v((2, 2, SHARE, EMB), BF16),
        a_in=v((2, 2, SHARE, EMB), BF16),
        half=v((2, SHARE, EMB), F32),
        b_out=v((2, SHARE, EMB), BF16),
        b_in=v((2, SHARE, EMB), BF16),
        emb=v((2, SHARE, EMB), F32),
        rst=v((2, SHARE, 128), F32),
        iu=v((4, 4, SHARE, EMB), BF16),
        tu=v((2, 8, SHARE, EMB), BF16),
        coef=v((512, 512), BF16),
        c_out=v((8, SHARE, EMB), BF16),
        c_in=v((8, SHARE, EMB), BF16),
        own_t=v((8, SHARE, EMB), F32),
        d_out=v((4, 2, SHARE, EMB), BF16),
        d_in=v((4, 2, SHARE, EMB), BF16),
        e1_out=v((2, 4, 4, SHARE, WIDE), BF16),
        e1_in=v((2, 4, 4, SHARE, WIDE), BF16),
        e2_out=v((2, 4, SHARE, WIDE), BF16),
        e2_in=v((2, 4, SHARE, WIDE), BF16),
        sum_i=v((SHARE, EMB), F32),
        gi=v((2, 4, 2, SHARE, EMB), BF16),
        gt=v((2, 4, 2, SHARE, EMB), BF16),
        ti=v((4, ROWS, FIY), BF16),
        tt=v((4, ROWS, FTY), BF16),
        mi=v((512, FIY), BF16),
        mt=v((512, FTY), BF16),
        ni=v((2, FIY, 256), BF16),
        nt=v((2, FTY, 256), BF16),
        pi=v((FIY, EMB), F32),
        pt=v((FTY, EMB), F32),
        fi_out=v((2, 4, 2, 2 * OI, WIDE), BF16),
        fi_in=v((2, 3, 2, 2 * OI, WIDE), BF16),
        fi_end=v((2, 2, 2 * OI, WIDE), BF16),
        fi_side=v((2, 2 * OI, WIDE), BF16),
        ft_out=v((2, 4, 2, OT, EMB), BF16),
        ft_in=v((2, 3, 2, OT, EMB), BF16),
        ft_end=v((2, 2, OT, EMB), BF16),
        ft_side=v((2, OT, EMB), BF16),
        in_sem=dma((7,)),
        x_sem=dma((2, 4)),
        a_sem=dma((2,)),
        b_sem=dma((2,)),
        iu_sem=dma((2, 2, 4)),
        tu_sem=dma((9,)),
        tc_sem=dma((2,)),
        c_sem=dma,
        d_sem=dma((4, 2)),
        e1_sem=dma((2, 4)),
        e2_sem=dma((2, 4)),
        far_sem=dma((2,)),
        g_sem=dma((2, 2, 4)),
        gc_sem=dma((2, 3)),
        f_sem=dma((2, 2, 3)),
        end_sem=dma((2, 2, 2)),
        h_sem=dma((2,)),
        send_sem=dma((SENDS,)),
    )


NAMES = tuple(scratch())
AROUND = (0, 1, -1, 2, -2, 3, -3, 4)
ABOUT = (0, 1, -1, 2)


def rows_half(h):
    return pl.ds(h * HALF, HALF)


def interleave(order, **tasks):
    for name in order:
        next(tasks[name], None)
    left = list(tasks.values())
    while left:
        left = [task for task in left if next(task, True) is not True]


def kernel(xi_h, xt_h, wi_h, wt_h, heat_ref, shift_ref, cot_ref, og_i, og_t, op_i, op_t, *refs):
    s = dict(zip(NAMES, refs))
    g = lax.axis_index("grp")
    b = lax.axis_index("blk")
    xh, co = lax.div(g, 2), lax.rem(g, 2)
    y, xl, z = lax.div(b, 16), lax.rem(lax.div(b, 8), 2), lax.rem(b, 8)
    x = xh * 2 + xl
    oc, ox = 1 - co, 1 - xh

    def dev(x_, y_, z_, co_):
        return (lax.div(x_, 2) * 2 + co_, (y_ * 2 + lax.rem(x_, 2)) * 8 + z_)

    other_core = dev(x, y, z, oc)
    near = dev(xh * 2 + (1 - xl), y, z, co)
    along_x = {k: dev(lax.rem(x + 4 + k, 4), y, z, co) for k in (1, -1, 2)}
    far = along_x[2]
    along_y = {k: dev(x, lax.rem(y + 4 + k, 4), z, co) for k in (1, -1, 2)}
    along_z = {k: dev(x, y, lax.rem(z + 8 + k, 8), co) for k in (1, -1, 2, -2)}
    corner = {
        (h, k): dev(xh * 2 + h, y, lax.rem(z + 8 + k, 8), co) for h in range(2) for k in (1, -1)
    }
    corners = [dev(xh * 2 + (1 - xl), y, lax.rem(z + 8 + k, 8), co) for k in (1, -1)]

    sends, drained = [], []

    def send(src, dst, sem, to):
        copy = pltpu.make_async_remote_copy(
            src_ref=src,
            dst_ref=dst,
            send_sem=s["send_sem"].at[len(sends)],
            recv_sem=sem,
            device_id=to,
            device_id_type=MESH,
        )
        copy.start()
        sends.append(copy)

    def arrived(dst, sem):
        pltpu.make_async_copy(dst, dst, sem).wait()

    def gather_eight(to, ref, sem, then):
        for way in (2, -2, 1, -1):
            send(ref(0, None), ref(-way, None), sem(-way), to[way])
        yield
        for half, way in enumerate((1, -1)):
            far_ = -2 * way
            arrived(ref(far_, None), sem(far_))
            send(ref(far_, half), ref(4, half), s["tu_sem"].at[7 + half], to[2 * way])
            send(ref(far_, None), ref(-3 * way, None), sem(-3 * way), to[way])
        for k in (1, -1):
            arrived(ref(k, None), sem(k))
        then(0)
        yield
        for k in (3, -3):
            arrived(ref(k, None), sem(k))
        for half in range(2):
            arrived(ref(4, half), s["tu_sem"].at[7 + half])
        then(1)

    def scatter_eight(to, own, out, inn, sem, totals):
        for n, way in enumerate((1, -1)):
            rows = rows_half(n)
            out[3, n, rows] = own(4)[n * HALF : (n + 1) * HALF].astype(BF16)
            send(out.at[3, n, rows], inn.at[3, n, rows], sem.at[3, n], to[2 * way])
        for n, way in enumerate((1, -1)):
            out[2, n] = own(3 * way).astype(BF16)
            send(out.at[2, n], inn.at[2, n], sem.at[2, n], to[way])
        for n, way in enumerate((1, -1)):
            out[0, n] = own(way).astype(BF16)
            send(out.at[0, n], inn.at[0, n], sem.at[0, n], to[way])
        yield
        for n, way in enumerate((1, -1)):
            rows = slice(n * HALF, (n + 1) * HALF)
            rest = slice((1 - n) * HALF, (2 - n) * HALF)
            value = own(2 * way)
            arrived(inn.at[2, n], sem.at[2, n])
            arrived(inn.at[3, n, rows_half(n)], sem.at[3, n])
            more = inn[2, n, rows].astype(F32) + inn[3, n, rows].astype(F32)
            out[1, n, rows] = (value[rows] + more).astype(BF16)
            out[1, n, rest] = (value[rest] + inn[2, n, rest].astype(F32)).astype(BF16)
            send(out.at[1, n], inn.at[1, n], sem.at[1, n], to[2 * way])
        value = own(0)
        yield
        for m in range(2):
            for n in range(2):
                arrived(inn.at[m, n], sem.at[m, n])
                value = value + inn[m, n].astype(F32)
        totals.append(value)

    def gather_four(to, ref, sem):
        for way in (1, -1):
            send(ref(0, None), ref(-way, None), sem.at[0 if way > 0 else 1], to[way])
        yield
        for way in (1, -1):
            n = 0 if way > 0 else 1
            arrived(ref(-way, None), sem.at[n])
            send(ref(-way, n), ref(2, n), sem.at[2 + n], to[way])
        yield
        for n in range(2):
            arrived(ref(2, n), sem.at[2 + n])

    def gather_direct(to, ref, sem):
        for way in (2, 1, -1):
            send(ref(0, None), ref(-way, None), sem.at[-way % 4], to[way])
        yield
        for k in (1, -1, 2):
            arrived(ref(k, None), sem.at[k % 4])

    def scatter_direct(to, src, mine_, inn, sem, totals):
        for way in (2, 1, -1):
            k = -way % 4
            send(src(way % 4), inn.at[k], sem.at[k], to[way])
        yield
        value = mine_()
        for k in (1, -1, 2):
            arrived(inn.at[k % 4], sem.at[k % 4])
            value = value + inn[k % 4].astype(F32)
        totals.append(value)

    def scatter_corner(t, own, name, totals):
        out, inn, end, side = (s[name + part] for part in ("_out", "_in", "_end", "_side"))
        sem, end_sem = s["f_sem"].at[t], s["end_sem"].at[t]
        for step in range(1, 5):
            if step > 1:
                yield
            for d, way in enumerate((1, -1)):
                if step == 1:
                    out[d, 0, d] = own(4 * way, d).astype(BF16)
                    send(out.at[d, 0, d], inn.at[d, 0, d], sem.at[d, 0], along_z[way])
                    continue
                before = inn.at[d, step - 2]
                arrived(before.at[d] if step == 2 else before, sem.at[d, step - 2])
                for half in range(2):
                    value = own(way * (5 - step), half)
                    if step > 2 or half == d:
                        value = value + inn[d, step - 2, half].astype(F32)
                    out[d, step - 1, half] = value.astype(BF16)
                    if step == 4:
                        origin = lax.rem(xl + half, 2)
                        send(out.at[d, 3, half], end.at[origin, d], end_sem.at[origin, d], corner[half, way])
                if step < 4:
                    send(out.at[d, step - 1], inn.at[d, step - 1], sem.at[d, step - 1], along_z[way])
            if step == 1:
                side[0] = own(0, 1 - xl).astype(BF16)
                send(side.at[0], side.at[1], s["h_sem"].at[t], near)
        value = own(0, xl)
        yield
        arrived(side.at[1], s["h_sem"].at[t])
        value = value + side[1].astype(F32)
        for origin in range(2):
            for d in range(2):
                arrived(end.at[origin, d], end_sem.at[origin, d])
                value = value + end[origin, d].astype(F32)
        totals.append(value)

    def load(src, dst, n):
        copy = pltpu.make_async_copy(src, dst, s["in_sem"].at[n])
        copy.start()
        return copy

    def load_rows(src, dst, k, n):
        rows = pl.ds(k * CHUNK, CHUNK)
        return load(src.at[rows], dst.at[rows], n)

    xi_load = load(xi_h, s["xi"], 0)
    wi_loads = [load_rows(wi_h, s["wi"], k, 1 + k) for k in range(FI // CHUNK)]
    xt_load = load(xt_h, s["xt"], 4)
    wt_loads = [load_rows(wt_h, s["wt"], k, 5 + k) for k in range(FT // CHUNK)]

    barrier = pltpu.get_barrier_semaphore()
    peers = [other_core, *along_x.values(), *along_y.values(), *along_z.values(), *corners]
    for to in peers:
        pl.semaphore_signal(barrier, inc=1, device_id=to, device_id_type=MESH)

    def partial(t, x_ref, w_ref, x_load, w_loads):
        x_load.wait()
        for k, w_load in enumerate(w_loads):
            w_load.wait()
            rows = slice(k * CHUNK, (k + 1) * CHUNK)
            part = dot_nn(x_ref[:, rows], w_ref[rows, :])
            s["part"][t] = part if k == 0 else s["part"][t] + part
            yield
        for h in range(2):
            rows = pl.ds(pl.multiple_of((h * 2 + oc) * SHARE, SHARE), SHARE)
            s["a_out"][t, h] = s["part"][t, rows, :].astype(BF16)
        send(s["a_out"].at[t], s["a_in"].at[t], s["a_sem"].at[t], other_core)

    def mine(t, h):
        rows = pl.ds(pl.multiple_of((h * 2 + co) * SHARE, SHARE), SHARE)
        got = s["a_in"][t, pl.ds(h, 1)].reshape(SHARE, EMB)
        return s["part"][t, rows, :] + got.astype(F32)

    def to_far(t):
        arrived(s["a_in"].at[t], s["a_sem"].at[t])
        s["b_out"][t] = mine(t, ox).astype(BF16)
        send(s["b_out"].at[t], s["b_in"].at[t], s["b_sem"].at[t], far)
        s["half"][t] = mine(t, xh)

    def exchange(t, x_ref, t_ref, width):
        for k, to in along_y.items():
            cols = pl.ds(pl.multiple_of(lax.rem(y + 4 + k, 4) * width, 128), width)
            send(x_ref.at[:, cols], t_ref.at[-k % 4], s["x_sem"].at[t, -k % 4], to)
        cols = pl.ds(pl.multiple_of(y * width, 128), width)
        t_ref[0] = x_ref[:, cols]

    image_part = partial(0, s["xi"], s["wi"], xi_load, wi_loads)
    text_part = partial(1, s["xt"], s["wt"], xt_load, wt_loads)
    for _ in wi_loads:
        next(image_part)
    pl.semaphore_wait(barrier, len(peers))
    next(image_part, None)
    for _ in text_part:
        pass
    to_far(0)
    exchange(0, s["xi"], s["ti"], FIY)
    to_far(1)
    exchange(1, s["xt"], s["tt"], FTY)

    def units(t):
        arrived(s["b_in"].at[t], s["b_sem"].at[t])
        e = s["half"][t] + s["b_in"][t].astype(F32)
        rs = lax.rsqrt(jnp.sum(e * e, axis=-1, keepdims=True) + EPS)
        s["emb"][t] = e
        s["rst"][t] = jnp.broadcast_to(rs, (SHARE, 128))
        return (e * rs).astype(BF16)

    def images_ring(w):
        if w == 0:
            s["iu"][0, 0] = units(0)
        cols = pl.ds(w * WIDE, WIDE)

        def one(k, half):
            at = (k % 4, 0) if w == 0 else (0, k % 4)
            return s["iu"].at[at + (pl.ds(0, SHARE), cols)]

        def four(k, half):
            at = (pl.ds(0, 4), k % 4) if w == 0 else (k % 4, pl.ds(0, 4))
            return s["iu"].at[at + (pl.ds(0, SHARE), cols)]

        first, second = (along_x, along_y) if w == 0 else (along_y, along_x)
        yield from gather_direct(first, one, s["iu_sem"].at[w, 0])
        yield from gather_direct(second, four, s["iu_sem"].at[w, 1])

    def texts_ring():
        s["tu"][0, 0] = units(1)

        def ref(k, half):
            rows = pl.ds(0, SHARE) if half is None else rows_half(half)
            return s["tu"].at[0, AROUND.index(k), rows]

        def sem(k):
            return s["tu_sem"].at[AROUND.index(k)]

        def across(part):
            slots = (pl.ds(0, 5), pl.ds(5, 3))[part]
            send(s["tu"].at[0, slots], s["tu"].at[1, slots], s["tc_sem"].at[part], other_core)

        yield from gather_eight(along_z, ref, sem, across)

    def turned(t, t_ref, m_ref, n_ref):
        for k in range(1, 4):
            arrived(t_ref.at[k], s["x_sem"].at[t, k])
        for n, core in enumerate((co, oc)):
            for k, dy in enumerate(ABOUT):
                for h in range(2):
                    at = (n * 8 + k * 2 + h) * SHARE
                    rows = pl.ds(pl.multiple_of((h * 2 + core) * SHARE, SHARE), SHARE)
                    m_ref[at : at + SHARE, :] = t_ref[dy % 4, rows, :]
            n_ref[n] = m_ref[n * 256 : (n + 1) * 256, :].T
            yield

    def towers():
        yield from turned(0, s["ti"], s["mi"], s["ni"])
        yield from turned(1, s["tt"], s["mt"], s["nt"])

    towers_task = towers()
    interleave(
        "tabwabtwatb",
        t=texts_ring(),
        a=images_ring(0),
        b=images_ring(1),
        w=(next(towers_task, None) for _ in range(2)),
    )

    heat, shift = heat_ref[0], shift_ref[0]
    mult = cot_ref[0] * heat / 8192.0

    def texts():
        return s["tu"][...].reshape(512, EMB)

    def images():
        return s["iu"][...].reshape(512, EMB)

    def coefficients(n):
        score = dot_nt(images(), s["tu"][n].reshape(256, EMB))
        value = jax.nn.sigmoid(heat * score + shift)
        if n == 0:
            row = lax.broadcasted_iota(jnp.int32, (512, 256), 0)
            col = lax.broadcasted_iota(jnp.int32, (512, 256), 1)
            value = value - ((row == col) & (row < SHARE)).astype(F32)
        s["coef"][:, n * 256 : (n + 1) * 256] = (mult * value).astype(BF16)

    def text_half(n, out):
        grad = dot_tn(s["coef"][:, n * 256 : (n + 1) * 256], images())
        out[...] = grad.reshape(8, SHARE, EMB).astype(out.dtype)

    coefficients(0)
    arrived(s["tu"].at[1, pl.ds(0, 5)], s["tc_sem"].at[0])
    arrived(s["tu"].at[1, pl.ds(5, 3)], s["tc_sem"].at[1])
    coefficients(1)
    text_half(1, s["c_out"])
    send(s["c_out"], s["c_in"], s["c_sem"], other_core)

    def back(t, grads, grad):
        rs = s["rst"][t][:, :1]
        u = s["emb"][t] * rs
        value = (grad - u * jnp.sum(u * grad, axis=-1, keepdims=True)) * rs
        grads[0, 0, pl.ds(xh, 1)] = value.astype(BF16).reshape(1, SHARE, EMB)

    def text_grad():
        text_half(0, s["own_t"])
        yield
        arrived(s["c_in"], s["c_sem"])

        def own(k):
            at = AROUND.index(k)
            return s["own_t"][at] + s["c_in"][at].astype(F32)

        totals = []
        yield from scatter_eight(along_z, own, s["d_out"], s["d_in"], s["d_sem"], totals)
        back(1, s["gt"], totals[0])

    def image_half(w):
        first, second = (along_y, along_x) if w == 0 else (along_x, along_y)
        out = s["e1_out"].at[w]
        grad = dot_nn(s["coef"][...], texts()[:, w * WIDE : (w + 1) * WIDE])
        out[...] = grad.astype(BF16).reshape(4, 4, SHARE, WIDE)

        def group(k):
            return out.at[:, k] if w == 0 else out.at[k]

        totals = []
        yield from scatter_direct(
            first, group, lambda: group(0)[...].astype(F32), s["e1_in"].at[w], s["e1_sem"].at[w], totals
        )
        line = s["e2_out"].at[w]
        line[...] = totals[0].astype(BF16)
        yield from scatter_direct(
            second, lambda k: line.at[k], lambda: totals[0][0], s["e2_in"].at[w], s["e2_sem"].at[w], totals
        )
        s["sum_i"][:, w * WIDE : (w + 1) * WIDE] = totals[1]

    def spread(t, grads, first_dot):
        def across(slots, h, n):
            send(grads.at[0, slots, h], grads.at[1, slots, h], s["gc_sem"].at[t, n], other_core)

        def ring(h, n):
            def ref(k, half):
                rows = pl.ds(0, SHARE) if half is None else rows_half(half)
                return grads.at[0, ABOUT.index(k if k != -2 else 2), h, rows]

            if n == 0:
                send(ref(0, None), ref(0, None), s["far_sem"].at[t], far)
            else:
                arrived(ref(0, None), s["far_sem"].at[t])
            task = gather_four(along_y, ref, s["g_sem"].at[t, n])
            next(task)
            yield
            next(task)
            if n == 1:
                across(pl.ds(0, 3), h, 1)
            yield
            yield from task
            across(pl.ds(0, 4) if n == 0 else pl.ds(3, 1), h, 2 * n)

        first, second = ring(xh, 0), ring(ox, 1)
        next(first)
        yield
        next(first)
        next(second)
        yield
        next(first, None)
        next(second)
        yield
        next(second, None)
        first_dot()
        yield
        for n, (h, slots) in enumerate(((xh, pl.ds(0, 4)), (ox, pl.ds(0, 3)), (ox, pl.ds(3, 1)))):
            arrived(grads.at[1, slots, h], s["gc_sem"].at[t, n])

    def weights(t, grads, n_ref, p_ref, own, names):
        def term(n):
            return dot_nn(n_ref[n], grads[n].reshape(256, EMB))

        def first_dot():
            p_ref[...] = term(0)

        yield from spread(t, grads, first_dot)
        p_ref[...] = p_ref[...] + term(1)
        totals = []
        ring = scatter_corner(t, own, names, totals)
        yield from ring
        return totals[0]

    def inputs(grads, w_ref, out):
        for k in range(0, w_ref.shape[0], CHUNK):
            cols = slice(k, k + CHUNK)
            value = dot_nt(grads[:, 0].reshape(ROWS, EMB), w_ref[cols, :]).astype(BF16)
            for n, core in enumerate((co, oc)):
                for h in range(2):
                    rows = pl.ds(pl.multiple_of((h * 2 + core) * SHARE, SHARE), SHARE)
                    at = (n * 2 + h) * SHARE
                    out[rows, cols] = value[at : at + SHARE]
            yield

    def drain():
        while True:
            for _ in range(len(sends) - len(drained)):
                drained.append(sends[len(drained)])
                drained[-1].wait_send()
            yield

    def own_i(k, half):
        n = half * 8 + lax.rem(z + 8 + k, 8)
        rows = s["pi"][pl.ds(pl.multiple_of(n * OI, 8), OI), :]
        return jnp.concatenate([rows[:, :WIDE], rows[:, WIDE:]], axis=0)

    def own_t(k, half):
        n = half * 8 + lax.rem(z + 8 + k, 8)
        return s["pt"][pl.ds(pl.multiple_of(n * OT, 8), OT), :]

    def texts_back():
        yield from text_grad()
        op_t[...] = yield from weights(1, s["gt"], s["nt"], s["pt"], own_t, "ft")

    def images_back():
        back(0, s["gi"], s["sum_i"][...])
        total = yield from weights(0, s["gi"], s["ni"], s["pi"], own_i, "fi")
        op_i[:, :WIDE] = total[:OI]
        op_i[:, WIDE:] = total[OI:]

    drains = drain()
    interleave(
        "abttwatbabitwititiittiptiotoiptowxiopxt",
        t=texts_back(),
        a=image_half(0),
        b=image_half(1),
        i=images_back(),
        w=towers_task,
        o=inputs(s["gi"], s["wi"], og_i),
        p=inputs(s["gt"], s["wt"], og_t),
        x=(next(drains) for _ in range(2)),
    )
    next(drains)


def per_device(xi, xt, wi, wt, heat, shift, cot):
    vmem = pl.BlockSpec(memory_space=pltpu.VMEM)
    smem = pl.BlockSpec(memory_space=pltpu.SMEM)
    hbm = pl.BlockSpec(memory_space=pl.ANY)
    shapes = (
        jax.ShapeDtypeStruct((ROWS, FI), BF16),
        jax.ShapeDtypeStruct((ROWS, FT), BF16),
        jax.ShapeDtypeStruct((OI, EMB), F32),
        jax.ShapeDtypeStruct((OT, EMB), F32),
    )
    return pl.pallas_call(
        kernel,
        out_shape=shapes,
        in_specs=[hbm] * 4 + [smem] * 3,
        out_specs=[vmem] * 4,
        scratch_shapes=list(scratch().values()),
        compiler_params=pltpu.CompilerParams(
            collective_id=0, has_side_effects=True, vmem_limit_bytes=55_250_000
        ),
    )(xi, xt, wi, wt, heat, shift, cot)


def solution(mesh):
    placed = (P("blk", "grp"), P("blk", "grp"), P("grp", None), P("grp", None), P(), P(), P())
    return jax.shard_map(
        per_device,
        mesh=mesh,
        in_specs=placed,
        out_specs=(
            P("blk", "grp"),
            P("blk", "grp"),
            P(("grp", "blk"), None),
            P(("grp", "blk"), None),
        ),
        check_vma=False,
    )
```

```python
import functools

import jax
import jax.numpy as jnp
from jax import lax
from jax.experimental import pallas as pl
from jax.experimental.pallas import tpu as pltpu
from jax.sharding import PartitionSpec as P

MESH = pl.DeviceIdType.MESH
F32 = jnp.float32
BF16 = jnp.bfloat16
EPS = 1e-06

ROWS = 128
SHARE = 32
HALF = 16
EMB = 1024
WIDE = 512
FI, FT = 1536, 1024
FIY, FTY = FI // 4, FT // 4
OI, OT = FIY // 16, FTY // 16
CHUNK = 512
SENDS = 112


def dot_nn(a, b):
    return lax.dot_general(a, b, (((1,), (0,)), ((), ())), preferred_element_type=F32)


def dot_nt(a, b):
    return lax.dot_general(a, b, (((1,), (1,)), ((), ())), preferred_element_type=F32)


def dot_tn(a, b):
    return lax.dot_general(a, b, (((0,), (0,)), ((), ())), preferred_element_type=F32)


def scratch():
    v = pltpu.VMEM
    dma = pltpu.SemaphoreType.DMA
    return dict(
        xi=v((ROWS, FI), BF16),
        xt=v((ROWS, FT), BF16),
        wi=v((FI, EMB), BF16),
        wt=v((FT, EMB), BF16),
        part=v((2, ROWS, EMB), F32),
        a_out=v((2, 2, SHARE, EMB), BF16),
        a_in=v((2, 2, SHARE, EMB), BF16),
        half=v((2, SHARE, EMB), F32),
        b_out=v((2, SHARE, EMB), BF16),
        b_in=v((2, SHARE, EMB), BF16),
        emb=v((2, SHARE, EMB), F32),
        rst=v((2, SHARE, 128), F32),
        iu=v((4, 4, SHARE, EMB), BF16),
        tu=v((2, 8, SHARE, EMB), BF16),
        coef=v((512, 512), BF16),
        c_out=v((8, SHARE, EMB), BF16),
        c_in=v((8, SHARE, EMB), BF16),
        own_t=v((8, SHARE, EMB), F32),
        d_out=v((4, 2, SHARE, EMB), BF16),
        d_in=v((4, 2, SHARE, EMB), BF16),
        e1_out=v((2, 4, 4, SHARE, WIDE), BF16),
        e1_in=v((2, 4, 4, SHARE, WIDE), BF16),
        e2_out=v((2, 4, SHARE, WIDE), BF16),
        e2_in=v((2, 4, SHARE, WIDE), BF16),
        sum_i=v((SHARE, EMB), F32),
        gi=v((2, 4, 2, SHARE, EMB), BF16),
        gt=v((2, 4, 2, SHARE, EMB), BF16),
        ti=v((4, ROWS, FIY), BF16),
        tt=v((4, ROWS, FTY), BF16),
        mi=v((512, FIY), BF16),
        mt=v((512, FTY), BF16),
        ni=v((2, FIY, 256), BF16),
        nt=v((2, FTY, 256), BF16),
        pi=v((FIY, EMB), F32),
        pt=v((FTY, EMB), F32),
        fi_out=v((2, 4, 2, 2 * OI, WIDE), BF16),
        fi_in=v((2, 3, 2, 2 * OI, WIDE), BF16),
        fi_end=v((2, 2, 2 * OI, WIDE), BF16),
        fi_side=v((2, 2 * OI, WIDE), BF16),
        ft_out=v((2, 4, 2, OT, EMB), BF16),
        ft_in=v((2, 3, 2, OT, EMB), BF16),
        ft_end=v((2, 2, OT, EMB), BF16),
        ft_side=v((2, OT, EMB), BF16),
        in_sem=dma((7,)),
        x_sem=dma((2, 4)),
        a_sem=dma((2,)),
        b_sem=dma((2,)),
        iu_sem=dma((2, 2, 4)),
        tu_sem=dma((9,)),
        tc_sem=dma((2,)),
        c_sem=dma,
        d_sem=dma((4, 2)),
        e1_sem=dma((2, 4)),
        e2_sem=dma((2, 4)),
        far_sem=dma((2,)),
        g_sem=dma((2, 2, 4)),
        gc_sem=dma((2, 3)),
        f_sem=dma((2, 2, 3)),
        end_sem=dma((2, 2, 2)),
        h_sem=dma((2,)),
        send_sem=dma((SENDS,)),
    )


NAMES = tuple(scratch())
AROUND = (0, 1, -1, 2, -2, 3, -3, 4)
ABOUT = (0, 1, -1, 2)


def rows_half(h):
    return pl.ds(h * HALF, HALF)


def interleave(order, **tasks):
    for name in order:
        next(tasks[name], None)
    left = list(tasks.values())
    while left:
        left = [task for task in left if next(task, True) is not True]


def kernel(xi_h, xt_h, wi_h, wt_h, heat_ref, shift_ref, cot_ref, og_i, og_t, op_i, op_t, *refs):
    s = dict(zip(NAMES, refs))
    g = lax.axis_index("grp")
    b = lax.axis_index("blk")
    xh, co = lax.div(g, 2), lax.rem(g, 2)
    y, xl, z = lax.div(b, 16), lax.rem(lax.div(b, 8), 2), lax.rem(b, 8)
    x = xh * 2 + xl
    oc, ox = 1 - co, 1 - xh

    def dev(x_, y_, z_, co_):
        return (lax.div(x_, 2) * 2 + co_, (y_ * 2 + lax.rem(x_, 2)) * 8 + z_)

    other_core = dev(x, y, z, oc)
    near = dev(xh * 2 + (1 - xl), y, z, co)
    along_x = {k: dev(lax.rem(x + 4 + k, 4), y, z, co) for k in (1, -1, 2)}
    far = along_x[2]
    along_y = {k: dev(x, lax.rem(y + 4 + k, 4), z, co) for k in (1, -1, 2)}
    along_z = {k: dev(x, y, lax.rem(z + 8 + k, 8), co) for k in (1, -1, 2, -2)}
    corner = {
        (h, k): dev(xh * 2 + h, y, lax.rem(z + 8 + k, 8), co) for h in range(2) for k in (1, -1)
    }
    corners = [dev(xh * 2 + (1 - xl), y, lax.rem(z + 8 + k, 8), co) for k in (1, -1)]

    sends, drained = [], []

    def send(src, dst, sem, to):
        copy = pltpu.make_async_remote_copy(
            src_ref=src,
            dst_ref=dst,
            send_sem=s["send_sem"].at[len(sends)],
            recv_sem=sem,
            device_id=to,
            device_id_type=MESH,
        )
        copy.start()
        sends.append(copy)

    def arrived(dst, sem):
        pltpu.make_async_copy(dst, dst, sem).wait()

    def gather_eight(to, ref, sem, then):
        for way in (2, -2, 1, -1):
            send(ref(0, None), ref(-way, None), sem(-way), to[way])
        yield
        for half, way in enumerate((1, -1)):
            far_ = -2 * way
            arrived(ref(far_, None), sem(far_))
            send(ref(far_, half), ref(4, half), s["tu_sem"].at[7 + half], to[2 * way])
            send(ref(far_, None), ref(-3 * way, None), sem(-3 * way), to[way])
        for k in (1, -1):
            arrived(ref(k, None), sem(k))
        then(0)
        yield
        for k in (3, -3):
            arrived(ref(k, None), sem(k))
        for half in range(2):
            arrived(ref(4, half), s["tu_sem"].at[7 + half])
        then(1)

    def scatter_eight(to, own, out, inn, sem, totals):
        for n, way in enumerate((1, -1)):
            rows = rows_half(n)
            out[3, n, rows] = own(4)[n * HALF : (n + 1) * HALF].astype(BF16)
            send(out.at[3, n, rows], inn.at[3, n, rows], sem.at[3, n], to[2 * way])
        for n, way in enumerate((1, -1)):
            out[2, n] = own(3 * way).astype(BF16)
            send(out.at[2, n], inn.at[2, n], sem.at[2, n], to[way])
        for n, way in enumerate((1, -1)):
            out[0, n] = own(way).astype(BF16)
            send(out.at[0, n], inn.at[0, n], sem.at[0, n], to[way])
        yield
        for n, way in enumerate((1, -1)):
            rows = slice(n * HALF, (n + 1) * HALF)
            rest = slice((1 - n) * HALF, (2 - n) * HALF)
            value = own(2 * way)
            arrived(inn.at[2, n], sem.at[2, n])
            arrived(inn.at[3, n, rows_half(n)], sem.at[3, n])
            more = inn[2, n, rows].astype(F32) + inn[3, n, rows].astype(F32)
            out[1, n, rows] = (value[rows] + more).astype(BF16)
            out[1, n, rest] = (value[rest] + inn[2, n, rest].astype(F32)).astype(BF16)
            send(out.at[1, n], inn.at[1, n], sem.at[1, n], to[2 * way])
        value = own(0)
        yield
        for m in range(2):
            for n in range(2):
                arrived(inn.at[m, n], sem.at[m, n])
                value = value + inn[m, n].astype(F32)
        totals.append(value)

    def gather_four(to, ref, sem):
        for way in (1, -1):
            send(ref(0, None), ref(-way, None), sem.at[0 if way > 0 else 1], to[way])
        yield
        for way in (1, -1):
            n = 0 if way > 0 else 1
            arrived(ref(-way, None), sem.at[n])
            send(ref(-way, n), ref(2, n), sem.at[2 + n], to[way])
        yield
        for n in range(2):
            arrived(ref(2, n), sem.at[2 + n])

    def gather_direct(to, ref, sem):
        for way in (2, 1, -1):
            send(ref(0, None), ref(-way, None), sem.at[-way % 4], to[way])
        yield
        for k in (1, -1, 2):
            arrived(ref(k, None), sem.at[k % 4])

    def scatter_direct(to, src, mine_, inn, sem, totals):
        for way in (2, 1, -1):
            k = -way % 4
            send(src(way % 4), inn.at[k], sem.at[k], to[way])
        yield
        value = mine_()
        for k in (1, -1, 2):
            arrived(inn.at[k % 4], sem.at[k % 4])
            value = value + inn[k % 4].astype(F32)
        totals.append(value)

    def scatter_corner(t, own, name, totals):
        out, inn, end, side = (s[name + part] for part in ("_out", "_in", "_end", "_side"))
        sem, end_sem = s["f_sem"].at[t], s["end_sem"].at[t]
        for step in range(1, 5):
            if step > 1:
                yield
            for d, way in enumerate((1, -1)):
                if step == 1:
                    out[d, 0, d] = own(4 * way, d).astype(BF16)
                    send(out.at[d, 0, d], inn.at[d, 0, d], sem.at[d, 0], along_z[way])
                    continue
                before = inn.at[d, step - 2]
                arrived(before.at[d] if step == 2 else before, sem.at[d, step - 2])
                for half in range(2):
                    value = own(way * (5 - step), half)
                    if step > 2 or half == d:
                        value = value + inn[d, step - 2, half].astype(F32)
                    out[d, step - 1, half] = value.astype(BF16)
                    if step == 4:
                        origin = lax.rem(xl + half, 2)
                        send(out.at[d, 3, half], end.at[origin, d], end_sem.at[origin, d], corner[half, way])
                if step < 4:
                    send(out.at[d, step - 1], inn.at[d, step - 1], sem.at[d, step - 1], along_z[way])
            if step == 1:
                side[0] = own(0, 1 - xl).astype(BF16)
                send(side.at[0], side.at[1], s["h_sem"].at[t], near)
        value = own(0, xl)
        yield
        arrived(side.at[1], s["h_sem"].at[t])
        value = value + side[1].astype(F32)
        for origin in range(2):
            for d in range(2):
                arrived(end.at[origin, d], end_sem.at[origin, d])
                value = value + end[origin, d].astype(F32)
        totals.append(value)

    def load(src, dst, n):
        copy = pltpu.make_async_copy(src, dst, s["in_sem"].at[n])
        copy.start()
        return copy

    def load_rows(src, dst, k, n):
        rows = pl.ds(k * CHUNK, CHUNK)
        return load(src.at[rows], dst.at[rows], n)

    xi_load = load(xi_h, s["xi"], 0)
    wi_loads = [load_rows(wi_h, s["wi"], k, 1 + k) for k in range(FI // CHUNK)]
    xt_load = load(xt_h, s["xt"], 4)
    wt_loads = [load_rows(wt_h, s["wt"], k, 5 + k) for k in range(FT // CHUNK)]

    barrier = pltpu.get_barrier_semaphore()
    peers = [other_core, *along_x.values(), *along_y.values(), *along_z.values(), *corners]
    for to in peers:
        pl.semaphore_signal(barrier, inc=1, device_id=to, device_id_type=MESH)

    def partial(t, x_ref, w_ref, x_load, w_loads):
        x_load.wait()
        for k, w_load in enumerate(w_loads):
            w_load.wait()
            rows = slice(k * CHUNK, (k + 1) * CHUNK)
            part = dot_nn(x_ref[:, rows], w_ref[rows, :])
            s["part"][t] = part if k == 0 else s["part"][t] + part
            yield
        for h in range(2):
            rows = pl.ds(pl.multiple_of((h * 2 + oc) * SHARE, SHARE), SHARE)
            s["a_out"][t, h] = s["part"][t, rows, :].astype(BF16)
        send(s["a_out"].at[t], s["a_in"].at[t], s["a_sem"].at[t], other_core)

    def mine(t, h):
        rows = pl.ds(pl.multiple_of((h * 2 + co) * SHARE, SHARE), SHARE)
        got = s["a_in"][t, pl.ds(h, 1)].reshape(SHARE, EMB)
        return s["part"][t, rows, :] + got.astype(F32)

    def to_far(t):
        arrived(s["a_in"].at[t], s["a_sem"].at[t])
        s["b_out"][t] = mine(t, ox).astype(BF16)
        send(s["b_out"].at[t], s["b_in"].at[t], s["b_sem"].at[t], far)
        s["half"][t] = mine(t, xh)

    def exchange(t, x_ref, t_ref, width):
        for k, to in along_y.items():
            cols = pl.ds(pl.multiple_of(lax.rem(y + 4 + k, 4) * width, 128), width)
            send(x_ref.at[:, cols], t_ref.at[-k % 4], s["x_sem"].at[t, -k % 4], to)
        cols = pl.ds(pl.multiple_of(y * width, 128), width)
        t_ref[0] = x_ref[:, cols]

    image_part = partial(0, s["xi"], s["wi"], xi_load, wi_loads)
    text_part = partial(1, s["xt"], s["wt"], xt_load, wt_loads)
    for _ in wi_loads:
        next(image_part)
    pl.semaphore_wait(barrier, len(peers))
    next(image_part, None)
    for _ in text_part:
        pass
    to_far(0)
    exchange(0, s["xi"], s["ti"], FIY)
    to_far(1)
    exchange(1, s["xt"], s["tt"], FTY)

    def units(t):
        arrived(s["b_in"].at[t], s["b_sem"].at[t])
        e = s["half"][t] + s["b_in"][t].astype(F32)
        rs = lax.rsqrt(jnp.sum(e * e, axis=-1, keepdims=True) + EPS)
        s["emb"][t] = e
        s["rst"][t] = jnp.broadcast_to(rs, (SHARE, 128))
        return (e * rs).astype(BF16)

    def images_ring(w):
        if w == 0:
            s["iu"][0, 0] = units(0)
        cols = pl.ds(w * WIDE, WIDE)

        def one(k, half):
            at = (k % 4, 0) if w == 0 else (0, k % 4)
            return s["iu"].at[at + (pl.ds(0, SHARE), cols)]

        def four(k, half):
            at = (pl.ds(0, 4), k % 4) if w == 0 else (k % 4, pl.ds(0, 4))
            return s["iu"].at[at + (pl.ds(0, SHARE), cols)]

        first, second = (along_x, along_y) if w == 0 else (along_y, along_x)
        yield from gather_direct(first, one, s["iu_sem"].at[w, 0])
        yield from gather_direct(second, four, s["iu_sem"].at[w, 1])

    def texts_ring():
        s["tu"][0, 0] = units(1)

        def ref(k, half):
            rows = pl.ds(0, SHARE) if half is None else rows_half(half)
            return s["tu"].at[0, AROUND.index(k), rows]

        def sem(k):
            return s["tu_sem"].at[AROUND.index(k)]

        def across(part):
            slots = (pl.ds(0, 5), pl.ds(5, 3))[part]
            send(s["tu"].at[0, slots], s["tu"].at[1, slots], s["tc_sem"].at[part], other_core)

        yield from gather_eight(along_z, ref, sem, across)

    def turned(t, t_ref, m_ref, n_ref):
        for k in range(1, 4):
            arrived(t_ref.at[k], s["x_sem"].at[t, k])
        for n, core in enumerate((co, oc)):
            for k, dy in enumerate(ABOUT):
                for h in range(2):
                    at = (n * 8 + k * 2 + h) * SHARE
                    rows = pl.ds(pl.multiple_of((h * 2 + core) * SHARE, SHARE), SHARE)
                    m_ref[at : at + SHARE, :] = t_ref[dy % 4, rows, :]
            n_ref[n] = m_ref[n * 256 : (n + 1) * 256, :].T
            yield

    def towers():
        yield from turned(0, s["ti"], s["mi"], s["ni"])
        yield from turned(1, s["tt"], s["mt"], s["nt"])

    towers_task = towers()
    interleave(
        "atbwwabtatb",
        t=texts_ring(),
        a=images_ring(0),
        b=images_ring(1),
        w=(next(towers_task, None) for _ in range(2)),
    )

    heat, shift = heat_ref[0], shift_ref[0]
    mult = cot_ref[0] * heat / 8192.0

    def texts():
        return s["tu"][...].reshape(512, EMB)

    def images():
        return s["iu"][...].reshape(512, EMB)

    def coefficients(n):
        score = dot_nt(images(), s["tu"][n].reshape(256, EMB))
        value = jax.nn.sigmoid(heat * score + shift)
        if n == 0:
            row = lax.broadcasted_iota(jnp.int32, (512, 256), 0)
            col = lax.broadcasted_iota(jnp.int32, (512, 256), 1)
            value = value - ((row == col) & (row < SHARE)).astype(F32)
        s["coef"][:, n * 256 : (n + 1) * 256] = (mult * value).astype(BF16)

    def text_half(n, out):
        grad = dot_tn(s["coef"][:, n * 256 : (n + 1) * 256], images())
        out[...] = grad.reshape(8, SHARE, EMB).astype(out.dtype)

    coefficients(0)
    arrived(s["tu"].at[1, pl.ds(0, 5)], s["tc_sem"].at[0])
    arrived(s["tu"].at[1, pl.ds(5, 3)], s["tc_sem"].at[1])
    coefficients(1)
    text_half(1, s["c_out"])
    send(s["c_out"], s["c_in"], s["c_sem"], other_core)

    def back(t, grads, grad):
        rs = s["rst"][t][:, :1]
        u = s["emb"][t] * rs
        value = (grad - u * jnp.sum(u * grad, axis=-1, keepdims=True)) * rs
        grads[0, 0, pl.ds(xh, 1)] = value.astype(BF16).reshape(1, SHARE, EMB)

    def text_grad():
        text_half(0, s["own_t"])
        yield
        arrived(s["c_in"], s["c_sem"])

        def own(k):
            at = AROUND.index(k)
            return s["own_t"][at] + s["c_in"][at].astype(F32)

        totals = []
        yield from scatter_eight(along_z, own, s["d_out"], s["d_in"], s["d_sem"], totals)
        back(1, s["gt"], totals[0])

    def image_half(w):
        first, second = (along_y, along_x) if w == 0 else (along_x, along_y)
        out = s["e1_out"].at[w]
        grad = dot_nn(s["coef"][...], texts()[:, w * WIDE : (w + 1) * WIDE])
        out[...] = grad.astype(BF16).reshape(4, 4, SHARE, WIDE)

        def group(k):
            return out.at[:, k] if w == 0 else out.at[k]

        totals = []
        yield from scatter_direct(
            first, group, lambda: group(0)[...].astype(F32), s["e1_in"].at[w], s["e1_sem"].at[w], totals
        )
        line = s["e2_out"].at[w]
        line[...] = totals[0].astype(BF16)
        yield from scatter_direct(
            second, lambda k: line.at[k], lambda: totals[0][0], s["e2_in"].at[w], s["e2_sem"].at[w], totals
        )
        s["sum_i"][:, w * WIDE : (w + 1) * WIDE] = totals[1]

    def spread(t, grads, first_dot):
        def across(slots, h, n):
            send(grads.at[0, slots, h], grads.at[1, slots, h], s["gc_sem"].at[t, n], other_core)

        def ring(h, n):
            def ref(k, half):
                rows = pl.ds(0, SHARE) if half is None else rows_half(half)
                return grads.at[0, ABOUT.index(k if k != -2 else 2), h, rows]

            if n == 0:
                send(ref(0, None), ref(0, None), s["far_sem"].at[t], far)
            else:
                arrived(ref(0, None), s["far_sem"].at[t])
            task = gather_four(along_y, ref, s["g_sem"].at[t, n])
            next(task)
            yield
            next(task)
            if n == 1:
                across(pl.ds(0, 3), h, 1)
            yield
            yield from task
            across(pl.ds(0, 4) if n == 0 else pl.ds(3, 1), h, 2 * n)

        first, second = ring(xh, 0), ring(ox, 1)
        next(first)
        yield
        next(first)
        next(second)
        yield
        next(first, None)
        next(second)
        yield
        next(second, None)
        first_dot()
        yield
        for n, (h, slots) in enumerate(((xh, pl.ds(0, 4)), (ox, pl.ds(0, 3)), (ox, pl.ds(3, 1)))):
            arrived(grads.at[1, slots, h], s["gc_sem"].at[t, n])

    def weights(t, grads, n_ref, p_ref, own, names):
        def term(n):
            return dot_nn(n_ref[n], grads[n].reshape(256, EMB))

        def first_dot():
            p_ref[...] = term(0)

        yield from spread(t, grads, first_dot)
        p_ref[...] = p_ref[...] + term(1)
        totals = []
        ring = scatter_corner(t, own, names, totals)
        yield from ring
        return totals[0]

    def inputs(grads, w_ref, out):
        for k in range(0, w_ref.shape[0], CHUNK):
            cols = slice(k, k + CHUNK)
            value = dot_nt(grads[:, 0].reshape(ROWS, EMB), w_ref[cols, :]).astype(BF16)
            for n, core in enumerate((co, oc)):
                for h in range(2):
                    rows = pl.ds(pl.multiple_of((h * 2 + core) * SHARE, SHARE), SHARE)
                    at = (n * 2 + h) * SHARE
                    out[rows, cols] = value[at : at + SHARE]
            yield

    def drain():
        while True:
            for _ in range(len(sends) - len(drained)):
                drained.append(sends[len(drained)])
                drained[-1].wait_send()
            yield

    def own_i(k, half):
        n = half * 8 + lax.rem(z + 8 + k, 8)
        rows = s["pi"][pl.ds(pl.multiple_of(n * OI, 8), OI), :]
        return jnp.concatenate([rows[:, :WIDE], rows[:, WIDE:]], axis=0)

    def own_t(k, half):
        n = half * 8 + lax.rem(z + 8 + k, 8)
        return s["pt"][pl.ds(pl.multiple_of(n * OT, 8), OT), :]

    def texts_back():
        yield from text_grad()
        op_t[...] = yield from weights(1, s["gt"], s["nt"], s["pt"], own_t, "ft")

    def images_back():
        back(0, s["gi"], s["sum_i"][...])
        total = yield from weights(0, s["gi"], s["ni"], s["pi"], own_i, "fi")
        op_i[:, :WIDE] = total[:OI]
        op_i[:, WIDE:] = total[OI:]

    drains = drain()
    interleave(
        "battbtabaiwtititwititioptiotpoitwxixtop",
        t=texts_back(),
        a=image_half(0),
        b=image_half(1),
        i=images_back(),
        w=towers_task,
        o=inputs(s["gi"], s["wi"], og_i),
        p=inputs(s["gt"], s["wt"], og_t),
        x=(next(drains) for _ in range(2)),
    )
    next(drains)


def per_device(xi, xt, wi, wt, heat, shift, cot):
    vmem = pl.BlockSpec(memory_space=pltpu.VMEM)
    smem = pl.BlockSpec(memory_space=pltpu.SMEM)
    hbm = pl.BlockSpec(memory_space=pl.ANY)
    shapes = (
        jax.ShapeDtypeStruct((ROWS, FI), BF16),
        jax.ShapeDtypeStruct((ROWS, FT), BF16),
        jax.ShapeDtypeStruct((OI, EMB), F32),
        jax.ShapeDtypeStruct((OT, EMB), F32),
    )
    return pl.pallas_call(
        kernel,
        out_shape=shapes,
        in_specs=[hbm] * 4 + [smem] * 3,
        out_specs=[vmem] * 4,
        scratch_shapes=list(scratch().values()),
        compiler_params=pltpu.CompilerParams(
            collective_id=0, has_side_effects=True, vmem_limit_bytes=55_250_000
        ),
    )(xi, xt, wi, wt, heat, shift, cot)


def solution(mesh):
    placed = (P("blk", "grp"), P("blk", "grp"), P("grp", None), P("grp", None), P(), P(), P())
    return jax.shard_map(
        per_device,
        mesh=mesh,
        in_specs=placed,
        out_specs=(
            P("blk", "grp"),
            P("blk", "grp"),
            P(("grp", "blk"), None),
            P(("grp", "blk"), None),
        ),
        check_vma=False,
    )
```

```python
import functools

import jax
import jax.numpy as jnp
from jax import lax
from jax.experimental import pallas as pl
from jax.experimental.pallas import tpu as pltpu
from jax.sharding import PartitionSpec as P

MESH = pl.DeviceIdType.MESH
F32 = jnp.float32
BF16 = jnp.bfloat16
EPS = 1e-06

ROWS = 128
SHARE = 32
HALF = 16
EMB = 1024
WIDE = 512
FI, FT = 1536, 1024
FIY, FTY = FI // 4, FT // 4
OI, OT = FIY // 16, FTY // 16
CHUNK = 512
SENDS = 112


def dot_nn(a, b):
    return lax.dot_general(a, b, (((1,), (0,)), ((), ())), preferred_element_type=F32)


def dot_nt(a, b):
    return lax.dot_general(a, b, (((1,), (1,)), ((), ())), preferred_element_type=F32)


def dot_tn(a, b):
    return lax.dot_general(a, b, (((0,), (0,)), ((), ())), preferred_element_type=F32)


def scratch():
    v = pltpu.VMEM
    dma = pltpu.SemaphoreType.DMA
    return dict(
        xi=v((ROWS, FI), BF16),
        xt=v((ROWS, FT), BF16),
        wi=v((FI, EMB), BF16),
        wt=v((FT, EMB), BF16),
        part=v((2, ROWS, EMB), F32),
        a_out=v((2, 2, SHARE, EMB), BF16),
        a_in=v((2, 2, SHARE, EMB), BF16),
        half=v((2, SHARE, EMB), F32),
        b_out=v((2, SHARE, EMB), BF16),
        b_in=v((2, SHARE, EMB), BF16),
        emb=v((2, SHARE, EMB), F32),
        rst=v((2, SHARE, 128), F32),
        iu=v((4, 4, SHARE, EMB), BF16),
        tu=v((2, 8, SHARE, EMB), BF16),
        coef=v((512, 512), BF16),
        c_out=v((8, SHARE, EMB), BF16),
        c_in=v((8, SHARE, EMB), BF16),
        own_t=v((8, SHARE, EMB), F32),
        d_out=v((4, 2, SHARE, EMB), BF16),
        d_in=v((4, 2, SHARE, EMB), BF16),
        e1_out=v((2, 4, 4, SHARE, WIDE), BF16),
        e1_in=v((2, 4, 4, SHARE, WIDE), BF16),
        e2_out=v((2, 4, SHARE, WIDE), BF16),
        e2_in=v((2, 4, SHARE, WIDE), BF16),
        sum_i=v((SHARE, EMB), F32),
        gi=v((2, 4, 2, SHARE, EMB), BF16),
        gt=v((2, 4, 2, SHARE, EMB), BF16),
        ti=v((4, ROWS, FIY), BF16),
        tt=v((4, ROWS, FTY), BF16),
        mi=v((512, FIY), BF16),
        mt=v((512, FTY), BF16),
        ni=v((2, FIY, 256), BF16),
        nt=v((2, FTY, 256), BF16),
        pi=v((FIY, EMB), F32),
        pt=v((FTY, EMB), F32),
        fi_out=v((2, 4, 2, 2 * OI, WIDE), BF16),
        fi_in=v((2, 3, 2, 2 * OI, WIDE), BF16),
        fi_end=v((2, 2, 2 * OI, WIDE), BF16),
        fi_side=v((2, 2 * OI, WIDE), BF16),
        ft_out=v((2, 4, 2, OT, EMB), BF16),
        ft_in=v((2, 3, 2, OT, EMB), BF16),
        ft_end=v((2, 2, OT, EMB), BF16),
        ft_side=v((2, OT, EMB), BF16),
        in_sem=dma((5,)),
        x_sem=dma((2, 4)),
        a_sem=dma((2,)),
        b_sem=dma((2,)),
        iu_sem=dma((2, 2, 4)),
        tu_sem=dma((9,)),
        tc_sem=dma((2,)),
        c_sem=dma,
        d_sem=dma((4, 2)),
        e1_sem=dma((2, 4)),
        e2_sem=dma((2, 4)),
        far_sem=dma((2,)),
        g_sem=dma((2, 2, 4)),
        gc_sem=dma((2, 3)),
        f_sem=dma((2, 2, 3)),
        end_sem=dma((2, 2, 2)),
        h_sem=dma((2,)),
        send_sem=dma((SENDS,)),
    )


NAMES = tuple(scratch())
AROUND = (0, 1, -1, 2, -2, 3, -3, 4)
ABOUT = (0, 1, -1, 2)


def rows_half(h):
    return pl.ds(h * HALF, HALF)


def interleave(order, **tasks):
    for name in order:
        next(tasks[name], None)
    left = list(tasks.values())
    while left:
        left = [task for task in left if next(task, True) is not True]


def kernel(xi_h, xt_h, wi_h, wt_h, heat_ref, shift_ref, cot_ref, og_i, og_t, op_i, op_t, *refs):
    s = dict(zip(NAMES, refs))
    g = lax.axis_index("grp")
    b = lax.axis_index("blk")
    xh, co = lax.div(g, 2), lax.rem(g, 2)
    y, xl, z = lax.div(b, 16), lax.rem(lax.div(b, 8), 2), lax.rem(b, 8)
    x = xh * 2 + xl
    oc, ox = 1 - co, 1 - xh

    def dev(x_, y_, z_, co_):
        return (lax.div(x_, 2) * 2 + co_, (y_ * 2 + lax.rem(x_, 2)) * 8 + z_)

    other_core = dev(x, y, z, oc)
    near = dev(xh * 2 + (1 - xl), y, z, co)
    along_x = {k: dev(lax.rem(x + 4 + k, 4), y, z, co) for k in (1, -1, 2)}
    far = along_x[2]
    along_y = {k: dev(x, lax.rem(y + 4 + k, 4), z, co) for k in (1, -1, 2)}
    along_z = {k: dev(x, y, lax.rem(z + 8 + k, 8), co) for k in (1, -1, 2, -2)}
    corner = {
        (h, k): dev(xh * 2 + h, y, lax.rem(z + 8 + k, 8), co) for h in range(2) for k in (1, -1)
    }
    corners = [dev(xh * 2 + (1 - xl), y, lax.rem(z + 8 + k, 8), co) for k in (1, -1)]

    sends, drained = [], []

    def send(src, dst, sem, to):
        copy = pltpu.make_async_remote_copy(
            src_ref=src,
            dst_ref=dst,
            send_sem=s["send_sem"].at[len(sends)],
            recv_sem=sem,
            device_id=to,
            device_id_type=MESH,
        )
        copy.start()
        sends.append(copy)

    def arrived(dst, sem):
        pltpu.make_async_copy(dst, dst, sem).wait()

    def gather_eight(to, ref, sem, then):
        for way in (2, -2, 1, -1):
            send(ref(0, None), ref(-way, None), sem(-way), to[way])
        yield
        for half, way in enumerate((1, -1)):
            far_ = -2 * way
            arrived(ref(far_, None), sem(far_))
            send(ref(far_, half), ref(4, half), s["tu_sem"].at[7 + half], to[2 * way])
            send(ref(far_, None), ref(-3 * way, None), sem(-3 * way), to[way])
        for k in (1, -1):
            arrived(ref(k, None), sem(k))
        then(0)
        yield
        for k in (3, -3):
            arrived(ref(k, None), sem(k))
        for half in range(2):
            arrived(ref(4, half), s["tu_sem"].at[7 + half])
        then(1)

    def scatter_eight(to, own, out, inn, sem, totals):
        for n, way in enumerate((1, -1)):
            rows = rows_half(n)
            out[3, n, rows] = own(4)[n * HALF : (n + 1) * HALF].astype(BF16)
            send(out.at[3, n, rows], inn.at[3, n, rows], sem.at[3, n], to[2 * way])
        for n, way in enumerate((1, -1)):
            out[2, n] = own(3 * way).astype(BF16)
            send(out.at[2, n], inn.at[2, n], sem.at[2, n], to[way])
        for n, way in enumerate((1, -1)):
            out[0, n] = own(way).astype(BF16)
            send(out.at[0, n], inn.at[0, n], sem.at[0, n], to[way])
        yield
        for n, way in enumerate((1, -1)):
            rows = slice(n * HALF, (n + 1) * HALF)
            rest = slice((1 - n) * HALF, (2 - n) * HALF)
            value = own(2 * way)
            arrived(inn.at[2, n], sem.at[2, n])
            arrived(inn.at[3, n, rows_half(n)], sem.at[3, n])
            more = inn[2, n, rows].astype(F32) + inn[3, n, rows].astype(F32)
            out[1, n, rows] = (value[rows] + more).astype(BF16)
            out[1, n, rest] = (value[rest] + inn[2, n, rest].astype(F32)).astype(BF16)
            send(out.at[1, n], inn.at[1, n], sem.at[1, n], to[2 * way])
        value = own(0)
        yield
        for m in range(2):
            for n in range(2):
                arrived(inn.at[m, n], sem.at[m, n])
                value = value + inn[m, n].astype(F32)
        totals.append(value)

    def gather_four(to, ref, sem):
        for way in (1, -1):
            send(ref(0, None), ref(-way, None), sem.at[0 if way > 0 else 1], to[way])
        yield
        for way in (1, -1):
            n = 0 if way > 0 else 1
            arrived(ref(-way, None), sem.at[n])
            send(ref(-way, n), ref(2, n), sem.at[2 + n], to[way])
        yield
        for n in range(2):
            arrived(ref(2, n), sem.at[2 + n])

    def gather_direct(to, ref, sem):
        for way in (2, 1, -1):
            send(ref(0, None), ref(-way, None), sem.at[-way % 4], to[way])
        yield
        for k in (1, -1, 2):
            arrived(ref(k, None), sem.at[k % 4])

    def scatter_direct(to, src, mine_, inn, sem, totals):
        for way in (2, 1, -1):
            k = -way % 4
            send(src(way % 4), inn.at[k], sem.at[k], to[way])
        yield
        value = mine_()
        for k in (1, -1, 2):
            arrived(inn.at[k % 4], sem.at[k % 4])
            value = value + inn[k % 4].astype(F32)
        totals.append(value)

    def scatter_corner(t, own, name, totals):
        out, inn, end, side = (s[name + part] for part in ("_out", "_in", "_end", "_side"))
        sem, end_sem = s["f_sem"].at[t], s["end_sem"].at[t]
        for step in range(1, 5):
            if step > 1:
                yield
            for d, way in enumerate((1, -1)):
                if step == 1:
                    out[d, 0, d] = own(4 * way, d).astype(BF16)
                    send(out.at[d, 0, d], inn.at[d, 0, d], sem.at[d, 0], along_z[way])
                    continue
                before = inn.at[d, step - 2]
                arrived(before.at[d] if step == 2 else before, sem.at[d, step - 2])
                for half in range(2):
                    value = own(way * (5 - step), half)
                    if step > 2 or half == d:
                        value = value + inn[d, step - 2, half].astype(F32)
                    out[d, step - 1, half] = value.astype(BF16)
                    if step == 4:
                        origin = lax.rem(xl + half, 2)
                        send(out.at[d, 3, half], end.at[origin, d], end_sem.at[origin, d], corner[half, way])
                if step < 4:
                    send(out.at[d, step - 1], inn.at[d, step - 1], sem.at[d, step - 1], along_z[way])
            if step == 1:
                side[0] = own(0, 1 - xl).astype(BF16)
                send(side.at[0], side.at[1], s["h_sem"].at[t], near)
        value = own(0, xl)
        yield
        arrived(side.at[1], s["h_sem"].at[t])
        value = value + side[1].astype(F32)
        for origin in range(2):
            for d in range(2):
                arrived(end.at[origin, d], end_sem.at[origin, d])
                value = value + end[origin, d].astype(F32)
        totals.append(value)

    def load(src, dst, n):
        copy = pltpu.make_async_copy(src, dst, s["in_sem"].at[n])
        copy.start()
        return copy

    def load_rows(src, dst, at, size, n):
        rows = pl.ds(at, size)
        return slice(at, at + size), load(src.at[rows], dst.at[rows], n)

    xi_load = load(xi_h, s["xi"], 0)
    wi_loads = [load_rows(wi_h, s["wi"], 0, FI // 2, 1), load_rows(wi_h, s["wi"], FI // 2, FI // 2, 2)]

    barrier = pltpu.get_barrier_semaphore()
    peers = [other_core, *along_x.values(), *along_y.values(), *along_z.values(), *corners]
    for to in peers:
        pl.semaphore_signal(barrier, inc=1, device_id=to, device_id_type=MESH)

    xt_load = load(xt_h, s["xt"], 3)
    wt_loads = [load_rows(wt_h, s["wt"], 0, FT, 4)]

    def partial(t, x_ref, w_ref, x_load, w_loads):
        x_load.wait()
        for k, (rows, w_load) in enumerate(w_loads):
            w_load.wait()
            part = dot_nn(x_ref[:, rows], w_ref[rows, :])
            s["part"][t] = part if k == 0 else s["part"][t] + part
            yield
        for h in range(2):
            rows = pl.ds(pl.multiple_of((h * 2 + oc) * SHARE, SHARE), SHARE)
            s["a_out"][t, h] = s["part"][t, rows, :].astype(BF16)
        send(s["a_out"].at[t], s["a_in"].at[t], s["a_sem"].at[t], other_core)

    def mine(t, h):
        rows = pl.ds(pl.multiple_of((h * 2 + co) * SHARE, SHARE), SHARE)
        got = s["a_in"][t, pl.ds(h, 1)].reshape(SHARE, EMB)
        return s["part"][t, rows, :] + got.astype(F32)

    def to_far(t):
        arrived(s["a_in"].at[t], s["a_sem"].at[t])
        s["b_out"][t] = mine(t, ox).astype(BF16)
        send(s["b_out"].at[t], s["b_in"].at[t], s["b_sem"].at[t], far)
        s["half"][t] = mine(t, xh)

    def exchange(t, x_ref, t_ref, width):
        for k, to in along_y.items():
            cols = pl.ds(pl.multiple_of(lax.rem(y + 4 + k, 4) * width, 128), width)
            send(x_ref.at[:, cols], t_ref.at[-k % 4], s["x_sem"].at[t, -k % 4], to)
        cols = pl.ds(pl.multiple_of(y * width, 128), width)
        t_ref[0] = x_ref[:, cols]

    image_part = partial(0, s["xi"], s["wi"], xi_load, wi_loads)
    text_part = partial(1, s["xt"], s["wt"], xt_load, wt_loads)
    for _ in wi_loads:
        next(image_part)
    pl.semaphore_wait(barrier, len(peers))
    next(image_part, None)
    for _ in text_part:
        pass
    to_far(0)
    exchange(0, s["xi"], s["ti"], FIY)
    to_far(1)
    exchange(1, s["xt"], s["tt"], FTY)

    def units(t):
        arrived(s["b_in"].at[t], s["b_sem"].at[t])
        e = s["half"][t] + s["b_in"][t].astype(F32)
        rs = lax.rsqrt(jnp.sum(e * e, axis=-1, keepdims=True) + EPS)
        s["emb"][t] = e
        s["rst"][t] = jnp.broadcast_to(rs, (SHARE, 128))
        return (e * rs).astype(BF16)

    def images_ring(w):
        if w == 0:
            s["iu"][0, 0] = units(0)
        cols = pl.ds(w * WIDE, WIDE)

        def one(k, half):
            at = (k % 4, 0) if w == 0 else (0, k % 4)
            return s["iu"].at[at + (pl.ds(0, SHARE), cols)]

        def four(k, half):
            at = (pl.ds(0, 4), k % 4) if w == 0 else (k % 4, pl.ds(0, 4))
            return s["iu"].at[at + (pl.ds(0, SHARE), cols)]

        first, second = (along_x, along_y) if w == 0 else (along_y, along_x)
        yield from gather_direct(first, one, s["iu_sem"].at[w, 0])
        yield from gather_direct(second, four, s["iu_sem"].at[w, 1])

    def texts_ring():
        s["tu"][0, 0] = units(1)

        def ref(k, half):
            rows = pl.ds(0, SHARE) if half is None else rows_half(half)
            return s["tu"].at[0, AROUND.index(k), rows]

        def sem(k):
            return s["tu_sem"].at[AROUND.index(k)]

        def across(part):
            slots = (pl.ds(0, 5), pl.ds(5, 3))[part]
            send(s["tu"].at[0, slots], s["tu"].at[1, slots], s["tc_sem"].at[part], other_core)

        yield from gather_eight(along_z, ref, sem, across)

    def turned(t, t_ref, m_ref, n_ref):
        for k in range(1, 4):
            arrived(t_ref.at[k], s["x_sem"].at[t, k])
        for n, core in enumerate((co, oc)):
            for k, dy in enumerate(ABOUT):
                for h in range(2):
                    at = (n * 8 + k * 2 + h) * SHARE
                    rows = pl.ds(pl.multiple_of((h * 2 + core) * SHARE, SHARE), SHARE)
                    m_ref[at : at + SHARE, :] = t_ref[dy % 4, rows, :]
            n_ref[n] = m_ref[n * 256 : (n + 1) * 256, :].T
            yield

    def towers():
        yield from turned(0, s["ti"], s["mi"], s["ni"])
        yield from turned(1, s["tt"], s["mt"], s["nt"])

    towers_task = towers()
    interleave(
        "tabwabtwatb",
        t=texts_ring(),
        a=images_ring(0),
        b=images_ring(1),
        w=(next(towers_task, None) for _ in range(2)),
    )

    heat, shift = heat_ref[0], shift_ref[0]
    mult = cot_ref[0] * heat / 8192.0

    def texts():
        return s["tu"][...].reshape(512, EMB)

    def images():
        return s["iu"][...].reshape(512, EMB)

    def coefficients(n):
        score = dot_nt(images(), s["tu"][n].reshape(256, EMB))
        value = jax.nn.sigmoid(heat * score + shift)
        s["coef"][:, n * 256 : (n + 1) * 256] = (mult * value).astype(BF16)
        if n == 0:
            row = lax.broadcasted_iota(jnp.int32, (SHARE, 128), 0)
            col = lax.broadcasted_iota(jnp.int32, (SHARE, 128), 1)
            own = value[:SHARE, :128] - (row == col).astype(F32)
            s["coef"][:SHARE, :128] = (mult * own).astype(BF16)

    def text_half(n, out):
        grad = dot_tn(s["coef"][:, n * 256 : (n + 1) * 256], images())
        out[...] = grad.reshape(8, SHARE, EMB).astype(out.dtype)

    coefficients(0)
    arrived(s["tu"].at[1, pl.ds(0, 5)], s["tc_sem"].at[0])
    arrived(s["tu"].at[1, pl.ds(5, 3)], s["tc_sem"].at[1])
    coefficients(1)
    text_half(1, s["c_out"])
    send(s["c_out"], s["c_in"], s["c_sem"], other_core)

    def back(t, grads, grad):
        rs = s["rst"][t][:, :1]
        u = s["emb"][t] * rs
        value = (grad - u * jnp.sum(u * grad, axis=-1, keepdims=True)) * rs
        grads[0, 0, pl.ds(xh, 1)] = value.astype(BF16).reshape(1, SHARE, EMB)

    def text_grad():
        text_half(0, s["own_t"])
        yield
        arrived(s["c_in"], s["c_sem"])

        def own(k):
            at = AROUND.index(k)
            return s["own_t"][at] + s["c_in"][at].astype(F32)

        totals = []
        yield from scatter_eight(along_z, own, s["d_out"], s["d_in"], s["d_sem"], totals)
        back(1, s["gt"], totals[0])

    def image_half(w):
        first, second = (along_y, along_x) if w == 0 else (along_x, along_y)
        out = s["e1_out"].at[w]
        grad = dot_nn(s["coef"][...], texts()[:, w * WIDE : (w + 1) * WIDE])
        out[...] = grad.astype(BF16).reshape(4, 4, SHARE, WIDE)

        def group(k):
            return out.at[:, k] if w == 0 else out.at[k]

        totals = []
        yield from scatter_direct(
            first, group, lambda: group(0)[...].astype(F32), s["e1_in"].at[w], s["e1_sem"].at[w], totals
        )
        line = s["e2_out"].at[w]
        line[...] = totals[0].astype(BF16)
        yield from scatter_direct(
            second, lambda k: line.at[k], lambda: totals[0][0], s["e2_in"].at[w], s["e2_sem"].at[w], totals
        )
        s["sum_i"][:, w * WIDE : (w + 1) * WIDE] = totals[1]

    def spread(t, grads, first_dot):
        def across(slots, h, n):
            send(grads.at[0, slots, h], grads.at[1, slots, h], s["gc_sem"].at[t, n], other_core)

        def ring(h, n):
            def ref(k, half):
                rows = pl.ds(0, SHARE) if half is None else rows_half(half)
                return grads.at[0, ABOUT.index(k if k != -2 else 2), h, rows]

            if n == 0:
                send(ref(0, None), ref(0, None), s["far_sem"].at[t], far)
            else:
                arrived(ref(0, None), s["far_sem"].at[t])
            task = gather_four(along_y, ref, s["g_sem"].at[t, n])
            next(task)
            yield
            next(task)
            if n == 1:
                across(pl.ds(0, 3), h, 1)
            yield
            yield from task
            across(pl.ds(0, 4) if n == 0 else pl.ds(3, 1), h, 2 * n)

        first, second = ring(xh, 0), ring(ox, 1)
        next(first)
        yield
        next(first)
        next(second)
        yield
        next(first, None)
        next(second)
        yield
        next(second, None)
        first_dot()
        yield
        for n, (h, slots) in enumerate(((xh, pl.ds(0, 4)), (ox, pl.ds(0, 3)), (ox, pl.ds(3, 1)))):
            arrived(grads.at[1, slots, h], s["gc_sem"].at[t, n])

    def weights(t, grads, n_ref, p_ref, own, names):
        def term(n):
            return dot_nn(n_ref[n], grads[n].reshape(256, EMB))

        def first_dot():
            p_ref[...] = term(0)

        yield from spread(t, grads, first_dot)
        p_ref[...] = p_ref[...] + term(1)
        totals = []
        ring = scatter_corner(t, own, names, totals)
        yield from ring
        return totals[0]

    def inputs(grads, w_ref, out):
        for k in range(0, w_ref.shape[0], CHUNK):
            cols = slice(k, k + CHUNK)
            value = dot_nt(grads[:, 0].reshape(ROWS, EMB), w_ref[cols, :]).astype(BF16)
            for n, core in enumerate((co, oc)):
                for h in range(2):
                    rows = pl.ds(pl.multiple_of((h * 2 + core) * SHARE, SHARE), SHARE)
                    at = (n * 2 + h) * SHARE
                    out[rows, cols] = value[at : at + SHARE]
            yield

    def drain():
        while True:
            for _ in range(len(sends) - len(drained)):
                drained.append(sends[len(drained)])
                drained[-1].wait_send()
            yield

    def own_i(k, half):
        n = half * 8 + lax.rem(z + 8 + k, 8)
        rows = s["pi"][pl.ds(pl.multiple_of(n * OI, 8), OI), :]
        return jnp.concatenate([rows[:, :WIDE], rows[:, WIDE:]], axis=0)

    def own_t(k, half):
        n = half * 8 + lax.rem(z + 8 + k, 8)
        return s["pt"][pl.ds(pl.multiple_of(n * OT, 8), OT), :]

    def texts_back():
        yield from text_grad()
        op_t[...] = yield from weights(1, s["gt"], s["nt"], s["pt"], own_t, "ft")

    def images_back():
        back(0, s["gi"], s["sum_i"][...])
        total = yield from weights(0, s["gi"], s["ni"], s["pi"], own_i, "fi")
        op_i[:, :WIDE] = total[:OI]
        op_i[:, WIDE:] = total[OI:]

    drains = drain()
    interleave(
        "abttwatbabitwititiittiptiotoiptowxiopxt",
        t=texts_back(),
        a=image_half(0),
        b=image_half(1),
        i=images_back(),
        w=towers_task,
        o=inputs(s["gi"], s["wi"], og_i),
        p=inputs(s["gt"], s["wt"], og_t),
        x=(next(drains) for _ in range(2)),
    )
    next(drains)


def per_device(xi, xt, wi, wt, heat, shift, cot):
    vmem = pl.BlockSpec(memory_space=pltpu.VMEM)
    smem = pl.BlockSpec(memory_space=pltpu.SMEM)
    hbm = pl.BlockSpec(memory_space=pl.ANY)
    shapes = (
        jax.ShapeDtypeStruct((ROWS, FI), BF16),
        jax.ShapeDtypeStruct((ROWS, FT), BF16),
        jax.ShapeDtypeStruct((OI, EMB), F32),
        jax.ShapeDtypeStruct((OT, EMB), F32),
    )
    return pl.pallas_call(
        kernel,
        out_shape=shapes,
        in_specs=[hbm] * 4 + [smem] * 3,
        out_specs=[vmem] * 4,
        scratch_shapes=list(scratch().values()),
        compiler_params=pltpu.CompilerParams(
            collective_id=0, has_side_effects=True, vmem_limit_bytes=55_250_000
        ),
    )(xi, xt, wi, wt, heat, shift, cot)


def solution(mesh):
    placed = (P("blk", "grp"), P("blk", "grp"), P("grp", None), P("grp", None), P(), P(), P())
    return jax.shard_map(
        per_device,
        mesh=mesh,
        in_specs=placed,
        out_specs=(
            P("blk", "grp"),
            P("blk", "grp"),
            P(("grp", "blk"), None),
            P(("grp", "blk"), None),
        ),
        check_vma=False,
    )
```

```python
import functools

import jax
import jax.numpy as jnp
from jax import lax
from jax.experimental import pallas as pl
from jax.experimental.pallas import tpu as pltpu
from jax.sharding import PartitionSpec as P

MESH = pl.DeviceIdType.MESH
F32 = jnp.float32
BF16 = jnp.bfloat16
EPS = 1e-06

ROWS = 128
SHARE = 32
HALF = 16
EMB = 1024
WIDE = 512
FI, FT = 1536, 1024
FIY, FTY = FI // 4, FT // 4
OI, OT = FIY // 16, FTY // 16
CHUNK = 512
SENDS = 112


def dot_nn(a, b):
    return lax.dot_general(a, b, (((1,), (0,)), ((), ())), preferred_element_type=F32)


def dot_nt(a, b):
    return lax.dot_general(a, b, (((1,), (1,)), ((), ())), preferred_element_type=F32)


def dot_tn(a, b):
    return lax.dot_general(a, b, (((0,), (0,)), ((), ())), preferred_element_type=F32)


def scratch():
    v = pltpu.VMEM
    dma = pltpu.SemaphoreType.DMA
    return dict(
        xi=v((ROWS, FI), BF16),
        xt=v((ROWS, FT), BF16),
        wi=v((FI, EMB), BF16),
        wt=v((FT, EMB), BF16),
        part=v((2, ROWS, EMB), F32),
        a_out=v((2, 2, SHARE, EMB), BF16),
        a_in=v((2, 2, SHARE, EMB), BF16),
        half=v((2, SHARE, EMB), F32),
        b_out=v((2, SHARE, EMB), BF16),
        b_in=v((2, SHARE, EMB), BF16),
        emb=v((2, SHARE, EMB), F32),
        rst=v((2, SHARE, 128), F32),
        iu=v((4, 4, SHARE, EMB), BF16),
        tu=v((2, 8, SHARE, EMB), BF16),
        coef=v((512, 512), BF16),
        c_out=v((8, SHARE, EMB), BF16),
        c_in=v((8, SHARE, EMB), BF16),
        own_t=v((8, SHARE, EMB), F32),
        d_out=v((4, 2, SHARE, EMB), BF16),
        d_in=v((4, 2, SHARE, EMB), BF16),
        e1_out=v((2, 4, 4, SHARE, WIDE), BF16),
        e1_in=v((2, 4, 4, SHARE, WIDE), BF16),
        e2_out=v((2, 4, SHARE, WIDE), BF16),
        e2_in=v((2, 4, SHARE, WIDE), BF16),
        sum_i=v((SHARE, EMB), F32),
        gi=v((2, 4, 2, SHARE, EMB), BF16),
        gt=v((2, 4, 2, SHARE, EMB), BF16),
        ti=v((4, ROWS, FIY), BF16),
        tt=v((4, ROWS, FTY), BF16),
        mi=v((512, FIY), BF16),
        mt=v((512, FTY), BF16),
        ni=v((2, FIY, 256), BF16),
        nt=v((2, FTY, 256), BF16),
        pi=v((FIY, EMB), F32),
        pt=v((FTY, EMB), F32),
        fi_out=v((2, 4, 2, 2 * OI, WIDE), BF16),
        fi_in=v((2, 3, 2, 2 * OI, WIDE), BF16),
        fi_end=v((2, 2, 2 * OI, WIDE), BF16),
        fi_side=v((2, 2 * OI, WIDE), BF16),
        ft_out=v((2, 4, 2, OT, EMB), BF16),
        ft_in=v((2, 3, 2, OT, EMB), BF16),
        ft_end=v((2, 2, OT, EMB), BF16),
        ft_side=v((2, OT, EMB), BF16),
        in_sem=dma((5,)),
        x_sem=dma((2, 4)),
        a_sem=dma((2,)),
        b_sem=dma((2,)),
        iu_sem=dma((2, 2, 4)),
        tu_sem=dma((9,)),
        tc_sem=dma((2,)),
        c_sem=dma,
        d_sem=dma((4, 2)),
        e1_sem=dma((2, 4)),
        e2_sem=dma((2, 4)),
        far_sem=dma((2,)),
        g_sem=dma((2, 2, 4)),
        gc_sem=dma((2, 3)),
        f_sem=dma((2, 2, 3)),
        end_sem=dma((2, 2, 2)),
        h_sem=dma((2,)),
        send_sem=dma((SENDS,)),
    )


NAMES = tuple(scratch())
AROUND = (0, 1, -1, 2, -2, 3, -3, 4)
ABOUT = (0, 1, -1, 2)


def rows_half(h):
    return pl.ds(h * HALF, HALF)


def interleave(order, **tasks):
    for name in order:
        next(tasks[name], None)
    left = list(tasks.values())
    while left:
        left = [task for task in left if next(task, True) is not True]


def kernel(xi_h, xt_h, wi_h, wt_h, heat_ref, shift_ref, cot_ref, og_i, og_t, op_i, op_t, *refs):
    s = dict(zip(NAMES, refs))
    g = lax.axis_index("grp")
    b = lax.axis_index("blk")
    xh, co = lax.div(g, 2), lax.rem(g, 2)
    y, xl, z = lax.div(b, 16), lax.rem(lax.div(b, 8), 2), lax.rem(b, 8)
    x = xh * 2 + xl
    oc, ox = 1 - co, 1 - xh

    def dev(x_, y_, z_, co_):
        return (lax.div(x_, 2) * 2 + co_, (y_ * 2 + lax.rem(x_, 2)) * 8 + z_)

    other_core = dev(x, y, z, oc)
    near = dev(xh * 2 + (1 - xl), y, z, co)
    along_x = {k: dev(lax.rem(x + 4 + k, 4), y, z, co) for k in (1, -1, 2)}
    far = along_x[2]
    along_y = {k: dev(x, lax.rem(y + 4 + k, 4), z, co) for k in (1, -1, 2)}
    along_z = {k: dev(x, y, lax.rem(z + 8 + k, 8), co) for k in (1, -1, 2, -2)}
    corner = {
        (h, k): dev(xh * 2 + h, y, lax.rem(z + 8 + k, 8), co) for h in range(2) for k in (1, -1)
    }
    corners = [dev(xh * 2 + (1 - xl), y, lax.rem(z + 8 + k, 8), co) for k in (1, -1)]

    sends, drained = [], []

    def send(src, dst, sem, to):
        copy = pltpu.make_async_remote_copy(
            src_ref=src,
            dst_ref=dst,
            send_sem=s["send_sem"].at[len(sends)],
            recv_sem=sem,
            device_id=to,
            device_id_type=MESH,
        )
        copy.start()
        sends.append(copy)

    def arrived(dst, sem):
        pltpu.make_async_copy(dst, dst, sem).wait()

    def gather_eight(to, ref, sem, then):
        for way in (2, -2, 1, -1):
            send(ref(0, None), ref(-way, None), sem(-way), to[way])
        yield
        for half, way in enumerate((1, -1)):
            far_ = -2 * way
            arrived(ref(far_, None), sem(far_))
            send(ref(far_, half), ref(4, half), s["tu_sem"].at[7 + half], to[2 * way])
            send(ref(far_, None), ref(-3 * way, None), sem(-3 * way), to[way])
        for k in (1, -1):
            arrived(ref(k, None), sem(k))
        then(0)
        yield
        for k in (3, -3):
            arrived(ref(k, None), sem(k))
        for half in range(2):
            arrived(ref(4, half), s["tu_sem"].at[7 + half])
        then(1)

    def scatter_eight(to, own, out, inn, sem, totals):
        for n, way in enumerate((1, -1)):
            rows = rows_half(n)
            out[3, n, rows] = own(4)[n * HALF : (n + 1) * HALF].astype(BF16)
            send(out.at[3, n, rows], inn.at[3, n, rows], sem.at[3, n], to[2 * way])
        for n, way in enumerate((1, -1)):
            out[2, n] = own(3 * way).astype(BF16)
            send(out.at[2, n], inn.at[2, n], sem.at[2, n], to[way])
        for n, way in enumerate((1, -1)):
            out[0, n] = own(way).astype(BF16)
            send(out.at[0, n], inn.at[0, n], sem.at[0, n], to[way])
        yield
        for n, way in enumerate((1, -1)):
            rows = slice(n * HALF, (n + 1) * HALF)
            rest = slice((1 - n) * HALF, (2 - n) * HALF)
            value = own(2 * way)
            arrived(inn.at[2, n], sem.at[2, n])
            arrived(inn.at[3, n, rows_half(n)], sem.at[3, n])
            more = inn[2, n, rows].astype(F32) + inn[3, n, rows].astype(F32)
            out[1, n, rows] = (value[rows] + more).astype(BF16)
            out[1, n, rest] = (value[rest] + inn[2, n, rest].astype(F32)).astype(BF16)
            send(out.at[1, n], inn.at[1, n], sem.at[1, n], to[2 * way])
        value = own(0)
        yield
        for m in range(2):
            for n in range(2):
                arrived(inn.at[m, n], sem.at[m, n])
                value = value + inn[m, n].astype(F32)
        totals.append(value)

    def gather_four(to, ref, sem):
        for way in (1, -1):
            send(ref(0, None), ref(-way, None), sem.at[0 if way > 0 else 1], to[way])
        yield
        for way in (1, -1):
            n = 0 if way > 0 else 1
            arrived(ref(-way, None), sem.at[n])
            send(ref(-way, n), ref(2, n), sem.at[2 + n], to[way])
        yield
        for n in range(2):
            arrived(ref(2, n), sem.at[2 + n])

    def gather_direct(to, ref, sem):
        for way in (2, 1, -1):
            send(ref(0, None), ref(-way, None), sem.at[-way % 4], to[way])
        yield
        for k in (1, -1, 2):
            arrived(ref(k, None), sem.at[k % 4])

    def scatter_direct(to, src, mine_, inn, sem, totals):
        for way in (2, 1, -1):
            k = -way % 4
            send(src(way % 4), inn.at[k], sem.at[k], to[way])
        yield
        value = mine_()
        for k in (1, -1, 2):
            arrived(inn.at[k % 4], sem.at[k % 4])
            value = value + inn[k % 4].astype(F32)
        totals.append(value)

    def scatter_corner(t, own, name, totals):
        out, inn, end, side = (s[name + part] for part in ("_out", "_in", "_end", "_side"))
        sem, end_sem = s["f_sem"].at[t], s["end_sem"].at[t]
        for step in range(1, 5):
            if step > 1:
                yield
            for d, way in enumerate((1, -1)):
                if step == 1:
                    out[d, 0, d] = own(4 * way, d).astype(BF16)
                    send(out.at[d, 0, d], inn.at[d, 0, d], sem.at[d, 0], along_z[way])
                    continue
                before = inn.at[d, step - 2]
                arrived(before.at[d] if step == 2 else before, sem.at[d, step - 2])
                for half in range(2):
                    value = own(way * (5 - step), half)
                    if step > 2 or half == d:
                        value = value + inn[d, step - 2, half].astype(F32)
                    out[d, step - 1, half] = value.astype(BF16)
                    if step == 4:
                        origin = lax.rem(xl + half, 2)
                        send(out.at[d, 3, half], end.at[origin, d], end_sem.at[origin, d], corner[half, way])
                if step < 4:
                    send(out.at[d, step - 1], inn.at[d, step - 1], sem.at[d, step - 1], along_z[way])
            if step == 1:
                side[0] = own(0, 1 - xl).astype(BF16)
                send(side.at[0], side.at[1], s["h_sem"].at[t], near)
        value = own(0, xl)
        yield
        arrived(side.at[1], s["h_sem"].at[t])
        value = value + side[1].astype(F32)
        for origin in range(2):
            for d in range(2):
                arrived(end.at[origin, d], end_sem.at[origin, d])
                value = value + end[origin, d].astype(F32)
        totals.append(value)

    def load(src, dst, n):
        copy = pltpu.make_async_copy(src, dst, s["in_sem"].at[n])
        copy.start()
        return copy

    def load_rows(src, dst, at, size, n):
        rows = pl.ds(at, size)
        return slice(at, at + size), load(src.at[rows], dst.at[rows], n)

    xi_load = load(xi_h, s["xi"], 0)
    wi_loads = [load_rows(wi_h, s["wi"], 0, FI // 2, 1), load_rows(wi_h, s["wi"], FI // 2, FI // 2, 2)]

    barrier = pltpu.get_barrier_semaphore()
    peers = [other_core, *along_x.values(), *along_y.values(), *along_z.values(), *corners]
    for to in peers:
        pl.semaphore_signal(barrier, inc=1, device_id=to, device_id_type=MESH)

    xt_load = load(xt_h, s["xt"], 3)
    wt_loads = [load_rows(wt_h, s["wt"], 0, FT, 4)]

    def partial(t, x_ref, w_ref, x_load, w_loads):
        x_load.wait()
        for k, (rows, w_load) in enumerate(w_loads):
            w_load.wait()
            part = dot_nn(x_ref[:, rows], w_ref[rows, :])
            s["part"][t] = part if k == 0 else s["part"][t] + part
            yield
        for h in range(2):
            rows = pl.ds(pl.multiple_of((h * 2 + oc) * SHARE, SHARE), SHARE)
            s["a_out"][t, h] = s["part"][t, rows, :].astype(BF16)
        send(s["a_out"].at[t], s["a_in"].at[t], s["a_sem"].at[t], other_core)

    def mine(t, h):
        rows = pl.ds(pl.multiple_of((h * 2 + co) * SHARE, SHARE), SHARE)
        got = s["a_in"][t, pl.ds(h, 1)].reshape(SHARE, EMB)
        return s["part"][t, rows, :] + got.astype(F32)

    def to_far(t):
        arrived(s["a_in"].at[t], s["a_sem"].at[t])
        s["b_out"][t] = mine(t, ox).astype(BF16)
        send(s["b_out"].at[t], s["b_in"].at[t], s["b_sem"].at[t], far)
        s["half"][t] = mine(t, xh)

    def exchange(t, x_ref, t_ref, width):
        for k, to in along_y.items():
            cols = pl.ds(pl.multiple_of(lax.rem(y + 4 + k, 4) * width, 128), width)
            send(x_ref.at[:, cols], t_ref.at[-k % 4], s["x_sem"].at[t, -k % 4], to)
        cols = pl.ds(pl.multiple_of(y * width, 128), width)
        t_ref[0] = x_ref[:, cols]

    image_part = partial(0, s["xi"], s["wi"], xi_load, wi_loads)
    text_part = partial(1, s["xt"], s["wt"], xt_load, wt_loads)
    for _ in wi_loads:
        next(image_part)
    pl.semaphore_wait(barrier, len(peers))
    next(image_part, None)
    for _ in text_part:
        pass
    to_far(0)
    exchange(0, s["xi"], s["ti"], FIY)
    to_far(1)
    exchange(1, s["xt"], s["tt"], FTY)

    def units(t):
        arrived(s["b_in"].at[t], s["b_sem"].at[t])
        e = s["half"][t] + s["b_in"][t].astype(F32)
        rs = lax.rsqrt(jnp.sum(e * e, axis=-1, keepdims=True) + EPS)
        s["emb"][t] = e
        s["rst"][t] = jnp.broadcast_to(rs, (SHARE, 128))
        return (e * rs).astype(BF16)

    def images_ring(w):
        if w == 0:
            s["iu"][0, 0] = units(0)
        cols = pl.ds(w * WIDE, WIDE)

        def one(k, half):
            at = (k % 4, 0) if w == 0 else (0, k % 4)
            return s["iu"].at[at + (pl.ds(0, SHARE), cols)]

        def four(k, half):
            at = (pl.ds(0, 4), k % 4) if w == 0 else (k % 4, pl.ds(0, 4))
            return s["iu"].at[at + (pl.ds(0, SHARE), cols)]

        first, second = (along_x, along_y) if w == 0 else (along_y, along_x)
        yield from gather_direct(first, one, s["iu_sem"].at[w, 0])
        yield from gather_direct(second, four, s["iu_sem"].at[w, 1])

    def texts_ring():
        s["tu"][0, 0] = units(1)

        def ref(k, half):
            rows = pl.ds(0, SHARE) if half is None else rows_half(half)
            return s["tu"].at[0, AROUND.index(k), rows]

        def sem(k):
            return s["tu_sem"].at[AROUND.index(k)]

        def across(part):
            slots = (pl.ds(0, 5), pl.ds(5, 3))[part]
            send(s["tu"].at[0, slots], s["tu"].at[1, slots], s["tc_sem"].at[part], other_core)

        yield from gather_eight(along_z, ref, sem, across)

    def turned(t, t_ref, m_ref, n_ref):
        for k in range(1, 4):
            arrived(t_ref.at[k], s["x_sem"].at[t, k])
        for n, core in enumerate((co, oc)):
            for k, dy in enumerate(ABOUT):
                for h in range(2):
                    at = (n * 8 + k * 2 + h) * SHARE
                    rows = pl.ds(pl.multiple_of((h * 2 + core) * SHARE, SHARE), SHARE)
                    m_ref[at : at + SHARE, :] = t_ref[dy % 4, rows, :]
            n_ref[n] = m_ref[n * 256 : (n + 1) * 256, :].T
            yield

    def towers():
        yield from turned(0, s["ti"], s["mi"], s["ni"])
        yield from turned(1, s["tt"], s["mt"], s["nt"])

    towers_task = towers()
    interleave(
        "tabwabtwatb",
        t=texts_ring(),
        a=images_ring(0),
        b=images_ring(1),
        w=(next(towers_task, None) for _ in range(2)),
    )

    heat, shift = heat_ref[0], shift_ref[0]
    mult = cot_ref[0] * heat / 8192.0

    def texts():
        return s["tu"][...].reshape(512, EMB)

    def images():
        return s["iu"][...].reshape(512, EMB)

    def coefficients(n):
        score = dot_nt(images(), s["tu"][n].reshape(256, EMB))
        value = jax.nn.sigmoid(heat * score + shift)
        s["coef"][:, n * 256 : (n + 1) * 256] = (mult * value).astype(BF16)
        if n == 0:
            row = lax.broadcasted_iota(jnp.int32, (SHARE, 128), 0)
            col = lax.broadcasted_iota(jnp.int32, (SHARE, 128), 1)
            own = value[:SHARE, :128] - (row == col).astype(F32)
            s["coef"][:SHARE, :128] = (mult * own).astype(BF16)

    def text_half(n, out):
        grad = dot_tn(s["coef"][:, n * 256 : (n + 1) * 256], images())
        out[...] = grad.reshape(8, SHARE, EMB).astype(out.dtype)

    coefficients(0)
    arrived(s["tu"].at[1, pl.ds(0, 5)], s["tc_sem"].at[0])
    arrived(s["tu"].at[1, pl.ds(5, 3)], s["tc_sem"].at[1])
    coefficients(1)
    text_half(1, s["c_out"])
    send(s["c_out"], s["c_in"], s["c_sem"], other_core)

    def back(t, grads, grad):
        rs = s["rst"][t][:, :1]
        u = s["emb"][t] * rs
        value = (grad - u * jnp.sum(u * grad, axis=-1, keepdims=True)) * rs
        grads[0, 0, pl.ds(xh, 1)] = value.astype(BF16).reshape(1, SHARE, EMB)

    def text_grad():
        text_half(0, s["own_t"])
        yield
        arrived(s["c_in"], s["c_sem"])

        def own(k):
            at = AROUND.index(k)
            return s["own_t"][at] + s["c_in"][at].astype(F32)

        totals = []
        yield from scatter_eight(along_z, own, s["d_out"], s["d_in"], s["d_sem"], totals)
        back(1, s["gt"], totals[0])

    def image_half(w):
        first, second = (along_y, along_x) if w == 0 else (along_x, along_y)
        out = s["e1_out"].at[w]
        grad = dot_nn(s["coef"][...], texts()[:, w * WIDE : (w + 1) * WIDE])
        out[...] = grad.astype(BF16).reshape(4, 4, SHARE, WIDE)

        def group(k):
            return out.at[:, k] if w == 0 else out.at[k]

        totals = []
        yield from scatter_direct(
            first, group, lambda: group(0)[...].astype(F32), s["e1_in"].at[w], s["e1_sem"].at[w], totals
        )
        line = s["e2_out"].at[w]
        line[...] = totals[0].astype(BF16)
        yield from scatter_direct(
            second, lambda k: line.at[k], lambda: totals[0][0], s["e2_in"].at[w], s["e2_sem"].at[w], totals
        )
        s["sum_i"][:, w * WIDE : (w + 1) * WIDE] = totals[1]

    def spread(t, grads, first_dot):
        def across(slots, h, n):
            send(grads.at[0, slots, h], grads.at[1, slots, h], s["gc_sem"].at[t, n], other_core)

        def ring(h, n):
            def ref(k, half):
                rows = pl.ds(0, SHARE) if half is None else rows_half(half)
                return grads.at[0, ABOUT.index(k if k != -2 else 2), h, rows]

            if n == 0:
                send(ref(0, None), ref(0, None), s["far_sem"].at[t], far)
            else:
                arrived(ref(0, None), s["far_sem"].at[t])
            task = gather_four(along_y, ref, s["g_sem"].at[t, n])
            next(task)
            yield
            next(task)
            if n == 1:
                across(pl.ds(0, 3), h, 1)
            yield
            yield from task
            across(pl.ds(0, 4) if n == 0 else pl.ds(3, 1), h, 2 * n)

        first, second = ring(xh, 0), ring(ox, 1)
        next(first)
        yield
        next(first)
        next(second)
        yield
        next(first, None)
        next(second)
        yield
        next(second, None)
        first_dot()
        yield
        for n, (h, slots) in enumerate(((xh, pl.ds(0, 4)), (ox, pl.ds(0, 3)), (ox, pl.ds(3, 1)))):
            arrived(grads.at[1, slots, h], s["gc_sem"].at[t, n])

    def weights(t, grads, n_ref, p_ref, own, names):
        def term(n):
            return dot_nn(n_ref[n], grads[n].reshape(256, EMB))

        def first_dot():
            p_ref[...] = term(0)

        yield from spread(t, grads, first_dot)
        p_ref[...] = p_ref[...] + term(1)
        totals = []
        ring = scatter_corner(t, own, names, totals)
        yield from ring
        return totals[0]

    def inputs(grads, w_ref, out):
        for k in range(0, w_ref.shape[0], CHUNK):
            cols = slice(k, k + CHUNK)
            value = dot_nt(grads[:, 0].reshape(ROWS, EMB), w_ref[cols, :]).astype(BF16)
            for n, core in enumerate((co, oc)):
                for h in range(2):
                    rows = pl.ds(pl.multiple_of((h * 2 + core) * SHARE, SHARE), SHARE)
                    at = (n * 2 + h) * SHARE
                    out[rows, cols] = value[at : at + SHARE]
            yield

    def drain():
        while True:
            for _ in range(len(sends) - len(drained)):
                drained.append(sends[len(drained)])
                drained[-1].wait_send()
            yield

    def own_i(k, half):
        n = half * 8 + lax.rem(z + 8 + k, 8)
        rows = s["pi"][pl.ds(pl.multiple_of(n * OI, 8), OI), :]
        return jnp.concatenate([rows[:, :WIDE], rows[:, WIDE:]], axis=0)

    def own_t(k, half):
        n = half * 8 + lax.rem(z + 8 + k, 8)
        return s["pt"][pl.ds(pl.multiple_of(n * OT, 8), OT), :]

    def texts_back():
        yield from text_grad()
        op_t[...] = yield from weights(1, s["gt"], s["nt"], s["pt"], own_t, "ft")

    def images_back():
        back(0, s["gi"], s["sum_i"][...])
        total = yield from weights(0, s["gi"], s["ni"], s["pi"], own_i, "fi")
        op_i[:, :WIDE] = total[:OI]
        op_i[:, WIDE:] = total[OI:]

    drains = drain()
    interleave(
        "abttwatbabitwititiittiptiotoiptowxiopxt",
        t=texts_back(),
        a=image_half(0),
        b=image_half(1),
        i=images_back(),
        w=towers_task,
        o=inputs(s["gi"], s["wi"], og_i),
        p=inputs(s["gt"], s["wt"], og_t),
        x=(next(drains) for _ in range(2)),
    )
    next(drains)


def copy_out(*refs):
    copies = [pltpu.make_async_copy(refs[k], refs[4 + k], refs[8].at[k]) for k in range(4)]
    for copy in copies:
        copy.start()
    for copy in copies:
        copy.wait()


def per_device(xi, xt, wi, wt, heat, shift, cot):
    vmem = pl.BlockSpec(memory_space=pltpu.VMEM)
    smem = pl.BlockSpec(memory_space=pltpu.SMEM)
    hbm = pl.BlockSpec(memory_space=pl.ANY)
    shapes = (
        jax.ShapeDtypeStruct((ROWS, FI), BF16),
        jax.ShapeDtypeStruct((ROWS, FT), BF16),
        jax.ShapeDtypeStruct((OI, EMB), F32),
        jax.ShapeDtypeStruct((OT, EMB), F32),
    )
    outs = pl.pallas_call(
        kernel,
        out_shape=shapes,
        in_specs=[hbm] * 4 + [smem] * 3,
        out_specs=[vmem] * 4,
        scratch_shapes=list(scratch().values()),
        compiler_params=pltpu.CompilerParams(
            collective_id=0, has_side_effects=True, vmem_limit_bytes=55_250_000
        ),
    )(xi, xt, wi, wt, heat, shift, cot)
    return pl.pallas_call(
        copy_out,
        out_shape=shapes,
        in_specs=[hbm] * 4,
        out_specs=[hbm] * 4,
        scratch_shapes=[pltpu.SemaphoreType.DMA((4,))],
        compiler_params=pltpu.CompilerParams(vmem_limit_bytes=2 * 1024 * 1024),
    )(*outs)


def solution(mesh):
    placed = (P("blk", "grp"), P("blk", "grp"), P("grp", None), P("grp", None), P(), P(), P())
    return jax.shard_map(
        per_device,
        mesh=mesh,
        in_specs=placed,
        out_specs=(
            P("blk", "grp"),
            P("blk", "grp"),
            P(("grp", "blk"), None),
            P(("grp", "blk"), None),
        ),
        check_vma=False,
    )
```

```python
import functools

import jax
import jax.numpy as jnp
from jax import lax
from jax.experimental import pallas as pl
from jax.experimental.pallas import tpu as pltpu
from jax.sharding import PartitionSpec as P

MESH = pl.DeviceIdType.MESH
F32 = jnp.float32
BF16 = jnp.bfloat16
EPS = 1e-06

ROWS = 128
SHARE = 32
HALF = 16
EMB = 1024
WIDE = 512
FI, FT = 1536, 1024
FIY, FTY = FI // 4, FT // 4
OI, OT = FIY // 16, FTY // 16
CHUNK = 512
SENDS = 112


def dot_nn(a, b):
    return lax.dot_general(a, b, (((1,), (0,)), ((), ())), preferred_element_type=F32)


def dot_nt(a, b):
    return lax.dot_general(a, b, (((1,), (1,)), ((), ())), preferred_element_type=F32)


def dot_tn(a, b):
    return lax.dot_general(a, b, (((0,), (0,)), ((), ())), preferred_element_type=F32)


def scratch():
    v = pltpu.VMEM
    dma = pltpu.SemaphoreType.DMA
    return dict(
        xi=v((ROWS, FI), BF16),
        xt=v((ROWS, FT), BF16),
        wi=v((FI, EMB), BF16),
        wt=v((FT, EMB), BF16),
        part=v((2, ROWS, EMB), F32),
        a_out=v((2, 2, SHARE, EMB), BF16),
        a_in=v((2, 2, SHARE, EMB), BF16),
        half=v((2, SHARE, EMB), F32),
        b_out=v((2, SHARE, EMB), BF16),
        b_in=v((2, SHARE, EMB), BF16),
        emb=v((2, SHARE, EMB), F32),
        rst=v((2, SHARE, 128), F32),
        iu=v((4, 4, SHARE, EMB), BF16),
        tu=v((2, 8, SHARE, EMB), BF16),
        coef=v((512, 512), BF16),
        c_out=v((8, SHARE, EMB), BF16),
        c_in=v((8, SHARE, EMB), BF16),
        own_t=v((8, SHARE, EMB), F32),
        d_out=v((4, 2, SHARE, EMB), BF16),
        d_in=v((4, 2, SHARE, EMB), BF16),
        e1_out=v((2, 4, 4, SHARE, WIDE), BF16),
        e1_in=v((2, 4, 4, SHARE, WIDE), BF16),
        e2_out=v((2, 4, SHARE, WIDE), BF16),
        e2_in=v((2, 4, SHARE, WIDE), BF16),
        sum_i=v((SHARE, EMB), F32),
        gi=v((2, 4, 2, SHARE, EMB), BF16),
        gt=v((2, 4, 2, SHARE, EMB), BF16),
        ti=v((4, ROWS, FIY), BF16),
        tt=v((4, ROWS, FTY), BF16),
        mi=v((512, FIY), BF16),
        mt=v((512, FTY), BF16),
        ni=v((2, FIY, 256), BF16),
        nt=v((2, FTY, 256), BF16),
        pi=v((FIY, EMB), F32),
        pt=v((FTY, EMB), F32),
        fi_out=v((2, 4, 2, 2 * OI, WIDE), BF16),
        fi_in=v((2, 3, 2, 2 * OI, WIDE), BF16),
        fi_end=v((2, 2, 2 * OI, WIDE), BF16),
        fi_side=v((2, 2 * OI, WIDE), BF16),
        ft_out=v((2, 4, 2, OT, EMB), BF16),
        ft_in=v((2, 3, 2, OT, EMB), BF16),
        ft_end=v((2, 2, OT, EMB), BF16),
        ft_side=v((2, OT, EMB), BF16),
        in_sem=dma((5,)),
        x_sem=dma((2, 4)),
        a_sem=dma((2,)),
        b_sem=dma((2,)),
        iu_sem=dma((2, 2, 4)),
        tu_sem=dma((9,)),
        tc_sem=dma((2,)),
        c_sem=dma,
        d_sem=dma((4, 2)),
        e1_sem=dma((2, 4)),
        e2_sem=dma((2, 4)),
        far_sem=dma((2,)),
        g_sem=dma((2, 2, 4)),
        gc_sem=dma((2, 3)),
        f_sem=dma((2, 2, 3)),
        end_sem=dma((2, 2, 2)),
        h_sem=dma((2,)),
        send_sem=dma((SENDS,)),
    )


NAMES = tuple(scratch())
AROUND = (0, 1, -1, 2, -2, 3, -3, 4)
ABOUT = (0, 1, -1, 2)


def rows_half(h):
    return pl.ds(h * HALF, HALF)


def interleave(order, **tasks):
    for name in order:
        next(tasks[name], None)
    left = list(tasks.values())
    while left:
        left = [task for task in left if next(task, True) is not True]


def kernel(xi_h, xt_h, wi_h, wt_h, heat_ref, shift_ref, cot_ref, *refs):
    og_i, og_t, (op_i, op_t), refs = refs[:3], refs[3:5], refs[5:7], refs[7:]
    s = dict(zip(NAMES, refs))
    g = lax.axis_index("grp")
    b = lax.axis_index("blk")
    xh, co = lax.div(g, 2), lax.rem(g, 2)
    y, xl, z = lax.div(b, 16), lax.rem(lax.div(b, 8), 2), lax.rem(b, 8)
    x = xh * 2 + xl
    oc, ox = 1 - co, 1 - xh

    def dev(x_, y_, z_, co_):
        return (lax.div(x_, 2) * 2 + co_, (y_ * 2 + lax.rem(x_, 2)) * 8 + z_)

    other_core = dev(x, y, z, oc)
    near = dev(xh * 2 + (1 - xl), y, z, co)
    along_x = {k: dev(lax.rem(x + 4 + k, 4), y, z, co) for k in (1, -1, 2)}
    far = along_x[2]
    along_y = {k: dev(x, lax.rem(y + 4 + k, 4), z, co) for k in (1, -1, 2)}
    along_z = {k: dev(x, y, lax.rem(z + 8 + k, 8), co) for k in (1, -1, 2, -2)}
    corner = {
        (h, k): dev(xh * 2 + h, y, lax.rem(z + 8 + k, 8), co) for h in range(2) for k in (1, -1)
    }
    corners = [dev(xh * 2 + (1 - xl), y, lax.rem(z + 8 + k, 8), co) for k in (1, -1)]

    sends, drained = [], []

    def send(src, dst, sem, to):
        copy = pltpu.make_async_remote_copy(
            src_ref=src,
            dst_ref=dst,
            send_sem=s["send_sem"].at[len(sends)],
            recv_sem=sem,
            device_id=to,
            device_id_type=MESH,
        )
        copy.start()
        sends.append(copy)

    def arrived(dst, sem):
        pltpu.make_async_copy(dst, dst, sem).wait()

    def gather_eight(to, ref, sem, then):
        for way in (2, -2, 1, -1):
            send(ref(0, None), ref(-way, None), sem(-way), to[way])
        yield
        for half, way in enumerate((1, -1)):
            far_ = -2 * way
            arrived(ref(far_, None), sem(far_))
            send(ref(far_, half), ref(4, half), s["tu_sem"].at[7 + half], to[2 * way])
            send(ref(far_, None), ref(-3 * way, None), sem(-3 * way), to[way])
        for k in (1, -1):
            arrived(ref(k, None), sem(k))
        then(0)
        yield
        for k in (3, -3):
            arrived(ref(k, None), sem(k))
        for half in range(2):
            arrived(ref(4, half), s["tu_sem"].at[7 + half])
        then(1)

    def scatter_eight(to, own, out, inn, sem, totals):
        for n, way in enumerate((1, -1)):
            rows = rows_half(n)
            out[3, n, rows] = own(4)[n * HALF : (n + 1) * HALF].astype(BF16)
            send(out.at[3, n, rows], inn.at[3, n, rows], sem.at[3, n], to[2 * way])
        for n, way in enumerate((1, -1)):
            out[2, n] = own(3 * way).astype(BF16)
            send(out.at[2, n], inn.at[2, n], sem.at[2, n], to[way])
        for n, way in enumerate((1, -1)):
            out[0, n] = own(way).astype(BF16)
            send(out.at[0, n], inn.at[0, n], sem.at[0, n], to[way])
        yield
        for n, way in enumerate((1, -1)):
            rows = slice(n * HALF, (n + 1) * HALF)
            rest = slice((1 - n) * HALF, (2 - n) * HALF)
            value = own(2 * way)
            arrived(inn.at[2, n], sem.at[2, n])
            arrived(inn.at[3, n, rows_half(n)], sem.at[3, n])
            more = inn[2, n, rows].astype(F32) + inn[3, n, rows].astype(F32)
            out[1, n, rows] = (value[rows] + more).astype(BF16)
            out[1, n, rest] = (value[rest] + inn[2, n, rest].astype(F32)).astype(BF16)
            send(out.at[1, n], inn.at[1, n], sem.at[1, n], to[2 * way])
        value = own(0)
        yield
        for m in range(2):
            for n in range(2):
                arrived(inn.at[m, n], sem.at[m, n])
                value = value + inn[m, n].astype(F32)
        totals.append(value)

    def gather_four(to, ref, sem):
        for way in (1, -1):
            send(ref(0, None), ref(-way, None), sem.at[0 if way > 0 else 1], to[way])
        yield
        for way in (1, -1):
            n = 0 if way > 0 else 1
            arrived(ref(-way, None), sem.at[n])
            send(ref(-way, n), ref(2, n), sem.at[2 + n], to[way])
        yield
        for n in range(2):
            arrived(ref(2, n), sem.at[2 + n])

    def gather_direct(to, ref, sem):
        for way in (2, 1, -1):
            send(ref(0, None), ref(-way, None), sem.at[-way % 4], to[way])
        yield
        for k in (1, -1, 2):
            arrived(ref(k, None), sem.at[k % 4])

    def scatter_direct(to, src, mine_, inn, sem, totals):
        for way in (2, 1, -1):
            k = -way % 4
            send(src(way % 4), inn.at[k], sem.at[k], to[way])
        yield
        value = mine_()
        for k in (1, -1, 2):
            arrived(inn.at[k % 4], sem.at[k % 4])
            value = value + inn[k % 4].astype(F32)
        totals.append(value)

    def scatter_corner(t, own, name, totals):
        out, inn, end, side = (s[name + part] for part in ("_out", "_in", "_end", "_side"))
        sem, end_sem = s["f_sem"].at[t], s["end_sem"].at[t]
        for step in range(1, 5):
            if step > 1:
                yield
            for d, way in enumerate((1, -1)):
                if step == 1:
                    out[d, 0, d] = own(4 * way, d).astype(BF16)
                    send(out.at[d, 0, d], inn.at[d, 0, d], sem.at[d, 0], along_z[way])
                    continue
                before = inn.at[d, step - 2]
                arrived(before.at[d] if step == 2 else before, sem.at[d, step - 2])
                for half in range(2):
                    value = own(way * (5 - step), half)
                    if step > 2 or half == d:
                        value = value + inn[d, step - 2, half].astype(F32)
                    out[d, step - 1, half] = value.astype(BF16)
                    if step == 4:
                        origin = lax.rem(xl + half, 2)
                        send(out.at[d, 3, half], end.at[origin, d], end_sem.at[origin, d], corner[half, way])
                if step < 4:
                    send(out.at[d, step - 1], inn.at[d, step - 1], sem.at[d, step - 1], along_z[way])
            if step == 1:
                side[0] = own(0, 1 - xl).astype(BF16)
                send(side.at[0], side.at[1], s["h_sem"].at[t], near)
        value = own(0, xl)
        yield
        arrived(side.at[1], s["h_sem"].at[t])
        value = value + side[1].astype(F32)
        for origin in range(2):
            for d in range(2):
                arrived(end.at[origin, d], end_sem.at[origin, d])
                value = value + end[origin, d].astype(F32)
        totals.append(value)

    def load(src, dst, n):
        copy = pltpu.make_async_copy(src, dst, s["in_sem"].at[n])
        copy.start()
        return copy

    def load_rows(src, dst, at, size, n):
        rows = pl.ds(at, size)
        return slice(at, at + size), load(src.at[rows], dst.at[rows], n)

    xi_load = load(xi_h, s["xi"], 0)
    wi_loads = [load_rows(wi_h, s["wi"], 0, FI // 2, 1), load_rows(wi_h, s["wi"], FI // 2, FI // 2, 2)]

    barrier = pltpu.get_barrier_semaphore()
    peers = [other_core, *along_x.values(), *along_y.values(), *along_z.values(), *corners]
    for to in peers:
        pl.semaphore_signal(barrier, inc=1, device_id=to, device_id_type=MESH)

    xt_load = load(xt_h, s["xt"], 3)
    wt_loads = [load_rows(wt_h, s["wt"], 0, FT, 4)]

    def partial(t, x_ref, w_ref, x_load, w_loads):
        x_load.wait()
        for k, (rows, w_load) in enumerate(w_loads):
            w_load.wait()
            part = dot_nn(x_ref[:, rows], w_ref[rows, :])
            s["part"][t] = part if k == 0 else s["part"][t] + part
            yield
        for h in range(2):
            rows = pl.ds(pl.multiple_of((h * 2 + oc) * SHARE, SHARE), SHARE)
            s["a_out"][t, h] = s["part"][t, rows, :].astype(BF16)
        send(s["a_out"].at[t], s["a_in"].at[t], s["a_sem"].at[t], other_core)

    def mine(t, h):
        rows = pl.ds(pl.multiple_of((h * 2 + co) * SHARE, SHARE), SHARE)
        got = s["a_in"][t, pl.ds(h, 1)].reshape(SHARE, EMB)
        return s["part"][t, rows, :] + got.astype(F32)

    def to_far(t):
        arrived(s["a_in"].at[t], s["a_sem"].at[t])
        s["b_out"][t] = mine(t, ox).astype(BF16)
        send(s["b_out"].at[t], s["b_in"].at[t], s["b_sem"].at[t], far)
        s["half"][t] = mine(t, xh)

    def exchange(t, x_ref, t_ref, width):
        for k, to in along_y.items():
            cols = pl.ds(pl.multiple_of(lax.rem(y + 4 + k, 4) * width, 128), width)
            send(x_ref.at[:, cols], t_ref.at[-k % 4], s["x_sem"].at[t, -k % 4], to)
        cols = pl.ds(pl.multiple_of(y * width, 128), width)
        t_ref[0] = x_ref[:, cols]

    image_part = partial(0, s["xi"], s["wi"], xi_load, wi_loads)
    text_part = partial(1, s["xt"], s["wt"], xt_load, wt_loads)
    for _ in wi_loads:
        next(image_part)
    pl.semaphore_wait(barrier, len(peers))
    next(image_part, None)
    for _ in text_part:
        pass
    to_far(0)
    exchange(0, s["xi"], s["ti"], FIY)
    to_far(1)
    exchange(1, s["xt"], s["tt"], FTY)

    def units(t):
        arrived(s["b_in"].at[t], s["b_sem"].at[t])
        e = s["half"][t] + s["b_in"][t].astype(F32)
        rs = lax.rsqrt(jnp.sum(e * e, axis=-1, keepdims=True) + EPS)
        s["emb"][t] = e
        s["rst"][t] = jnp.broadcast_to(rs, (SHARE, 128))
        return (e * rs).astype(BF16)

    def images_ring(w):
        if w == 0:
            s["iu"][0, 0] = units(0)
        cols = pl.ds(w * WIDE, WIDE)

        def one(k, half):
            at = (k % 4, 0) if w == 0 else (0, k % 4)
            return s["iu"].at[at + (pl.ds(0, SHARE), cols)]

        def four(k, half):
            at = (pl.ds(0, 4), k % 4) if w == 0 else (k % 4, pl.ds(0, 4))
            return s["iu"].at[at + (pl.ds(0, SHARE), cols)]

        first, second = (along_x, along_y) if w == 0 else (along_y, along_x)
        yield from gather_direct(first, one, s["iu_sem"].at[w, 0])
        yield from gather_direct(second, four, s["iu_sem"].at[w, 1])

    def texts_ring():
        s["tu"][0, 0] = units(1)

        def ref(k, half):
            rows = pl.ds(0, SHARE) if half is None else rows_half(half)
            return s["tu"].at[0, AROUND.index(k), rows]

        def sem(k):
            return s["tu_sem"].at[AROUND.index(k)]

        def across(part):
            slots = (pl.ds(0, 5), pl.ds(5, 3))[part]
            send(s["tu"].at[0, slots], s["tu"].at[1, slots], s["tc_sem"].at[part], other_core)

        yield from gather_eight(along_z, ref, sem, across)

    def turned(t, t_ref, m_ref, n_ref):
        for k in range(1, 4):
            arrived(t_ref.at[k], s["x_sem"].at[t, k])
        for n, core in enumerate((co, oc)):
            for k, dy in enumerate(ABOUT):
                for h in range(2):
                    at = (n * 8 + k * 2 + h) * SHARE
                    rows = pl.ds(pl.multiple_of((h * 2 + core) * SHARE, SHARE), SHARE)
                    m_ref[at : at + SHARE, :] = t_ref[dy % 4, rows, :]
            n_ref[n] = m_ref[n * 256 : (n + 1) * 256, :].T
            yield

    def towers():
        yield from turned(0, s["ti"], s["mi"], s["ni"])
        yield from turned(1, s["tt"], s["mt"], s["nt"])

    towers_task = towers()
    interleave(
        "tabwabtwatb",
        t=texts_ring(),
        a=images_ring(0),
        b=images_ring(1),
        w=(next(towers_task, None) for _ in range(2)),
    )

    heat, shift = heat_ref[0], shift_ref[0]
    mult = cot_ref[0] * heat / 8192.0

    def texts():
        return s["tu"][...].reshape(512, EMB)

    def images():
        return s["iu"][...].reshape(512, EMB)

    def coefficients(n):
        score = dot_nt(images(), s["tu"][n].reshape(256, EMB))
        value = jax.nn.sigmoid(heat * score + shift)
        s["coef"][:, n * 256 : (n + 1) * 256] = (mult * value).astype(BF16)
        if n == 0:
            row = lax.broadcasted_iota(jnp.int32, (SHARE, 128), 0)
            col = lax.broadcasted_iota(jnp.int32, (SHARE, 128), 1)
            own = value[:SHARE, :128] - (row == col).astype(F32)
            s["coef"][:SHARE, :128] = (mult * own).astype(BF16)

    def text_half(n, out):
        grad = dot_tn(s["coef"][:, n * 256 : (n + 1) * 256], images())
        out[...] = grad.reshape(8, SHARE, EMB).astype(out.dtype)

    coefficients(0)
    arrived(s["tu"].at[1, pl.ds(0, 5)], s["tc_sem"].at[0])
    arrived(s["tu"].at[1, pl.ds(5, 3)], s["tc_sem"].at[1])
    coefficients(1)
    text_half(1, s["c_out"])
    send(s["c_out"], s["c_in"], s["c_sem"], other_core)

    def back(t, grads, grad):
        rs = s["rst"][t][:, :1]
        u = s["emb"][t] * rs
        value = (grad - u * jnp.sum(u * grad, axis=-1, keepdims=True)) * rs
        grads[0, 0, pl.ds(xh, 1)] = value.astype(BF16).reshape(1, SHARE, EMB)

    def text_grad():
        text_half(0, s["own_t"])
        yield
        arrived(s["c_in"], s["c_sem"])

        def own(k):
            at = AROUND.index(k)
            return s["own_t"][at] + s["c_in"][at].astype(F32)

        totals = []
        yield from scatter_eight(along_z, own, s["d_out"], s["d_in"], s["d_sem"], totals)
        back(1, s["gt"], totals[0])

    def image_half(w):
        first, second = (along_y, along_x) if w == 0 else (along_x, along_y)
        out = s["e1_out"].at[w]
        grad = dot_nn(s["coef"][...], texts()[:, w * WIDE : (w + 1) * WIDE])
        out[...] = grad.astype(BF16).reshape(4, 4, SHARE, WIDE)

        def group(k):
            return out.at[:, k] if w == 0 else out.at[k]

        totals = []
        yield from scatter_direct(
            first, group, lambda: group(0)[...].astype(F32), s["e1_in"].at[w], s["e1_sem"].at[w], totals
        )
        line = s["e2_out"].at[w]
        line[...] = totals[0].astype(BF16)
        yield from scatter_direct(
            second, lambda k: line.at[k], lambda: totals[0][0], s["e2_in"].at[w], s["e2_sem"].at[w], totals
        )
        s["sum_i"][:, w * WIDE : (w + 1) * WIDE] = totals[1]

    def spread(t, grads, first_dot):
        def across(slots, h, n):
            send(grads.at[0, slots, h], grads.at[1, slots, h], s["gc_sem"].at[t, n], other_core)

        def ring(h, n):
            def ref(k, half):
                rows = pl.ds(0, SHARE) if half is None else rows_half(half)
                return grads.at[0, ABOUT.index(k if k != -2 else 2), h, rows]

            if n == 0:
                send(ref(0, None), ref(0, None), s["far_sem"].at[t], far)
            else:
                arrived(ref(0, None), s["far_sem"].at[t])
            task = gather_four(along_y, ref, s["g_sem"].at[t, n])
            next(task)
            yield
            next(task)
            if n == 1:
                across(pl.ds(0, 3), h, 1)
            yield
            yield from task
            across(pl.ds(0, 4) if n == 0 else pl.ds(3, 1), h, 2 * n)

        first, second = ring(xh, 0), ring(ox, 1)
        next(first)
        yield
        next(first)
        next(second)
        yield
        next(first, None)
        next(second)
        yield
        next(second, None)
        first_dot()
        yield
        for n, (h, slots) in enumerate(((xh, pl.ds(0, 4)), (ox, pl.ds(0, 3)), (ox, pl.ds(3, 1)))):
            arrived(grads.at[1, slots, h], s["gc_sem"].at[t, n])

    def weights(t, grads, n_ref, p_ref, own, names):
        def term(n):
            return dot_nn(n_ref[n], grads[n].reshape(256, EMB))

        def first_dot():
            p_ref[...] = term(0)

        yield from spread(t, grads, first_dot)
        p_ref[...] = p_ref[...] + term(1)
        totals = []
        ring = scatter_corner(t, own, names, totals)
        yield from ring
        return totals[0]

    def inputs(grads, w_ref, out):
        for k in range(0, w_ref.shape[0], CHUNK):
            cols = slice(k, k + CHUNK)
            value = dot_nt(grads[:, 0].reshape(ROWS, EMB), w_ref[cols, :]).astype(BF16)
            for n, core in enumerate((co, oc)):
                for h in range(2):
                    rows = pl.ds(pl.multiple_of((h * 2 + core) * SHARE, SHARE), SHARE)
                    at = (n * 2 + h) * SHARE
                    out[k // CHUNK][rows, :] = value[at : at + SHARE]
            yield

    def drain():
        while True:
            for _ in range(len(sends) - len(drained)):
                drained.append(sends[len(drained)])
                drained[-1].wait_send()
            yield

    def own_i(k, half):
        n = half * 8 + lax.rem(z + 8 + k, 8)
        rows = s["pi"][pl.ds(pl.multiple_of(n * OI, 8), OI), :]
        return jnp.concatenate([rows[:, :WIDE], rows[:, WIDE:]], axis=0)

    def own_t(k, half):
        n = half * 8 + lax.rem(z + 8 + k, 8)
        return s["pt"][pl.ds(pl.multiple_of(n * OT, 8), OT), :]

    def texts_back():
        yield from text_grad()
        op_t[...] = yield from weights(1, s["gt"], s["nt"], s["pt"], own_t, "ft")

    def images_back():
        back(0, s["gi"], s["sum_i"][...])
        total = yield from weights(0, s["gi"], s["ni"], s["pi"], own_i, "fi")
        op_i[:, :WIDE] = total[:OI]
        op_i[:, WIDE:] = total[OI:]

    drains = drain()
    interleave(
        "abttwatbabitwititiittiptiotoiptowxiopxt",
        t=texts_back(),
        a=image_half(0),
        b=image_half(1),
        i=images_back(),
        w=towers_task,
        o=inputs(s["gi"], s["wi"], og_i),
        p=inputs(s["gt"], s["wt"], og_t),
        x=(next(drains) for _ in range(2)),
    )
    next(drains)


def copy_out(*refs):
    blocks, outs, sem = refs[:7], refs[7:11], refs[11]
    places = [outs[0].at[:, pl.ds(k, CHUNK)] for k in range(0, FI, CHUNK)]
    places += [outs[1].at[:, pl.ds(k, CHUNK)] for k in range(0, FT, CHUNK)]
    places += outs[2:]
    copies = [pltpu.make_async_copy(blocks[k], places[k], sem.at[k]) for k in range(7)]
    for copy in copies:
        copy.start()
    for copy in copies:
        copy.wait()


def per_device(xi, xt, wi, wt, heat, shift, cot):
    vmem = pl.BlockSpec(memory_space=pltpu.VMEM)
    smem = pl.BlockSpec(memory_space=pltpu.SMEM)
    hbm = pl.BlockSpec(memory_space=pl.ANY)
    shapes = (
        jax.ShapeDtypeStruct((ROWS, FI), BF16),
        jax.ShapeDtypeStruct((ROWS, FT), BF16),
        jax.ShapeDtypeStruct((OI, EMB), F32),
        jax.ShapeDtypeStruct((OT, EMB), F32),
    )
    outs = pl.pallas_call(
        kernel,
        out_shape=(jax.ShapeDtypeStruct((ROWS, CHUNK), BF16),) * 5 + shapes[2:],
        in_specs=[hbm] * 4 + [smem] * 3,
        out_specs=[vmem] * 7,
        scratch_shapes=list(scratch().values()),
        compiler_params=pltpu.CompilerParams(
            collective_id=0, has_side_effects=True, vmem_limit_bytes=55_600_000
        ),
    )(xi, xt, wi, wt, heat, shift, cot)
    return pl.pallas_call(
        copy_out,
        out_shape=shapes,
        in_specs=[hbm] * 7,
        out_specs=[hbm] * 4,
        scratch_shapes=[pltpu.SemaphoreType.DMA((7,))],
        compiler_params=pltpu.CompilerParams(vmem_limit_bytes=2 * 1024 * 1024),
    )(*outs)


def solution(mesh):
    placed = (P("blk", "grp"), P("blk", "grp"), P("grp", None), P("grp", None), P(), P(), P())
    return jax.shard_map(
        per_device,
        mesh=mesh,
        in_specs=placed,
        out_specs=(
            P("blk", "grp"),
            P("blk", "grp"),
            P(("grp", "blk"), None),
            P(("grp", "blk"), None),
        ),
        check_vma=False,
    )
```

```python
import functools

import jax
import jax.numpy as jnp
from jax import lax
from jax.experimental import pallas as pl
from jax.experimental.pallas import tpu as pltpu
from jax.sharding import PartitionSpec as P

MESH = pl.DeviceIdType.MESH
F32 = jnp.float32
BF16 = jnp.bfloat16
EPS = 1e-06

ROWS = 128
SHARE = 32
HALF = 16
EMB = 1024
WIDE = 512
FI, FT = 1536, 1024
FIY, FTY = FI // 4, FT // 4
OI, OT = FIY // 16, FTY // 16
CHUNK = 512
SENDS = 112


def dot_nn(a, b):
    return lax.dot_general(a, b, (((1,), (0,)), ((), ())), preferred_element_type=F32)


def dot_nt(a, b):
    return lax.dot_general(a, b, (((1,), (1,)), ((), ())), preferred_element_type=F32)


def dot_tn(a, b):
    return lax.dot_general(a, b, (((0,), (0,)), ((), ())), preferred_element_type=F32)


def scratch():
    v = pltpu.VMEM
    dma = pltpu.SemaphoreType.DMA
    return dict(
        xi=v((ROWS, FI), BF16),
        xt=v((ROWS, FT), BF16),
        wi=v((FI, EMB), BF16),
        wt=v((FT, EMB), BF16),
        part=v((2, ROWS, EMB), F32),
        a_out=v((2, 2, SHARE, EMB), BF16),
        a_in=v((2, 2, SHARE, EMB), BF16),
        half=v((2, SHARE, EMB), F32),
        b_out=v((2, SHARE, EMB), BF16),
        b_in=v((2, SHARE, EMB), BF16),
        emb=v((2, SHARE, EMB), F32),
        rst=v((2, SHARE, 128), F32),
        iu=v((4, 4, SHARE, EMB), BF16),
        tu=v((2, 8, SHARE, EMB), BF16),
        coef=v((512, 512), BF16),
        c_out=v((8, SHARE, EMB), BF16),
        c_in=v((8, SHARE, EMB), BF16),
        own_t=v((8, SHARE, EMB), F32),
        d_out=v((4, 2, SHARE, EMB), BF16),
        d_in=v((4, 2, SHARE, EMB), BF16),
        e1_out=v((2, 4, 4, SHARE, WIDE), BF16),
        e1_in=v((2, 4, 4, SHARE, WIDE), BF16),
        e2_out=v((2, 4, SHARE, WIDE), BF16),
        e2_in=v((2, 4, SHARE, WIDE), BF16),
        sum_i=v((SHARE, EMB), F32),
        gi=v((2, 4, 2, SHARE, EMB), BF16),
        gt=v((2, 4, 2, SHARE, EMB), BF16),
        ti=v((4, ROWS, FIY), BF16),
        tt=v((4, ROWS, FTY), BF16),
        mi=v((512, FIY), BF16),
        mt=v((512, FTY), BF16),
        ni=v((2, FIY, 256), BF16),
        nt=v((2, FTY, 256), BF16),
        pi=v((FIY, EMB), F32),
        pt=v((FTY, EMB), F32),
        fi_out=v((2, 4, 2, 2 * OI, WIDE), BF16),
        fi_in=v((2, 3, 2, 2 * OI, WIDE), BF16),
        fi_end=v((2, 2, 2 * OI, WIDE), BF16),
        fi_side=v((2, 2 * OI, WIDE), BF16),
        ft_out=v((2, 4, 2, OT, EMB), BF16),
        ft_in=v((2, 3, 2, OT, EMB), BF16),
        ft_end=v((2, 2, OT, EMB), BF16),
        ft_side=v((2, OT, EMB), BF16),
        in_sem=dma((5,)),
        x_sem=dma((2, 4)),
        a_sem=dma((2,)),
        b_sem=dma((2,)),
        iu_sem=dma((2, 2, 4)),
        tu_sem=dma((9,)),
        tc_sem=dma((2,)),
        c_sem=dma,
        d_sem=dma((4, 2)),
        e1_sem=dma((2, 4)),
        e2_sem=dma((2, 4)),
        far_sem=dma((2,)),
        g_sem=dma((2, 2, 4)),
        gc_sem=dma((2, 3)),
        f_sem=dma((2, 2, 3)),
        end_sem=dma((2, 2, 2)),
        h_sem=dma((2,)),
        send_sem=dma((SENDS,)),
    )


NAMES = tuple(scratch())
AROUND = (0, 1, -1, 2, -2, 3, -3, 4)
ABOUT = (0, 1, -1, 2)


def rows_half(h):
    return pl.ds(h * HALF, HALF)


def interleave(order, **tasks):
    for name in order:
        next(tasks[name], None)
    left = list(tasks.values())
    while left:
        left = [task for task in left if next(task, True) is not True]


def kernel(xi_h, xt_h, wi_h, wt_h, heat_ref, shift_ref, cot_ref, *refs):
    og_i, og_t, (op_i, op_t), refs = refs[:3], refs[3:5], refs[5:7], refs[7:]
    s = dict(zip(NAMES, refs))
    g = lax.axis_index("grp")
    b = lax.axis_index("blk")
    xh, co = lax.div(g, 2), lax.rem(g, 2)
    y, xl, z = lax.div(b, 16), lax.rem(lax.div(b, 8), 2), lax.rem(b, 8)
    x = xh * 2 + xl
    oc, ox = 1 - co, 1 - xh

    def dev(x_, y_, z_, co_):
        return (lax.div(x_, 2) * 2 + co_, (y_ * 2 + lax.rem(x_, 2)) * 8 + z_)

    other_core = dev(x, y, z, oc)
    near = dev(xh * 2 + (1 - xl), y, z, co)
    along_x = {k: dev(lax.rem(x + 4 + k, 4), y, z, co) for k in (1, -1, 2)}
    far = along_x[2]
    along_y = {k: dev(x, lax.rem(y + 4 + k, 4), z, co) for k in (1, -1, 2)}
    along_z = {k: dev(x, y, lax.rem(z + 8 + k, 8), co) for k in (1, -1, 2, -2)}
    corner = {
        (h, k): dev(xh * 2 + h, y, lax.rem(z + 8 + k, 8), co) for h in range(2) for k in (1, -1)
    }
    corners = [dev(xh * 2 + (1 - xl), y, lax.rem(z + 8 + k, 8), co) for k in (1, -1)]

    sends, drained = [], []

    def send(src, dst, sem, to):
        copy = pltpu.make_async_remote_copy(
            src_ref=src,
            dst_ref=dst,
            send_sem=s["send_sem"].at[len(sends)],
            recv_sem=sem,
            device_id=to,
            device_id_type=MESH,
        )
        copy.start()
        sends.append(copy)

    def arrived(dst, sem):
        pltpu.make_async_copy(dst, dst, sem).wait()

    def gather_eight(to, ref, sem, then):
        for way in (2, -2, 1, -1):
            send(ref(0, None), ref(-way, None), sem(-way), to[way])
        yield
        for half, way in enumerate((1, -1)):
            far_ = -2 * way
            arrived(ref(far_, None), sem(far_))
            send(ref(far_, half), ref(4, half), s["tu_sem"].at[7 + half], to[2 * way])
            send(ref(far_, None), ref(-3 * way, None), sem(-3 * way), to[way])
        for k in (1, -1):
            arrived(ref(k, None), sem(k))
        then(0)
        yield
        for k in (3, -3):
            arrived(ref(k, None), sem(k))
        for half in range(2):
            arrived(ref(4, half), s["tu_sem"].at[7 + half])
        then(1)

    def scatter_eight(to, own, out, inn, sem, totals):
        for n, way in enumerate((1, -1)):
            rows = rows_half(n)
            out[3, n, rows] = own(4)[n * HALF : (n + 1) * HALF].astype(BF16)
            send(out.at[3, n, rows], inn.at[3, n, rows], sem.at[3, n], to[2 * way])
        for n, way in enumerate((1, -1)):
            out[2, n] = own(3 * way).astype(BF16)
            send(out.at[2, n], inn.at[2, n], sem.at[2, n], to[way])
        for n, way in enumerate((1, -1)):
            out[0, n] = own(way).astype(BF16)
            send(out.at[0, n], inn.at[0, n], sem.at[0, n], to[way])
        yield
        for n, way in enumerate((1, -1)):
            rows = slice(n * HALF, (n + 1) * HALF)
            rest = slice((1 - n) * HALF, (2 - n) * HALF)
            value = own(2 * way)
            arrived(inn.at[2, n], sem.at[2, n])
            arrived(inn.at[3, n, rows_half(n)], sem.at[3, n])
            more = inn[2, n, rows].astype(F32) + inn[3, n, rows].astype(F32)
            out[1, n, rows] = (value[rows] + more).astype(BF16)
            out[1, n, rest] = (value[rest] + inn[2, n, rest].astype(F32)).astype(BF16)
            send(out.at[1, n], inn.at[1, n], sem.at[1, n], to[2 * way])
        value = own(0)
        yield
        for m in range(2):
            for n in range(2):
                arrived(inn.at[m, n], sem.at[m, n])
                value = value + inn[m, n].astype(F32)
        totals.append(value)

    def gather_four(to, ref, sem):
        for way in (1, -1):
            send(ref(0, None), ref(-way, None), sem.at[0 if way > 0 else 1], to[way])
        yield
        for way in (1, -1):
            n = 0 if way > 0 else 1
            arrived(ref(-way, None), sem.at[n])
            send(ref(-way, n), ref(2, n), sem.at[2 + n], to[way])
        yield
        for n in range(2):
            arrived(ref(2, n), sem.at[2 + n])

    def gather_direct(to, ref, sem):
        for way in (2, 1, -1):
            send(ref(0, None), ref(-way, None), sem.at[-way % 4], to[way])
        yield
        for k in (1, -1, 2):
            arrived(ref(k, None), sem.at[k % 4])

    def scatter_direct(to, src, mine_, inn, sem, totals):
        for way in (2, 1, -1):
            k = -way % 4
            send(src(way % 4), inn.at[k], sem.at[k], to[way])
        yield
        value = mine_()
        for k in (1, -1, 2):
            arrived(inn.at[k % 4], sem.at[k % 4])
            value = value + inn[k % 4].astype(F32)
        totals.append(value)

    def scatter_corner(t, own, name, totals):
        out, inn, end, side = (s[name + part] for part in ("_out", "_in", "_end", "_side"))
        sem, end_sem = s["f_sem"].at[t], s["end_sem"].at[t]
        for step in range(1, 5):
            if step > 1:
                yield
            for d, way in enumerate((1, -1)):
                if step == 1:
                    out[d, 0, d] = own(4 * way, d).astype(BF16)
                    send(out.at[d, 0, d], inn.at[d, 0, d], sem.at[d, 0], along_z[way])
                    continue
                before = inn.at[d, step - 2]
                arrived(before.at[d] if step == 2 else before, sem.at[d, step - 2])
                for half in range(2):
                    value = own(way * (5 - step), half)
                    if step > 2 or half == d:
                        value = value + inn[d, step - 2, half].astype(F32)
                    out[d, step - 1, half] = value.astype(BF16)
                    if step == 4:
                        origin = lax.rem(xl + half, 2)
                        send(out.at[d, 3, half], end.at[origin, d], end_sem.at[origin, d], corner[half, way])
                if step < 4:
                    send(out.at[d, step - 1], inn.at[d, step - 1], sem.at[d, step - 1], along_z[way])
            if step == 1:
                side[0] = own(0, 1 - xl).astype(BF16)
                send(side.at[0], side.at[1], s["h_sem"].at[t], near)
        value = own(0, xl)
        yield
        arrived(side.at[1], s["h_sem"].at[t])
        value = value + side[1].astype(F32)
        for origin in range(2):
            for d in range(2):
                arrived(end.at[origin, d], end_sem.at[origin, d])
                value = value + end[origin, d].astype(F32)
        totals.append(value)

    def load(src, dst, n):
        copy = pltpu.make_async_copy(src, dst, s["in_sem"].at[n])
        copy.start()
        return copy

    def load_rows(src, dst, at, size, n):
        rows = pl.ds(at, size)
        return slice(at, at + size), load(src.at[rows], dst.at[rows], n)

    xi_load = load(xi_h, s["xi"], 0)
    wi_loads = [load_rows(wi_h, s["wi"], 0, FI // 2, 1), load_rows(wi_h, s["wi"], FI // 2, FI // 2, 2)]

    barrier = pltpu.get_barrier_semaphore()
    peers = [other_core, *along_x.values(), *along_y.values(), *along_z.values(), *corners]
    for to in peers:
        pl.semaphore_signal(barrier, inc=1, device_id=to, device_id_type=MESH)

    xt_load = load(xt_h, s["xt"], 3)
    wt_loads = [load_rows(wt_h, s["wt"], 0, FT, 4)]

    def partial(t, x_ref, w_ref, x_load, w_loads):
        x_load.wait()
        for k, (rows, w_load) in enumerate(w_loads):
            w_load.wait()
            part = dot_nn(x_ref[:, rows], w_ref[rows, :])
            s["part"][t] = part if k == 0 else s["part"][t] + part
            yield
        for h in range(2):
            rows = pl.ds(pl.multiple_of((h * 2 + oc) * SHARE, SHARE), SHARE)
            s["a_out"][t, h] = s["part"][t, rows, :].astype(BF16)
        send(s["a_out"].at[t], s["a_in"].at[t], s["a_sem"].at[t], other_core)

    def mine(t, h):
        rows = pl.ds(pl.multiple_of((h * 2 + co) * SHARE, SHARE), SHARE)
        got = s["a_in"][t, pl.ds(h, 1)].reshape(SHARE, EMB)
        return s["part"][t, rows, :] + got.astype(F32)

    def to_far(t):
        arrived(s["a_in"].at[t], s["a_sem"].at[t])
        s["b_out"][t] = mine(t, ox).astype(BF16)
        send(s["b_out"].at[t], s["b_in"].at[t], s["b_sem"].at[t], far)
        s["half"][t] = mine(t, xh)

    def exchange(t, x_ref, t_ref, width):
        for k, to in along_y.items():
            cols = pl.ds(pl.multiple_of(lax.rem(y + 4 + k, 4) * width, 128), width)
            send(x_ref.at[:, cols], t_ref.at[-k % 4], s["x_sem"].at[t, -k % 4], to)
        cols = pl.ds(pl.multiple_of(y * width, 128), width)
        t_ref[0] = x_ref[:, cols]

    image_part = partial(0, s["xi"], s["wi"], xi_load, wi_loads)
    text_part = partial(1, s["xt"], s["wt"], xt_load, wt_loads)
    for _ in wi_loads:
        next(image_part)
    pl.semaphore_wait(barrier, len(peers))
    next(image_part, None)
    for _ in text_part:
        pass
    to_far(0)
    exchange(0, s["xi"], s["ti"], FIY)
    to_far(1)
    exchange(1, s["xt"], s["tt"], FTY)

    def units(t):
        arrived(s["b_in"].at[t], s["b_sem"].at[t])
        e = s["half"][t] + s["b_in"][t].astype(F32)
        rs = lax.rsqrt(jnp.sum(e * e, axis=-1, keepdims=True) + EPS)
        s["emb"][t] = e
        s["rst"][t] = jnp.broadcast_to(rs, (SHARE, 128))
        return (e * rs).astype(BF16)

    def images_ring(w):
        if w == 0:
            s["iu"][0, 0] = units(0)
        cols = pl.ds(w * WIDE, WIDE)

        def one(k, half):
            at = (k % 4, 0) if w == 0 else (0, k % 4)
            return s["iu"].at[at + (pl.ds(0, SHARE), cols)]

        def four(k, half):
            at = (pl.ds(0, 4), k % 4) if w == 0 else (k % 4, pl.ds(0, 4))
            rows = pl.ds(0, SHARE) if half is None else rows_half(half)
            return s["iu"].at[at + (rows, cols)]

        first, second = (along_x, along_y) if w == 0 else (along_y, along_x)
        yield from gather_direct(first, one, s["iu_sem"].at[w, 0])
        yield from gather_four(second, four, s["iu_sem"].at[w, 1])

    def texts_ring():
        s["tu"][0, 0] = units(1)

        def ref(k, half):
            rows = pl.ds(0, SHARE) if half is None else rows_half(half)
            return s["tu"].at[0, AROUND.index(k), rows]

        def sem(k):
            return s["tu_sem"].at[AROUND.index(k)]

        def across(part):
            slots = (pl.ds(0, 5), pl.ds(5, 3))[part]
            send(s["tu"].at[0, slots], s["tu"].at[1, slots], s["tc_sem"].at[part], other_core)

        yield from gather_eight(along_z, ref, sem, across)

    def turned(t, t_ref, m_ref, n_ref):
        for k in range(1, 4):
            arrived(t_ref.at[k], s["x_sem"].at[t, k])
        for n, core in enumerate((co, oc)):
            for k, dy in enumerate(ABOUT):
                for h in range(2):
                    at = (n * 8 + k * 2 + h) * SHARE
                    rows = pl.ds(pl.multiple_of((h * 2 + core) * SHARE, SHARE), SHARE)
                    m_ref[at : at + SHARE, :] = t_ref[dy % 4, rows, :]
            n_ref[n] = m_ref[n * 256 : (n + 1) * 256, :].T
            yield

    def towers():
        yield from turned(0, s["ti"], s["mi"], s["ni"])
        yield from turned(1, s["tt"], s["mt"], s["nt"])

    towers_task = towers()
    interleave(
        "tabwabtwabtab",
        t=texts_ring(),
        a=images_ring(0),
        b=images_ring(1),
        w=(next(towers_task, None) for _ in range(2)),
    )

    heat, shift = heat_ref[0], shift_ref[0]
    mult = cot_ref[0] * heat / 8192.0

    def texts():
        return s["tu"][...].reshape(512, EMB)

    def images():
        return s["iu"][...].reshape(512, EMB)

    def coefficients(n):
        score = dot_nt(images(), s["tu"][n].reshape(256, EMB))
        value = jax.nn.sigmoid(heat * score + shift)
        s["coef"][:, n * 256 : (n + 1) * 256] = (mult * value).astype(BF16)
        if n == 0:
            row = lax.broadcasted_iota(jnp.int32, (SHARE, 128), 0)
            col = lax.broadcasted_iota(jnp.int32, (SHARE, 128), 1)
            own = value[:SHARE, :128] - (row == col).astype(F32)
            s["coef"][:SHARE, :128] = (mult * own).astype(BF16)

    def text_half(n, out):
        grad = dot_tn(s["coef"][:, n * 256 : (n + 1) * 256], images())
        out[...] = grad.reshape(8, SHARE, EMB).astype(out.dtype)

    coefficients(0)
    arrived(s["tu"].at[1, pl.ds(0, 5)], s["tc_sem"].at[0])
    arrived(s["tu"].at[1, pl.ds(5, 3)], s["tc_sem"].at[1])
    coefficients(1)
    text_half(1, s["c_out"])
    send(s["c_out"], s["c_in"], s["c_sem"], other_core)

    def back(t, grads, grad):
        rs = s["rst"][t][:, :1]
        u = s["emb"][t] * rs
        value = (grad - u * jnp.sum(u * grad, axis=-1, keepdims=True)) * rs
        grads[0, 0, pl.ds(xh, 1)] = value.astype(BF16).reshape(1, SHARE, EMB)

    def text_grad():
        text_half(0, s["own_t"])
        yield
        arrived(s["c_in"], s["c_sem"])

        def own(k):
            at = AROUND.index(k)
            return s["own_t"][at] + s["c_in"][at].astype(F32)

        totals = []
        yield from scatter_eight(along_z, own, s["d_out"], s["d_in"], s["d_sem"], totals)
        back(1, s["gt"], totals[0])

    def image_half(w):
        first, second = (along_y, along_x) if w == 0 else (along_x, along_y)
        out = s["e1_out"].at[w]
        grad = dot_nn(s["coef"][...], texts()[:, w * WIDE : (w + 1) * WIDE])
        out[...] = grad.astype(BF16).reshape(4, 4, SHARE, WIDE)

        def group(k):
            return out.at[:, k] if w == 0 else out.at[k]

        totals = []
        yield from scatter_direct(
            first, group, lambda: group(0)[...].astype(F32), s["e1_in"].at[w], s["e1_sem"].at[w], totals
        )
        line = s["e2_out"].at[w]
        line[...] = totals[0].astype(BF16)
        yield from scatter_direct(
            second, lambda k: line.at[k], lambda: totals[0][0], s["e2_in"].at[w], s["e2_sem"].at[w], totals
        )
        s["sum_i"][:, w * WIDE : (w + 1) * WIDE] = totals[1]

    def spread(t, grads, first_dot):
        def across(slots, h, n):
            send(grads.at[0, slots, h], grads.at[1, slots, h], s["gc_sem"].at[t, n], other_core)

        def ring(h, n):
            def ref(k, half):
                rows = pl.ds(0, SHARE) if half is None else rows_half(half)
                return grads.at[0, ABOUT.index(k if k != -2 else 2), h, rows]

            if n == 0:
                send(ref(0, None), ref(0, None), s["far_sem"].at[t], far)
            else:
                arrived(ref(0, None), s["far_sem"].at[t])
            task = gather_four(along_y, ref, s["g_sem"].at[t, n])
            next(task)
            yield
            next(task)
            if n == 1:
                across(pl.ds(0, 3), h, 1)
            yield
            yield from task
            across(pl.ds(0, 4) if n == 0 else pl.ds(3, 1), h, 2 * n)

        first, second = ring(xh, 0), ring(ox, 1)
        next(first)
        yield
        next(first)
        next(second)
        yield
        next(first, None)
        next(second)
        yield
        next(second, None)
        first_dot()
        yield
        for n, (h, slots) in enumerate(((xh, pl.ds(0, 4)), (ox, pl.ds(0, 3)), (ox, pl.ds(3, 1)))):
            arrived(grads.at[1, slots, h], s["gc_sem"].at[t, n])

    def weights(t, grads, n_ref, p_ref, own, names):
        def term(n):
            return dot_nn(n_ref[n], grads[n].reshape(256, EMB))

        def first_dot():
            p_ref[...] = term(0)

        yield from spread(t, grads, first_dot)
        p_ref[...] = p_ref[...] + term(1)
        totals = []
        ring = scatter_corner(t, own, names, totals)
        yield from ring
        return totals[0]

    def inputs(grads, w_ref, out):
        for k in range(0, w_ref.shape[0], CHUNK):
            cols = slice(k, k + CHUNK)
            value = dot_nt(grads[:, 0].reshape(ROWS, EMB), w_ref[cols, :]).astype(BF16)
            for n, core in enumerate((co, oc)):
                for h in range(2):
                    rows = pl.ds(pl.multiple_of((h * 2 + core) * SHARE, SHARE), SHARE)
                    at = (n * 2 + h) * SHARE
                    out[k // CHUNK][rows, :] = value[at : at + SHARE]
            yield

    def drain():
        while True:
            for _ in range(len(sends) - len(drained)):
                drained.append(sends[len(drained)])
                drained[-1].wait_send()
            yield

    def own_i(k, half):
        n = half * 8 + lax.rem(z + 8 + k, 8)
        rows = s["pi"][pl.ds(pl.multiple_of(n * OI, 8), OI), :]
        return jnp.concatenate([rows[:, :WIDE], rows[:, WIDE:]], axis=0)

    def own_t(k, half):
        n = half * 8 + lax.rem(z + 8 + k, 8)
        return s["pt"][pl.ds(pl.multiple_of(n * OT, 8), OT), :]

    def texts_back():
        yield from text_grad()
        op_t[...] = yield from weights(1, s["gt"], s["nt"], s["pt"], own_t, "ft")

    def images_back():
        back(0, s["gi"], s["sum_i"][...])
        total = yield from weights(0, s["gi"], s["ni"], s["pi"], own_i, "fi")
        op_i[:, :WIDE] = total[:OI]
        op_i[:, WIDE:] = total[OI:]

    drains = drain()
    interleave(
        "abttwatbabitwititiittiptiotoiptowxiopxt",
        t=texts_back(),
        a=image_half(0),
        b=image_half(1),
        i=images_back(),
        w=towers_task,
        o=inputs(s["gi"], s["wi"], og_i),
        p=inputs(s["gt"], s["wt"], og_t),
        x=(next(drains) for _ in range(2)),
    )
    next(drains)


def copy_out(*refs):
    blocks, outs, sem = refs[:7], refs[7:11], refs[11]
    places = [outs[0].at[:, pl.ds(k, CHUNK)] for k in range(0, FI, CHUNK)]
    places += [outs[1].at[:, pl.ds(k, CHUNK)] for k in range(0, FT, CHUNK)]
    places += outs[2:]
    copies = [pltpu.make_async_copy(blocks[k], places[k], sem.at[k]) for k in range(7)]
    for copy in copies:
        copy.start()
    for copy in copies:
        copy.wait()


def per_device(xi, xt, wi, wt, heat, shift, cot):
    vmem = pl.BlockSpec(memory_space=pltpu.VMEM)
    smem = pl.BlockSpec(memory_space=pltpu.SMEM)
    hbm = pl.BlockSpec(memory_space=pl.ANY)
    shapes = (
        jax.ShapeDtypeStruct((ROWS, FI), BF16),
        jax.ShapeDtypeStruct((ROWS, FT), BF16),
        jax.ShapeDtypeStruct((OI, EMB), F32),
        jax.ShapeDtypeStruct((OT, EMB), F32),
    )
    outs = pl.pallas_call(
        kernel,
        out_shape=(jax.ShapeDtypeStruct((ROWS, CHUNK), BF16),) * 5 + shapes[2:],
        in_specs=[hbm] * 4 + [smem] * 3,
        out_specs=[vmem] * 7,
        scratch_shapes=list(scratch().values()),
        compiler_params=pltpu.CompilerParams(
            collective_id=0, has_side_effects=True, vmem_limit_bytes=55_600_000
        ),
    )(xi, xt, wi, wt, heat, shift, cot)
    return pl.pallas_call(
        copy_out,
        out_shape=shapes,
        in_specs=[hbm] * 7,
        out_specs=[hbm] * 4,
        scratch_shapes=[pltpu.SemaphoreType.DMA((7,))],
        compiler_params=pltpu.CompilerParams(vmem_limit_bytes=2 * 1024 * 1024),
    )(*outs)


def solution(mesh):
    placed = (P("blk", "grp"), P("blk", "grp"), P("grp", None), P("grp", None), P(), P(), P())
    return jax.shard_map(
        per_device,
        mesh=mesh,
        in_specs=placed,
        out_specs=(
            P("blk", "grp"),
            P("blk", "grp"),
            P(("grp", "blk"), None),
            P(("grp", "blk"), None),
        ),
        check_vma=False,
    )
```

```python
import functools

import jax
import jax.numpy as jnp
from jax import lax
from jax.experimental import pallas as pl
from jax.experimental.pallas import tpu as pltpu
from jax.sharding import PartitionSpec as P

MESH = pl.DeviceIdType.MESH
F32 = jnp.float32
BF16 = jnp.bfloat16
EPS = 1e-06

ROWS = 128
SHARE = 32
HALF = 16
EMB = 1024
WIDE = 512
FI, FT = 1536, 1024
FIY, FTY = FI // 4, FT // 4
OI, OT = FIY // 16, FTY // 16
CHUNK = 512
SENDS = 112


def dot_nn(a, b):
    return lax.dot_general(a, b, (((1,), (0,)), ((), ())), preferred_element_type=F32)


def dot_nt(a, b):
    return lax.dot_general(a, b, (((1,), (1,)), ((), ())), preferred_element_type=F32)


def dot_tn(a, b):
    return lax.dot_general(a, b, (((0,), (0,)), ((), ())), preferred_element_type=F32)


def scratch():
    v = pltpu.VMEM
    dma = pltpu.SemaphoreType.DMA
    return dict(
        xi=v((ROWS, FI), BF16),
        xt=v((ROWS, FT), BF16),
        wi=v((FI, EMB), BF16),
        wt=v((FT, EMB), BF16),
        part=v((2, ROWS, EMB), F32),
        a_out=v((2, 2, SHARE, EMB), BF16),
        a_in=v((2, 2, SHARE, EMB), BF16),
        half=v((2, SHARE, EMB), F32),
        b_out=v((2, SHARE, EMB), BF16),
        b_in=v((2, SHARE, EMB), BF16),
        emb=v((2, SHARE, EMB), F32),
        rst=v((2, SHARE, 128), F32),
        iu=v((4, 4, SHARE, EMB), BF16),
        tu=v((2, 8, SHARE, EMB), BF16),
        coef=v((512, 512), BF16),
        c_out=v((8, SHARE, EMB), BF16),
        c_in=v((8, SHARE, EMB), BF16),
        own_t=v((8, SHARE, EMB), F32),
        d_out=v((4, 2, SHARE, EMB), BF16),
        d_in=v((4, 2, SHARE, EMB), BF16),
        e1_out=v((2, 4, 4, SHARE, WIDE), BF16),
        e1_in=v((2, 4, 4, SHARE, WIDE), BF16),
        e2_out=v((2, 4, SHARE, WIDE), BF16),
        e2_in=v((2, 4, SHARE, WIDE), BF16),
        sum_i=v((SHARE, EMB), F32),
        gi=v((2, 4, 2, SHARE, EMB), BF16),
        gt=v((2, 4, 2, SHARE, EMB), BF16),
        ti=v((4, ROWS, FIY), BF16),
        tt=v((4, ROWS, FTY), BF16),
        mi=v((512, FIY), BF16),
        mt=v((512, FTY), BF16),
        ni=v((2, FIY, 256), BF16),
        nt=v((2, FTY, 256), BF16),
        pi=v((FIY, EMB), F32),
        pt=v((FTY, EMB), F32),
        fi_out=v((2, 4, 2, 2 * OI, WIDE), BF16),
        fi_in=v((2, 3, 2, 2 * OI, WIDE), BF16),
        fi_end=v((2, 2, 2 * OI, WIDE), BF16),
        fi_side=v((2, 2 * OI, WIDE), BF16),
        ft_out=v((2, 4, 2, OT, EMB), BF16),
        ft_in=v((2, 3, 2, OT, EMB), BF16),
        ft_end=v((2, 2, OT, EMB), BF16),
        ft_side=v((2, OT, EMB), BF16),
        in_sem=dma((5,)),
        x_sem=dma((2, 4)),
        a_sem=dma((2,)),
        b_sem=dma((2,)),
        iu_sem=dma((2, 2, 4)),
        tu_sem=dma((9,)),
        tc_sem=dma((2,)),
        c_sem=dma,
        d_sem=dma((4, 2)),
        e1_sem=dma((2, 4)),
        e2_sem=dma((2, 4)),
        far_sem=dma((2,)),
        g_sem=dma((2, 2, 4)),
        gc_sem=dma((2, 3)),
        f_sem=dma((2, 2, 3)),
        end_sem=dma((2, 2, 2)),
        h_sem=dma((2,)),
        send_sem=dma((SENDS,)),
    )


NAMES = tuple(scratch())
AROUND = (0, 1, -1, 2, -2, 3, -3, 4)
ABOUT = (0, 1, -1, 2)


def rows_half(h):
    return pl.ds(h * HALF, HALF)


def interleave(order, **tasks):
    for name in order:
        next(tasks[name], None)
    left = list(tasks.values())
    while left:
        left = [task for task in left if next(task, True) is not True]


def kernel(xi_h, xt_h, wi_h, wt_h, heat_ref, shift_ref, cot_ref, *refs):
    og_i, og_t, (op_i, op_t), refs = refs[:3], refs[3:5], refs[5:7], refs[7:]
    s = dict(zip(NAMES, refs))
    g = lax.axis_index("grp")
    b = lax.axis_index("blk")
    xh, co = lax.div(g, 2), lax.rem(g, 2)
    y, xl, z = lax.div(b, 16), lax.rem(lax.div(b, 8), 2), lax.rem(b, 8)
    x = xh * 2 + xl
    oc, ox = 1 - co, 1 - xh

    def dev(x_, y_, z_, co_):
        return (lax.div(x_, 2) * 2 + co_, (y_ * 2 + lax.rem(x_, 2)) * 8 + z_)

    other_core = dev(x, y, z, oc)
    near = dev(xh * 2 + (1 - xl), y, z, co)
    along_x = {k: dev(lax.rem(x + 4 + k, 4), y, z, co) for k in (1, -1, 2)}
    far = along_x[2]
    along_y = {k: dev(x, lax.rem(y + 4 + k, 4), z, co) for k in (1, -1, 2)}
    along_z = {k: dev(x, y, lax.rem(z + 8 + k, 8), co) for k in (1, -1, 2, -2)}
    corner = {
        (h, k): dev(xh * 2 + h, y, lax.rem(z + 8 + k, 8), co) for h in range(2) for k in (1, -1)
    }
    corners = [dev(xh * 2 + (1 - xl), y, lax.rem(z + 8 + k, 8), co) for k in (1, -1)]

    sends, drained = [], []

    def send(src, dst, sem, to):
        copy = pltpu.make_async_remote_copy(
            src_ref=src,
            dst_ref=dst,
            send_sem=s["send_sem"].at[len(sends)],
            recv_sem=sem,
            device_id=to,
            device_id_type=MESH,
        )
        copy.start()
        sends.append(copy)

    def arrived(dst, sem):
        pltpu.make_async_copy(dst, dst, sem).wait()

    def gather_eight(to, ref, sem, then):
        for way in (2, -2, 1, -1):
            send(ref(0, None), ref(-way, None), sem(-way), to[way])
        yield
        for half, way in enumerate((1, -1)):
            far_ = -2 * way
            arrived(ref(far_, None), sem(far_))
            send(ref(far_, half), ref(4, half), s["tu_sem"].at[7 + half], to[2 * way])
            send(ref(far_, None), ref(-3 * way, None), sem(-3 * way), to[way])
        for k in (1, -1):
            arrived(ref(k, None), sem(k))
        then(0)
        yield
        for k in (3, -3):
            arrived(ref(k, None), sem(k))
        for half in range(2):
            arrived(ref(4, half), s["tu_sem"].at[7 + half])
        then(1)

    def scatter_eight(to, own, out, inn, sem, totals):
        for n, way in enumerate((1, -1)):
            rows = rows_half(n)
            out[3, n, rows] = own(4)[n * HALF : (n + 1) * HALF].astype(BF16)
            send(out.at[3, n, rows], inn.at[3, n, rows], sem.at[3, n], to[2 * way])
        for n, way in enumerate((1, -1)):
            out[2, n] = own(3 * way).astype(BF16)
            send(out.at[2, n], inn.at[2, n], sem.at[2, n], to[way])
        for n, way in enumerate((1, -1)):
            out[0, n] = own(way).astype(BF16)
            send(out.at[0, n], inn.at[0, n], sem.at[0, n], to[way])
        yield
        for n, way in enumerate((1, -1)):
            rows = slice(n * HALF, (n + 1) * HALF)
            rest = slice((1 - n) * HALF, (2 - n) * HALF)
            value = own(2 * way)
            arrived(inn.at[2, n], sem.at[2, n])
            arrived(inn.at[3, n, rows_half(n)], sem.at[3, n])
            more = inn[2, n, rows].astype(F32) + inn[3, n, rows].astype(F32)
            out[1, n, rows] = (value[rows] + more).astype(BF16)
            out[1, n, rest] = (value[rest] + inn[2, n, rest].astype(F32)).astype(BF16)
            send(out.at[1, n], inn.at[1, n], sem.at[1, n], to[2 * way])
        value = own(0)
        yield
        for m in range(2):
            for n in range(2):
                arrived(inn.at[m, n], sem.at[m, n])
                value = value + inn[m, n].astype(F32)
        totals.append(value)

    def gather_four(to, ref, sem):
        for way in (1, -1):
            send(ref(0, None), ref(-way, None), sem.at[0 if way > 0 else 1], to[way])
        yield
        for way in (1, -1):
            n = 0 if way > 0 else 1
            arrived(ref(-way, None), sem.at[n])
            send(ref(-way, n), ref(2, n), sem.at[2 + n], to[way])
        yield
        for n in range(2):
            arrived(ref(2, n), sem.at[2 + n])

    def gather_direct(to, ref, sem):
        for way in (2, 1, -1):
            send(ref(0, None), ref(-way, None), sem.at[-way % 4], to[way])
        yield
        for k in (1, -1, 2):
            arrived(ref(k, None), sem.at[k % 4])

    def scatter_direct(to, src, mine_, inn, sem, totals):
        for way in (2, 1, -1):
            k = -way % 4
            send(src(way % 4), inn.at[k], sem.at[k], to[way])
        yield
        value = mine_()
        for k in (1, -1, 2):
            arrived(inn.at[k % 4], sem.at[k % 4])
            value = value + inn[k % 4].astype(F32)
        totals.append(value)

    def scatter_four(to, src, inn, sem, totals):
        for n, way in enumerate((1, -1)):
            there = inn.at[2, pl.ds(0, 4), rows_half(n)]
            send(src(2, rows_half(n)), there, sem.at[2 * n], to[way])
        yield
        for n, way in enumerate((1, -1)):
            there = inn.at[2, pl.ds(0, 4), rows_half(n)]
            arrived(there, sem.at[2 * n])
            part = src(way % 4, rows_half(n))
            part[...] = (part[...].astype(F32) + there[...].astype(F32)).astype(BF16)
            k = -way % 4
            send(src(way % 4, pl.ds(0, SHARE)), inn.at[k], sem.at[k], to[way])
        yield
        value = src(0, pl.ds(0, SHARE))[...].astype(F32)
        for k in (3, 1):
            arrived(inn.at[k], sem.at[k])
            value = value + inn[k].astype(F32)
        totals.append(value)

    def scatter_corner(t, own, name, totals):
        out, inn, end, side = (s[name + part] for part in ("_out", "_in", "_end", "_side"))
        sem, end_sem = s["f_sem"].at[t], s["end_sem"].at[t]
        for step in range(1, 5):
            if step > 1:
                yield
            for d, way in enumerate((1, -1)):
                if step == 1:
                    out[d, 0, d] = own(4 * way, d).astype(BF16)
                    send(out.at[d, 0, d], inn.at[d, 0, d], sem.at[d, 0], along_z[way])
                    continue
                before = inn.at[d, step - 2]
                arrived(before.at[d] if step == 2 else before, sem.at[d, step - 2])
                for half in range(2):
                    value = own(way * (5 - step), half)
                    if step > 2 or half == d:
                        value = value + inn[d, step - 2, half].astype(F32)
                    out[d, step - 1, half] = value.astype(BF16)
                    if step == 4:
                        origin = lax.rem(xl + half, 2)
                        send(out.at[d, 3, half], end.at[origin, d], end_sem.at[origin, d], corner[half, way])
                if step < 4:
                    send(out.at[d, step - 1], inn.at[d, step - 1], sem.at[d, step - 1], along_z[way])
            if step == 1:
                side[0] = own(0, 1 - xl).astype(BF16)
                send(side.at[0], side.at[1], s["h_sem"].at[t], near)
        value = own(0, xl)
        yield
        arrived(side.at[1], s["h_sem"].at[t])
        value = value + side[1].astype(F32)
        for origin in range(2):
            for d in range(2):
                arrived(end.at[origin, d], end_sem.at[origin, d])
                value = value + end[origin, d].astype(F32)
        totals.append(value)

    def load(src, dst, n):
        copy = pltpu.make_async_copy(src, dst, s["in_sem"].at[n])
        copy.start()
        return copy

    def load_rows(src, dst, at, size, n):
        rows = pl.ds(at, size)
        return slice(at, at + size), load(src.at[rows], dst.at[rows], n)

    xi_load = load(xi_h, s["xi"], 0)
    wi_loads = [load_rows(wi_h, s["wi"], 0, FI // 2, 1), load_rows(wi_h, s["wi"], FI // 2, FI // 2, 2)]

    barrier = pltpu.get_barrier_semaphore()
    peers = [other_core, *along_x.values(), *along_y.values(), *along_z.values(), *corners]
    for to in peers:
        pl.semaphore_signal(barrier, inc=1, device_id=to, device_id_type=MESH)

    xt_load = load(xt_h, s["xt"], 3)
    wt_loads = [load_rows(wt_h, s["wt"], 0, FT, 4)]

    def partial(t, x_ref, w_ref, x_load, w_loads):
        x_load.wait()
        for k, (rows, w_load) in enumerate(w_loads):
            w_load.wait()
            part = dot_nn(x_ref[:, rows], w_ref[rows, :])
            s["part"][t] = part if k == 0 else s["part"][t] + part
            yield
        for h in range(2):
            rows = pl.ds(pl.multiple_of((h * 2 + oc) * SHARE, SHARE), SHARE)
            s["a_out"][t, h] = s["part"][t, rows, :].astype(BF16)
        send(s["a_out"].at[t], s["a_in"].at[t], s["a_sem"].at[t], other_core)

    def mine(t, h):
        rows = pl.ds(pl.multiple_of((h * 2 + co) * SHARE, SHARE), SHARE)
        got = s["a_in"][t, pl.ds(h, 1)].reshape(SHARE, EMB)
        return s["part"][t, rows, :] + got.astype(F32)

    def to_far(t):
        arrived(s["a_in"].at[t], s["a_sem"].at[t])
        s["b_out"][t] = mine(t, ox).astype(BF16)
        send(s["b_out"].at[t], s["b_in"].at[t], s["b_sem"].at[t], far)
        s["half"][t] = mine(t, xh)

    def exchange(t, x_ref, t_ref, width):
        for k, to in along_y.items():
            cols = pl.ds(pl.multiple_of(lax.rem(y + 4 + k, 4) * width, 128), width)
            send(x_ref.at[:, cols], t_ref.at[-k % 4], s["x_sem"].at[t, -k % 4], to)
        cols = pl.ds(pl.multiple_of(y * width, 128), width)
        t_ref[0] = x_ref[:, cols]

    image_part = partial(0, s["xi"], s["wi"], xi_load, wi_loads)
    text_part = partial(1, s["xt"], s["wt"], xt_load, wt_loads)
    for _ in wi_loads:
        next(image_part)
    pl.semaphore_wait(barrier, len(peers))
    next(image_part, None)
    for _ in text_part:
        pass
    to_far(0)
    exchange(0, s["xi"], s["ti"], FIY)
    to_far(1)
    exchange(1, s["xt"], s["tt"], FTY)

    def units(t):
        arrived(s["b_in"].at[t], s["b_sem"].at[t])
        e = s["half"][t] + s["b_in"][t].astype(F32)
        rs = lax.rsqrt(jnp.sum(e * e, axis=-1, keepdims=True) + EPS)
        s["emb"][t] = e
        s["rst"][t] = jnp.broadcast_to(rs, (SHARE, 128))
        return (e * rs).astype(BF16)

    def images_ring(w):
        if w == 0:
            s["iu"][0, 0] = units(0)
        cols = pl.ds(w * WIDE, WIDE)

        def one(k, half):
            at = (k % 4, 0) if w == 0 else (0, k % 4)
            return s["iu"].at[at + (pl.ds(0, SHARE), cols)]

        def four(k, half):
            at = (pl.ds(0, 4), k % 4) if w == 0 else (k % 4, pl.ds(0, 4))
            rows = pl.ds(0, SHARE) if half is None else rows_half(half)
            return s["iu"].at[at + (rows, cols)]

        first, second = (along_x, along_y) if w == 0 else (along_y, along_x)
        yield from gather_direct(first, one, s["iu_sem"].at[w, 0])
        yield from gather_four(second, four, s["iu_sem"].at[w, 1])

    def texts_ring():
        s["tu"][0, 0] = units(1)

        def ref(k, half):
            rows = pl.ds(0, SHARE) if half is None else rows_half(half)
            return s["tu"].at[0, AROUND.index(k), rows]

        def sem(k):
            return s["tu_sem"].at[AROUND.index(k)]

        def across(part):
            slots = (pl.ds(0, 5), pl.ds(5, 3))[part]
            send(s["tu"].at[0, slots], s["tu"].at[1, slots], s["tc_sem"].at[part], other_core)

        yield from gather_eight(along_z, ref, sem, across)

    def turned(t, t_ref, m_ref, n_ref):
        for k in range(1, 4):
            arrived(t_ref.at[k], s["x_sem"].at[t, k])
        for n, core in enumerate((co, oc)):
            for k, dy in enumerate(ABOUT):
                for h in range(2):
                    at = (n * 8 + k * 2 + h) * SHARE
                    rows = pl.ds(pl.multiple_of((h * 2 + core) * SHARE, SHARE), SHARE)
                    m_ref[at : at + SHARE, :] = t_ref[dy % 4, rows, :]
            n_ref[n] = m_ref[n * 256 : (n + 1) * 256, :].T
            yield

    def towers():
        yield from turned(0, s["ti"], s["mi"], s["ni"])
        yield from turned(1, s["tt"], s["mt"], s["nt"])

    towers_task = towers()
    interleave(
        "tabwabtwabtab",
        t=texts_ring(),
        a=images_ring(0),
        b=images_ring(1),
        w=(next(towers_task, None) for _ in range(2)),
    )

    heat, shift = heat_ref[0], shift_ref[0]
    mult = cot_ref[0] * heat / 8192.0

    def texts():
        return s["tu"][...].reshape(512, EMB)

    def images():
        return s["iu"][...].reshape(512, EMB)

    def coefficients(n):
        score = dot_nt(images(), s["tu"][n].reshape(256, EMB))
        value = jax.nn.sigmoid(heat * score + shift)
        s["coef"][:, n * 256 : (n + 1) * 256] = (mult * value).astype(BF16)
        if n == 0:
            row = lax.broadcasted_iota(jnp.int32, (SHARE, 128), 0)
            col = lax.broadcasted_iota(jnp.int32, (SHARE, 128), 1)
            own = value[:SHARE, :128] - (row == col).astype(F32)
            s["coef"][:SHARE, :128] = (mult * own).astype(BF16)

    def text_half(n, out):
        grad = dot_tn(s["coef"][:, n * 256 : (n + 1) * 256], images())
        out[...] = grad.reshape(8, SHARE, EMB).astype(out.dtype)

    coefficients(0)
    arrived(s["tu"].at[1, pl.ds(0, 5)], s["tc_sem"].at[0])
    arrived(s["tu"].at[1, pl.ds(5, 3)], s["tc_sem"].at[1])
    coefficients(1)
    text_half(1, s["c_out"])
    send(s["c_out"], s["c_in"], s["c_sem"], other_core)

    def back(t, grads, grad):
        rs = s["rst"][t][:, :1]
        u = s["emb"][t] * rs
        value = (grad - u * jnp.sum(u * grad, axis=-1, keepdims=True)) * rs
        grads[0, 0, pl.ds(xh, 1)] = value.astype(BF16).reshape(1, SHARE, EMB)

    def text_grad():
        text_half(0, s["own_t"])
        yield
        arrived(s["c_in"], s["c_sem"])

        def own(k):
            at = AROUND.index(k)
            return s["own_t"][at] + s["c_in"][at].astype(F32)

        totals = []
        yield from scatter_eight(along_z, own, s["d_out"], s["d_in"], s["d_sem"], totals)
        back(1, s["gt"], totals[0])

    def image_half(w):
        first, second = (along_y, along_x) if w == 0 else (along_x, along_y)
        out = s["e1_out"].at[w]
        grad = dot_nn(s["coef"][...], texts()[:, w * WIDE : (w + 1) * WIDE])
        out[...] = grad.astype(BF16).reshape(4, 4, SHARE, WIDE)

        def group(k, rows):
            return out.at[pl.ds(0, 4), k, rows] if w == 0 else out.at[k, pl.ds(0, 4), rows]

        totals = []
        yield from scatter_four(first, group, s["e1_in"].at[w], s["e1_sem"].at[w], totals)
        line = s["e2_out"].at[w]
        line[...] = totals[0].astype(BF16)
        yield from scatter_direct(
            second, lambda k: line.at[k], lambda: totals[0][0], s["e2_in"].at[w], s["e2_sem"].at[w], totals
        )
        s["sum_i"][:, w * WIDE : (w + 1) * WIDE] = totals[1]

    def spread(t, grads, first_dot):
        def across(slots, h, n):
            send(grads.at[0, slots, h], grads.at[1, slots, h], s["gc_sem"].at[t, n], other_core)

        def ring(h, n):
            def ref(k, half):
                rows = pl.ds(0, SHARE) if half is None else rows_half(half)
                return grads.at[0, ABOUT.index(k if k != -2 else 2), h, rows]

            if n == 0:
                send(ref(0, None), ref(0, None), s["far_sem"].at[t], far)
            else:
                arrived(ref(0, None), s["far_sem"].at[t])
            task = gather_four(along_y, ref, s["g_sem"].at[t, n])
            next(task)
            yield
            next(task)
            if n == 1:
                across(pl.ds(0, 3), h, 1)
            yield
            yield from task
            across(pl.ds(0, 4) if n == 0 else pl.ds(3, 1), h, 2 * n)

        first, second = ring(xh, 0), ring(ox, 1)
        next(first)
        yield
        next(first)
        next(second)
        yield
        next(first, None)
        next(second)
        yield
        next(second, None)
        first_dot()
        yield
        for n, (h, slots) in enumerate(((xh, pl.ds(0, 4)), (ox, pl.ds(0, 3)), (ox, pl.ds(3, 1)))):
            arrived(grads.at[1, slots, h], s["gc_sem"].at[t, n])

    def weights(t, grads, n_ref, p_ref, own, names):
        def term(n):
            return dot_nn(n_ref[n], grads[n].reshape(256, EMB))

        def first_dot():
            p_ref[...] = term(0)

        yield from spread(t, grads, first_dot)
        p_ref[...] = p_ref[...] + term(1)
        totals = []
        ring = scatter_corner(t, own, names, totals)
        yield from ring
        return totals[0]

    def inputs(grads, w_ref, out):
        for k in range(0, w_ref.shape[0], CHUNK):
            cols = slice(k, k + CHUNK)
            value = dot_nt(grads[:, 0].reshape(ROWS, EMB), w_ref[cols, :]).astype(BF16)
            for n, core in enumerate((co, oc)):
                for h in range(2):
                    rows = pl.ds(pl.multiple_of((h * 2 + core) * SHARE, SHARE), SHARE)
                    at = (n * 2 + h) * SHARE
                    out[k // CHUNK][rows, :] = value[at : at + SHARE]
            yield

    def drain():
        while True:
            for _ in range(len(sends) - len(drained)):
                drained.append(sends[len(drained)])
                drained[-1].wait_send()
            yield

    def own_i(k, half):
        n = half * 8 + lax.rem(z + 8 + k, 8)
        rows = s["pi"][pl.ds(pl.multiple_of(n * OI, 8), OI), :]
        return jnp.concatenate([rows[:, :WIDE], rows[:, WIDE:]], axis=0)

    def own_t(k, half):
        n = half * 8 + lax.rem(z + 8 + k, 8)
        return s["pt"][pl.ds(pl.multiple_of(n * OT, 8), OT), :]

    def texts_back():
        yield from text_grad()
        op_t[...] = yield from weights(1, s["gt"], s["nt"], s["pt"], own_t, "ft")

    def images_back():
        back(0, s["gi"], s["sum_i"][...])
        total = yield from weights(0, s["gi"], s["ni"], s["pi"], own_i, "fi")
        op_i[:, :WIDE] = total[:OI]
        op_i[:, WIDE:] = total[OI:]

    drains = drain()
    interleave(
        "abttwabtababitwititiittiptiotoiptowxiopxt",
        t=texts_back(),
        a=image_half(0),
        b=image_half(1),
        i=images_back(),
        w=towers_task,
        o=inputs(s["gi"], s["wi"], og_i),
        p=inputs(s["gt"], s["wt"], og_t),
        x=(next(drains) for _ in range(2)),
    )
    next(drains)


def copy_out(*refs):
    blocks, outs, sem = refs[:7], refs[7:11], refs[11]
    places = [outs[0].at[:, pl.ds(k, CHUNK)] for k in range(0, FI, CHUNK)]
    places += [outs[1].at[:, pl.ds(k, CHUNK)] for k in range(0, FT, CHUNK)]
    places += outs[2:]
    copies = [pltpu.make_async_copy(blocks[k], places[k], sem.at[k]) for k in range(7)]
    for copy in copies:
        copy.start()
    for copy in copies:
        copy.wait()


def per_device(xi, xt, wi, wt, heat, shift, cot):
    vmem = pl.BlockSpec(memory_space=pltpu.VMEM)
    smem = pl.BlockSpec(memory_space=pltpu.SMEM)
    hbm = pl.BlockSpec(memory_space=pl.ANY)
    shapes = (
        jax.ShapeDtypeStruct((ROWS, FI), BF16),
        jax.ShapeDtypeStruct((ROWS, FT), BF16),
        jax.ShapeDtypeStruct((OI, EMB), F32),
        jax.ShapeDtypeStruct((OT, EMB), F32),
    )
    outs = pl.pallas_call(
        kernel,
        out_shape=(jax.ShapeDtypeStruct((ROWS, CHUNK), BF16),) * 5 + shapes[2:],
        in_specs=[hbm] * 4 + [smem] * 3,
        out_specs=[vmem] * 7,
        scratch_shapes=list(scratch().values()),
        compiler_params=pltpu.CompilerParams(
            collective_id=0, has_side_effects=True, vmem_limit_bytes=55_600_000
        ),
    )(xi, xt, wi, wt, heat, shift, cot)
    return pl.pallas_call(
        copy_out,
        out_shape=shapes,
        in_specs=[hbm] * 7,
        out_specs=[hbm] * 4,
        scratch_shapes=[pltpu.SemaphoreType.DMA((7,))],
        compiler_params=pltpu.CompilerParams(vmem_limit_bytes=2 * 1024 * 1024),
    )(*outs)


def solution(mesh):
    placed = (P("blk", "grp"), P("blk", "grp"), P("grp", None), P("grp", None), P(), P(), P())
    return jax.shard_map(
        per_device,
        mesh=mesh,
        in_specs=placed,
        out_specs=(
            P("blk", "grp"),
            P("blk", "grp"),
            P(("grp", "blk"), None),
            P(("grp", "blk"), None),
        ),
        check_vma=False,
    )
```
